32 devices in a mesh: shard: 8 (over y, x, core), rep: 4 (over z).
Axes of the slice: x: 2, y: 2, z: 4, core: 2. Of those that a mesh axis runs over, the one named last changes fastest.
Arguments:
- hidden_in: bfloat16 [32, 128, 2048], P(('shard', 'rep')), may hold values from -6 to 6
- segments: int32 [32, 128], P(('shard', 'rep')), may hold values from 0 to 3, never falling along the last dimension, each value on 1 to 64 neighbouring positions
- ln1_gain: bfloat16 [2, 2048], P(None, 'shard'), may hold values from 0.099609375 to 1.8984375
- ln1_bias: bfloat16 [2, 2048], P(None, 'shard'), may hold values from -4 to 4
- qkv_weight: bfloat16 [2, 2048, 6144], P(None, 'shard'), may hold values from -0.125 to 0.125
- qkv_bias: bfloat16 [2, 6144], P(None, 'shard'), may hold values from -6 to 6
- out_weight: bfloat16 [2, 2048, 2048], P(None, 'shard'), may hold values from -0.5 to 0.5
- ln2_gain: bfloat16 [2, 2048], P(None, 'shard'), may hold values from 0.099609375 to 1.8984375
- ln2_bias: bfloat16 [2, 2048], P(None, 'shard'), may hold values from -4 to 4
- gate_weight: bfloat16 [2, 2048, 5632], P(None, 'shard'), may hold values from -0.125 to 0.125
- up_weight: bfloat16 [2, 2048, 5632], P(None, 'shard'), may hold values from -0.125 to 0.125
- down_weight: bfloat16 [2, 5632, 2048], P(None, 'shard'), may hold values from -0.109375 to 0.109375
- cotangent: bfloat16 [32, 128, 2048], P(('shard', 'rep')), may hold values from -6 to 6
Outputs:
- block_out: bfloat16 [32, 128, 2048], P(('shard', 'rep'))
- input_grad: bfloat16 [32, 128, 2048], P(('shard', 'rep'))
- ln1_gain_grad: float32 [2, 2048], P(None, 'shard')
- ln1_bias_grad: float32 [2, 2048], P(None, 'shard')
- qkv_weight_grad: float32 [2, 2048, 6144], P(None, 'shard')
- qkv_bias_grad: float32 [2, 6144], P(None, 'shard')
- out_weight_grad: float32 [2, 2048, 2048], P(None, 'shard')
- ln2_gain_grad: float32 [2, 2048], P(None, 'shard')
- ln2_bias_grad: float32 [2, 2048], P(None, 'shard')
- gate_weight_grad: float32 [2, 2048, 5632], P(None, 'shard')
- up_weight_grad: float32 [2, 2048, 5632], P(None, 'shard')
- down_weight_grad: float32 [2, 5632, 2048], P(None, 'shard')
The draws below stay inside these ranges and needn't reach their ends.
Inputs may be any that keep to these rules, and one draw needn't show every extreme that they name: `segments`: along each sequence the numbers never fall; each of the 4 documents holds one token or more and at most half of 128.
All inputs are finite; a program needn't handle non-finite values.
Results may differ from the reference program's by a relative error of at most 0.02.
Values may be sent and summed in bfloat16 or wider, within the bound.
No kernel may reach another device: no remote copies, remote signals or barrier semaphores. Data moves between devices by JAX's collectives and lax.ppermute only.
A program may use at most 512 MiB of HBM per device.

```python
import math
import jax
import jax.numpy as jnp
import numpy as np
from jax import lax

D = 2048
HEADS = 32
ROTARY = 16
FF = 5632
LAYERS = 2
TOK_DEV = 128
DOCS = 4
SEQS = 32


def block_scale(rng, shape, shards, smallest, top_value):
    def one(dim, parts):
        draws = jax.random.uniform(jax.random.fold_in(jax.random.fold_in(rng, 6), dim), (parts,), jnp.float32, smallest / len(shards), top_value / len(shards))
        return jnp.repeat(jnp.exp(draws), shape[dim] // parts).reshape((-1,) + (1,) * (len(shape) - dim - 1))

    factor_of = one(*shards[0])
    for cut in shards[1:]:
        factor_of = factor_of * one(*cut)
    return factor_of


def split_up(number_of, total, bound, slope):
    loads = [(1 << 20) // math.isqrt(grade ** slope) + 1 for grade in range(2, number_of + 1)]
    rest, given = total - bound - (number_of - 1), [1] * (number_of - 1)
    while rest > 0:
        candidates = [i for i in range(number_of - 1) if given[i] < bound]
        mass, budget = sum([loads[i] for i in candidates]), rest
        for i in candidates:
            more = min(bound - given[i], max(1, budget * loads[i] // mass), rest)
            given[i] = given[i] + more
            rest = rest - more
    return np.array([bound] + given)


def uneven_parts(stream_key, count, total, bound, slope):
    if count == 2:
        one = jax.random.randint(stream_key, (), max(1, total - bound), min(bound, total - 1) + 1)
        return jnp.stack([one, total - one])
    sizes = jnp.asarray(split_up(count, total, bound, slope), jnp.int32)
    pairs = (count - 1) // 2
    source_of, sink = sizes[1:1 + 2 * pairs:2], sizes[2:2 + 2 * pairs:2]
    margin = jnp.minimum(source_of - 1, bound - sink)
    moved = jax.random.randint(jax.random.fold_in(stream_key, 1), (pairs,), 0, 1 << 20) % (margin + 1)
    sizes = sizes.at[1:1 + 2 * pairs:2].set(source_of - moved).at[2:2 + 2 * pairs:2].set(sink + moved)
    return sizes[jax.random.permutation(jax.random.fold_in(stream_key, 2), count)]


def normal_values(rng, extent, deviation, most, shards=(), kind=jnp.bfloat16):
    array = deviation * jax.random.normal(rng, extent, jnp.float32)
    if shards:
        array = array * block_scale(rng, extent, shards, -0.22, 0.18)
    return jnp.clip(array, -most, most).astype(kind)


def setup_inputs(seed: int = 0) -> dict:
    key_list = jax.random.split(jax.random.key(seed), 14)
    hidden_in = normal_values(key_list[0], (SEQS, TOK_DEV, D), 1.0, 6.0, ((0, 32),))
    segments = jax.vmap(lambda own: jnp.searchsorted(jnp.cumsum(uneven_parts(own, DOCS, TOK_DEV, TOK_DEV // 2, 0)), jnp.arange(TOK_DEV), side="right"))(jax.random.split(key_list[1], SEQS)).reshape((SEQS, TOK_DEV)).astype(jnp.int32)
    ln1_gain = jnp.clip(1.0 + 0.18 * jax.random.normal(key_list[2], (LAYERS, D), jnp.float32), 0.099609375, 1.8984375).astype(jnp.bfloat16)
    ln1_bias = normal_values(key_list[3], (LAYERS, D), 0.3, 4.0, ((1, 8),))
    qkv_weight = normal_values(key_list[4], (LAYERS, D, 3 * D), D ** -0.5, 0.125, ((1, 8),))
    qkv_bias = normal_values(key_list[5], (LAYERS, 3 * D), 0.5, 6.0, ((1, 8),))
    out_weight = normal_values(key_list[6], (LAYERS, D, D), (D // 16) ** -0.5, 0.5, ((1, 8),))
    ln2_gain = jnp.clip(1.0 + 0.18 * jax.random.normal(key_list[7], (LAYERS, D), jnp.float32), 0.099609375, 1.8984375).astype(jnp.bfloat16)
    ln2_bias = normal_values(key_list[8], (LAYERS, D), 0.3, 4.0, ((1, 8),))
    gate_weight = normal_values(key_list[9], (LAYERS, D, FF), D ** -0.5, 0.125, ((1, 8),))
    up_weight = normal_values(key_list[10], (LAYERS, D, FF), D ** -0.5, 0.125, ((1, 8),))
    down_weight = normal_values(key_list[11], (LAYERS, FF, D), (FF // 2) ** -0.5, 0.109375, ((1, 8),))
    cotangent = normal_values(key_list[12], (SEQS, TOK_DEV, D), 1.0, 6.0, ((0, 32),))
    return {"hidden_in": hidden_in, "segments": segments, "ln1_gain": ln1_gain, "ln1_bias": ln1_bias, "qkv_weight": qkv_weight, "qkv_bias": qkv_bias, "out_weight": out_weight, "ln2_gain": ln2_gain, "ln2_bias": ln2_bias, "gate_weight": gate_weight, "up_weight": up_weight, "down_weight": down_weight, "cotangent": cotangent}


@jax.custom_vjp
def low(v):
    return lax.optimization_barrier(v.astype(jnp.bfloat16)).astype(jnp.float32)

@jax.custom_vjp
def low_back(v):
    return v

def low_keep(v):
    return (low(v), None)

def low_pass(kept, grad):
    return (grad,)

def back_keep(v):
    return (v, None)

def back_low(kept, grad):
    return (low(grad),)
low.defvjp(low_keep, low_pass)
low_back.defvjp(back_keep, back_low)
norm_eps = 1e-05
highest = lax.Precision.HIGHEST

def layer_norm(values, norm_gain, norm_shift):
    centred = values - lax.optimization_barrier(jnp.mean(values, axis=-1, keepdims=True))
    variance = lax.optimization_barrier(jnp.mean(centred * centred, axis=-1, keepdims=True))
    return centred * lax.rsqrt(variance + norm_eps) * norm_gain + norm_shift

def positions_and_mask(segments):
    length = segments.shape[-1]
    earlier = (segments[..., None, :] < segments[..., :, None]).astype(jnp.int32)
    starts = lax.optimization_barrier(jnp.sum(earlier, axis=-1)).astype(jnp.int32)
    places = jnp.arange(length, dtype=jnp.int32)
    positions = places - starts
    allowed = (segments[..., None, :] == segments[..., :, None]) & (places[None, :] <= places[:, None])
    return (positions, allowed)

def rotary_tables(positions):
    half_dims = ROTARY // 2
    exponents = jnp.arange(half_dims, dtype=jnp.float32) * (2.0 / ROTARY)
    inverse = 10000.0 ** (-exponents)
    angles = positions.astype(jnp.float32)[..., None] * inverse
    return (jnp.cos(angles)[..., None, :], jnp.sin(angles)[..., None, :])

def rotate(heads_in, cosine, sine_table):
    half_dims = ROTARY // 2
    leading = heads_in[..., :half_dims]
    trailing = heads_in[..., half_dims:ROTARY]
    unturned = heads_in[..., ROTARY:]
    return jnp.concatenate([leading * cosine - trailing * sine_table, trailing * cosine + leading * sine_table, unturned], axis=-1)

def attention_block(state, allowed, cosine, sine_table, norm_gain, norm_shift, proj_in, proj_bias, proj_out):
    groups, tokens, width = state.shape
    head_size = width // HEADS
    normed = low(layer_norm(state, norm_gain, norm_shift))
    joined = low_back(jnp.einsum('gtd,de->gte', normed, proj_in, precision=highest) + proj_bias)
    split = joined.reshape(groups, tokens, 3, HEADS, head_size)
    query = low(rotate(split[:, :, 0], cosine, sine_table))
    key_vals = low(rotate(split[:, :, 1], cosine, sine_table))
    values = low(split[:, :, 2])
    scores = low_back(jnp.einsum('gqhd,gkhd->ghqk', query, key_vals, precision=highest) * head_size ** (-0.5))
    masked = jnp.where(allowed[:, None], scores, -1000000000.0)
    probs = low(jax.nn.softmax(masked, axis=-1))
    mixed = low(low_back(jnp.einsum('ghqk,gkhd->gqhd', probs, values, precision=highest)))
    mixed = mixed.reshape(groups, tokens, width)
    return state + low_back(jnp.einsum('gtd,de->gte', mixed, proj_out, precision=highest))

def feed_block(state, norm_gain, norm_shift, weight_gate, weight_up, weight_down):
    normed = low(layer_norm(state, norm_gain, norm_shift))
    gate = low_back(jnp.einsum('gtd,df->gtf', normed, weight_gate, precision=highest))
    upper = low_back(jnp.einsum('gtd,df->gtf', normed, weight_up, precision=highest))
    inner = low(jax.nn.silu(gate) * upper)
    return state + low_back(jnp.einsum('gtf,fd->gtd', inner, weight_down, precision=highest))

def forward_group(state, segments, params):
    positions, allowed = positions_and_mask(segments)
    cosine, sine_table = rotary_tables(positions)
    for layer in range(LAYERS):
        state = attention_block(state, allowed, cosine, sine_table, params[0][layer], params[1][layer], params[2][layer], params[3][layer], params[4][layer])
        state = feed_block(state, params[5][layer], params[6][layer], params[7][layer], params[8][layer], params[9][layer])
    return state

def reference(hidden_in, segments, ln1_gain, ln1_bias, qkv_weight, qkv_bias, out_weight, ln2_gain, ln2_bias, gate_weight, up_weight, down_weight, cotangent):
    params = tuple((weight.astype(jnp.float32) for weight in (ln1_gain, ln1_bias, qkv_weight, qkv_bias, out_weight, ln2_gain, ln2_bias, gate_weight, up_weight, down_weight)))
    group = math.gcd(SEQS, 16)
    blocks = SEQS // group
    inputs = hidden_in.astype(jnp.float32).reshape(blocks, group, TOK_DEV, D)
    grouped = segments.reshape(blocks, group, TOK_DEV)

    def whole(block_inputs, weights):

        def one_block(pair):
            return forward_group(pair[0], pair[1], weights)
        return lax.map(jax.checkpoint(one_block), (block_inputs, grouped))
    outputs, pullback = jax.vjp(whole, inputs, params)
    input_grad, param_grads = pullback(cotangent.astype(jnp.float32).reshape(blocks, group, TOK_DEV, D))
    return (outputs.reshape(SEQS, TOK_DEV, D).astype(jnp.bfloat16), input_grad.reshape(SEQS, TOK_DEV, D).astype(jnp.bfloat16), param_grads[0], param_grads[1], param_grads[2], param_grads[3], param_grads[4], param_grads[5], param_grads[6], param_grads[7], param_grads[8], param_grads[9])
```

```python
import jax
import jax.numpy as jnp
from jax import lax
from jax.sharding import PartitionSpec as P

HEADS = 32
ROTARY = 16
HALF = ROTARY // 2

norm_eps = 1e-05
bf16 = jnp.bfloat16
f32 = jnp.float32


def dot(a, b):
    return jnp.dot(a, b, preferred_element_type=f32)


def dot_t(a, b):
    return lax.dot_general(a, b, (((1,), (1,)), ((), ())), preferred_element_type=f32)


def t_dot(a, b):
    return lax.dot_general(a, b, (((0,), (0,)), ((), ())), preferred_element_type=f32)


def normalize(values):
    centred = values - jnp.mean(values, axis=-1, keepdims=True)
    variance = jnp.mean(centred * centred, axis=-1, keepdims=True)
    inverse = lax.rsqrt(variance + norm_eps)
    return centred * inverse, inverse


def normalize_back(grad, xhat, inverse, gain):
    scaled = grad * gain
    inner = jnp.mean(scaled * xhat, axis=-1, keepdims=True)
    grad_in = inverse * (scaled - jnp.mean(scaled, axis=-1, keepdims=True) - xhat * inner)
    return grad_in, jnp.sum(grad * xhat, axis=0), jnp.sum(grad, axis=0)


def positions_and_mask(segments):
    length = segments.shape[-1]
    earlier = (segments[..., None, :] < segments[..., :, None]).astype(jnp.int32)
    starts = jnp.sum(earlier, axis=-1)
    places = jnp.arange(length, dtype=jnp.int32)
    positions = places - starts
    allowed = (segments[..., None, :] == segments[..., :, None]) & (
        places[None, :] <= places[:, None]
    )
    return positions, allowed


def rotary_tables(positions):
    exponents = jnp.arange(HALF, dtype=f32) * (2.0 / ROTARY)
    inverse = 10000.0 ** (-exponents)
    angles = positions.astype(f32)[..., None] * inverse
    return jnp.cos(angles)[..., None, :], jnp.sin(angles)[..., None, :]


def rotate(heads_in, cosine, sine):
    leading = heads_in[..., :HALF]
    trailing = heads_in[..., HALF:ROTARY]
    return jnp.concatenate(
        [
            leading * cosine - trailing * sine,
            trailing * cosine + leading * sine,
            heads_in[..., ROTARY:],
        ],
        axis=-1,
    )


class Exchange:
    def __init__(self, mesh):
        self.shards = mesh.shape["shard"]
        self.reps = mesh.shape["rep"]
        self.cube = self.shards == 8
        self.line = self.reps == 4

    def swap(self, values, bit):
        pairs = [(i, i ^ bit) for i in range(self.shards)]
        return lax.ppermute(values, "shard", pairs)

    def gather(self, own):
        if not self.cube:
            return lax.all_gather(own, "shard", axis=0, tiled=False)
        first = self.swap(own, 1)
        x, y, d = self.swap(own, 2), self.swap(own, 4), self.swap(own, 6)
        others = self.swap(jnp.stack([x, y, d]), 1)
        return jnp.stack([own, first, x, others[0], y, others[1], d, others[2]])

    def scatter_sum(self, blocks):
        if not self.cube:
            return lax.psum_scatter(blocks.astype(bf16), "shard", scatter_dimension=0, tiled=False).astype(f32)
        low = blocks.astype(bf16)
        arrived = self.swap(jnp.stack([low[1], low[3], low[5], low[7]]), 1).astype(f32)
        x = self.swap((blocks[2] + arrived[1]).astype(bf16), 2)
        y = self.swap((blocks[4] + arrived[2]).astype(bf16), 4)
        d = self.swap((blocks[6] + arrived[3]).astype(bf16), 6)
        own = blocks[0] + arrived[0]
        return own + x.astype(f32) + (y.astype(f32) + d.astype(f32))

    def spread(self, blocks):
        return lax.all_to_all(blocks, "shard", split_axis=0, concat_axis=0, tiled=False)

    def total(self, grad, turn=None):
        turn = turn or (lambda v: v)
        if not self.line:
            full = lax.psum(grad.astype(bf16), "rep")
            return jnp.stack([turn(full[0]), turn(full[1])]).astype(f32)
        rep = lax.axis_index("rep")
        low = grad.astype(bf16)
        inward = lax.ppermute(low, "rep", [(0, 1), (3, 2)])
        part = (grad + inward.astype(f32)).astype(bf16)
        lower = rep < 2
        sent = jnp.where(lower, part[0], part[1])
        kept = jnp.where(lower, part[1], part[0])
        middle = lax.ppermute(sent, "rep", [(1, 2), (2, 1)])
        final = turn((kept.astype(f32) + middle.astype(f32)).astype(bf16))
        other = lax.ppermute(final, "rep", [(1, 2), (2, 1)])
        whole = jnp.where(lower, jnp.stack([other, final]), jnp.stack([final, other]))
        outward = lax.ppermute(whole, "rep", [(1, 0), (2, 3)])
        return jnp.where((rep == 1) | (rep == 2), whole, outward).astype(f32)


def make_local(mesh):
    net = Exchange(mesh)
    shards = net.shards

    def local(
        hidden_in,
        segments,
        ln1_gain,
        ln1_bias,
        qkv_weight,
        qkv_bias,
        out_weight,
        ln2_gain,
        ln2_bias,
        gate_weight,
        up_weight,
        down_weight,
        cotangent,
    ):
        layers, rows = qkv_weight.shape[:2]
        width = hidden_in.shape[2]
        tokens = hidden_in.shape[1]
        head_size = width // HEADS
        scale = head_size ** (-0.5)
        own_heads = HEADS // shards
        cols = own_heads * head_size
        hidden_units = down_weight.shape[1]
        everyone = shards * tokens
        me = lax.axis_index("shard")

        small = jnp.concatenate(
            [v.reshape(-1) for v in (ln1_gain, ln1_bias, ln2_gain, ln2_bias, qkv_bias)]
        )
        small = lax.all_gather(small, "shard", axis=0, tiled=False)
        cuts = [0]
        for v in (ln1_gain, ln1_bias, ln2_gain, ln2_bias, qkv_bias):
            cuts.append(cuts[-1] + v.size)

        def whole_of(index, like):
            part = small[:, cuts[index] : cuts[index + 1]].reshape(shards, layers, like.shape[1])
            return part.transpose(1, 0, 2).reshape(layers, -1).astype(f32)

        gain1, shift1 = whole_of(0, ln1_gain), whole_of(1, ln1_bias)
        gain2, shift2 = whole_of(2, ln2_gain), whole_of(3, ln2_bias)
        bias_all = whole_of(4, qkv_bias).reshape(layers, 3, shards, cols)
        bias_own = lax.dynamic_index_in_dim(bias_all, me, axis=2, keepdims=False)
        bias_own = bias_own.reshape(layers, 3 * cols)

        group_segments = net.gather(segments[0].astype(bf16)).astype(jnp.int32)
        positions, allowed = positions_and_mask(group_segments)
        cosine, sine = rotary_tables(positions)
        allowed = allowed[:, None]

        def columns_of(weight):
            cut = weight.reshape(rows, shards, -1).transpose(1, 0, 2)
            return net.spread(cut).reshape(width, -1)

        def qkv_columns(weight):
            cut = weight.reshape(rows, 3, shards, cols).transpose(2, 0, 1, 3)
            return net.spread(cut).reshape(width, 3 * cols)

        proj_in = [qkv_columns(qkv_weight[layer]) for layer in range(layers)]
        weight_gate = [columns_of(gate_weight[layer]) for layer in range(layers)]
        weight_up = [columns_of(up_weight[layer]) for layer in range(layers)]

        def gather(values):
            return net.gather(values).reshape(everyone, -1)

        def scatter_sum(values):
            return net.scatter_sum(values.reshape(shards, tokens, -1))

        state = hidden_in[0].astype(f32)
        saved = []
        for layer in range(layers):
            xhat1, inverse1 = normalize(state)
            normed1 = gather((xhat1 * gain1[layer] + shift1[layer]).astype(bf16))
            joined = dot(normed1, proj_in[layer]) + bias_own[layer]
            split = joined.reshape(shards, tokens, 3, own_heads, head_size)
            query = rotate(split[:, :, 0], cosine, sine).astype(bf16)
            keys = rotate(split[:, :, 1], cosine, sine).astype(bf16)
            value = split[:, :, 2].astype(bf16)
            scores = (
                jnp.einsum("gqhd,gkhd->ghqk", query, keys, preferred_element_type=f32) * scale
            )
            masked = jnp.where(allowed, scores, -1000000000.0)
            peak = jnp.max(masked, axis=-1, keepdims=True)
            raised = jnp.exp(masked - peak)
            probs = raised / jnp.sum(raised, axis=-1, keepdims=True)
            probs_low = probs.astype(bf16)
            mixed = (
                jnp.einsum("ghqk,gkhd->gqhd", probs_low, value, preferred_element_type=f32)
                .astype(bf16)
                .reshape(everyone, cols)
            )
            state_mid = state + scatter_sum(dot(mixed, out_weight[layer]))
            xhat2, inverse2 = normalize(state_mid)
            normed2 = gather((xhat2 * gain2[layer] + shift2[layer]).astype(bf16))
            gate = dot(normed2, weight_gate[layer])
            upper = dot(normed2, weight_up[layer])
            inner = (jax.nn.silu(gate) * upper).astype(bf16)
            state = state_mid + scatter_sum(dot(inner, down_weight[layer]))
            saved.append(
                (xhat1, inverse1, normed1, query, keys, value, probs, mixed)
                + (xhat2, inverse2, normed2, gate, upper, inner)
            )
        block_out = state.astype(bf16)[None]

        def from_columns(grad):
            return grad.reshape(shards, 2, rows // 2, -1).transpose(1, 0, 2, 3)

        def turn_columns(half):
            return net.spread(half).transpose(1, 0, 2).reshape(rows // 2, -1)

        def turn_qkv(half):
            whole = net.spread(half).reshape(shards, rows // 2, 3, cols)
            return whole.transpose(1, 2, 0, 3).reshape(rows // 2, -1)

        def halves(grad):
            return grad.reshape(2, grad.shape[0] // 2, -1)

        grad_state = cotangent[0].astype(f32)
        weight_grads = [None] * layers
        small_grads = [None] * layers
        for layer in reversed(range(layers)):
            xhat1, inverse1, normed1, query, keys, value, probs, mixed = saved[layer][:8]
            xhat2, inverse2, normed2, gate, upper, inner = saved[layer][8:]
            down_in = gather(grad_state.astype(bf16))
            grad_inner = dot_t(down_in, down_weight[layer])
            sigmoid = jax.nn.sigmoid(gate)
            silu = gate * sigmoid
            grad_gate = (grad_inner * upper * (sigmoid * (1.0 + gate * (1.0 - sigmoid)))).astype(bf16)
            grad_up = (grad_inner * silu).astype(bf16)
            grad_normed2 = scatter_sum(
                dot_t(grad_gate, weight_gate[layer]) + dot_t(grad_up, weight_up[layer])
            )
            grad_down_weight = net.total(halves(t_dot(inner, down_in)))
            grad_gate_weight = net.total(from_columns(t_dot(normed2, grad_gate)), turn_columns)
            grad_up_weight = net.total(from_columns(t_dot(normed2, grad_up)), turn_columns)
            back2, gain2_grad, shift2_grad = normalize_back(
                grad_normed2, xhat2, inverse2, gain2[layer]
            )
            grad_state = grad_state + back2

            branch = gather(grad_state.astype(bf16))
            grad_mixed = dot_t(branch, out_weight[layer]).astype(bf16)
            grad_out_weight = net.total(halves(t_dot(mixed, branch)))
            grad_mixed = grad_mixed.reshape(shards, tokens, own_heads, head_size)
            grad_probs = jnp.einsum(
                "gqhd,gkhd->ghqk", grad_mixed, value, preferred_element_type=f32
            )
            grad_value = jnp.einsum(
                "ghqk,gqhd->gkhd", probs.astype(bf16), grad_mixed, preferred_element_type=f32
            )
            inner_sum = jnp.sum(probs * grad_probs, axis=-1, keepdims=True)
            grad_scores = (probs * (grad_probs - inner_sum)).astype(bf16)
            grad_query = (
                jnp.einsum("ghqk,gkhd->gqhd", grad_scores, keys, preferred_element_type=f32) * scale
            )
            grad_key = (
                jnp.einsum("ghqk,gqhd->gkhd", grad_scores, query, preferred_element_type=f32)
                * scale
            )
            grad_query = rotate(grad_query, cosine, -sine)
            grad_key = rotate(grad_key, cosine, -sine)
            grad_joined = jnp.stack([grad_query, grad_key, grad_value], axis=2)
            bias_grad = jnp.sum(grad_joined.astype(bf16).astype(f32), axis=(0, 1))
            grad_joined = grad_joined.reshape(everyone, 3 * cols).astype(bf16)
            grad_normed1 = scatter_sum(dot_t(grad_joined, proj_in[layer]))
            grad_qkv_weight = net.total(from_columns(t_dot(normed1, grad_joined)), turn_qkv)
            back1, gain1_grad, shift1_grad = normalize_back(
                grad_normed1, xhat1, inverse1, gain1[layer]
            )
            grad_state = grad_state + back1
            weight_grads[layer] = (
                grad_qkv_weight.reshape(rows, -1),
                grad_out_weight.reshape(rows, -1),
                grad_gate_weight.reshape(rows, -1),
                grad_up_weight.reshape(rows, -1),
                grad_down_weight.reshape(hidden_units, -1),
            )
            placed = jnp.where(
                (jnp.arange(shards) == me)[None, :, None], bias_grad.reshape(3, 1, cols), 0.0
            )
            small_grads[layer] = jnp.concatenate(
                [gain1_grad, shift1_grad, gain2_grad, shift2_grad, placed.reshape(-1)]
            )

        summed = lax.psum(jnp.stack(small_grads), ("shard", "rep"))

        def owned(begin, count):
            part = summed[:, begin : begin + count].reshape(layers, shards, count // shards)
            return lax.dynamic_index_in_dim(part, me, axis=1, keepdims=False)

        stacked = [
            jnp.stack([weight_grads[layer][index] for layer in range(layers)]) for index in range(5)
        ]
        return (
            block_out,
            grad_state.astype(bf16)[None],
            owned(0, width),
            owned(width, width),
            stacked[0],
            owned(4 * width, 3 * width),
            stacked[1],
            owned(2 * width, width),
            owned(3 * width, width),
            stacked[2],
            stacked[3],
            stacked[4],
        )

    return local


def solution(mesh):
    tokens3 = P(("shard", "rep"), None, None)
    vector = P(None, "shard")
    matrix = P(None, "shard", None)
    in_specs = (
        tokens3,
        P(("shard", "rep"), None),
        vector,
        vector,
        matrix,
        vector,
        matrix,
        vector,
        vector,
        matrix,
        matrix,
        matrix,
        tokens3,
    )
    out_specs = (
        tokens3,
        tokens3,
        vector,
        vector,
        matrix,
        vector,
        matrix,
        vector,
        vector,
        matrix,
        matrix,
        matrix,
    )
    return jax.shard_map(
        make_local(mesh), mesh=mesh, in_specs=in_specs, out_specs=out_specs, check_vma=False
    )
```

```python
import functools

import jax
import jax.numpy as jnp
from jax import lax
from jax.experimental import pallas as pl
from jax.experimental.pallas import tpu as pltpu
from jax.sharding import PartitionSpec as P

HEADS = 32
ROTARY = 16
HALF = ROTARY // 2

norm_eps = 1e-05
bf16 = jnp.bfloat16
f32 = jnp.float32


def dot(a, b):
    return jnp.dot(a, b, preferred_element_type=f32)


def dot_t(a, b):
    return lax.dot_general(a, b, (((1,), (1,)), ((), ())), preferred_element_type=f32)


def t_dot(a, b):
    return lax.dot_general(a, b, (((0,), (0,)), ((), ())), preferred_element_type=f32)


def normalize(values):
    centred = values - jnp.mean(values, axis=-1, keepdims=True)
    variance = jnp.mean(centred * centred, axis=-1, keepdims=True)
    inverse = lax.rsqrt(variance + norm_eps)
    return centred * inverse, inverse


def normalize_back(grad, xhat, inverse, gain):
    scaled = grad * gain
    inner = jnp.mean(scaled * xhat, axis=-1, keepdims=True)
    grad_in = inverse * (scaled - jnp.mean(scaled, axis=-1, keepdims=True) - xhat * inner)
    return grad_in, jnp.sum(grad * xhat, axis=0), jnp.sum(grad, axis=0)


def positions_and_mask(segments):
    length = segments.shape[-1]
    earlier = (segments[..., None, :] < segments[..., :, None]).astype(jnp.int32)
    starts = jnp.sum(earlier, axis=-1)
    places = jnp.arange(length, dtype=jnp.int32)
    positions = places - starts
    allowed = (segments[..., None, :] == segments[..., :, None]) & (
        places[None, :] <= places[:, None]
    )
    return positions, allowed


def rotary_tables(positions):
    exponents = jnp.arange(HALF, dtype=f32) * (2.0 / ROTARY)
    inverse = 10000.0 ** (-exponents)
    angles = positions.astype(f32)[..., None] * inverse
    return jnp.cos(angles)[..., None, :], jnp.sin(angles)[..., None, :]


def rotate(heads_in, cosine, sine):
    leading = heads_in[..., :HALF]
    trailing = heads_in[..., HALF:ROTARY]
    return jnp.concatenate(
        [
            leading * cosine - trailing * sine,
            trailing * cosine + leading * sine,
            heads_in[..., ROTARY:],
        ],
        axis=-1,
    )


def call(kernel, grid, in_specs, out_specs, out_shape, flops, moved, vmem=48, scratch=()):
    return pl.pallas_call(
        kernel,
        grid=grid or (),
        in_specs=in_specs,
        out_specs=out_specs,
        out_shape=out_shape,
        scratch_shapes=scratch,
        compiler_params=pltpu.CompilerParams(vmem_limit_bytes=vmem << 20),
        cost_estimate=pl.CostEstimate(flops=flops, bytes_accessed=moved, transcendentals=0),
    )


def whole(shape):
    zeros = (0,) * len(shape)
    return pl.BlockSpec(shape, lambda *_: zeros, pipeline_mode=pl.Buffered(1))


def shape_of(shape, dtype):
    return jax.ShapeDtypeStruct(shape, dtype)


def head_lanes(values, head, head_size):
    lanes = lax.broadcasted_iota(jnp.int32, values.shape, 1)
    inside = (lanes >= head * head_size) & (lanes < (head + 1) * head_size)
    return jnp.where(inside, values, jnp.zeros_like(values))


def join_rows(own_ref, pair_ref):
    pieces = []
    for s in range(own_ref.shape[0]):
        pieces += [own_ref[s], pair_ref[s]]
    return jnp.concatenate(pieces, axis=0)


def part_rows(values, keep_ref, send_ref):
    count, half, _ = keep_ref.shape
    for s in range(count):
        first = 2 * s * half
        keep_ref[s] = values[first : first + half]
        send_ref[s] = values[first + half : first + 2 * half].astype(bf16)


def attend_kernel(
    own_ref, pair_ref, w_ref, bias_ref, cos_ref, low_ref, high_ref, mask_ref, out_w_ref,
    keep_ref, send_ref, normed_ref, q_ref, k_ref, v_ref, mixed_ref,
    *, heads, head_size,
):
    cols = heads * head_size
    normed = join_rows(own_ref, pair_ref)
    normed_ref[...] = normed
    joined = dot(normed, w_ref[...]) + bias_ref[...]
    cosine, low, high = cos_ref[...], low_ref[...], high_ref[...]

    def turn(v):
        return v * cosine + pltpu.roll(v, cols - HALF, 1) * low + pltpu.roll(v, HALF, 1) * high

    q = turn(joined[:, :cols]).astype(bf16)
    k = turn(joined[:, cols : 2 * cols]).astype(bf16)
    v = joined[:, 2 * cols :].astype(bf16)
    q_ref[...] = q
    k_ref[...] = k
    v_ref[...] = v
    tokens = mask_ref.shape[1]
    mixed = []
    for s in range(mask_ref.shape[0]):
        at = slice(s * tokens, (s + 1) * tokens)
        allowed = mask_ref[s] > 0.5
        total = None
        for h in range(heads):
            scores = dot_t(head_lanes(q[at], h, head_size), k[at]) * head_size ** (-0.5)
            masked = jnp.where(allowed, scores, -1000000000.0)
            raised = jnp.exp(masked - jnp.max(masked, axis=-1, keepdims=True))
            probs = raised / jnp.sum(raised, axis=-1, keepdims=True)
            term = dot(probs.astype(bf16), head_lanes(v[at], h, head_size))
            total = term if total is None else total + term
        mixed.append(total.astype(bf16))
    mixed = jnp.concatenate(mixed, axis=0)
    mixed_ref[...] = mixed
    part_rows(dot(mixed, out_w_ref[...]), keep_ref, send_ref)


def attend_back_kernel(
    own_ref, pair_ref, w_ref, cos_ref, low_ref, high_ref, mask_ref, out_w_ref, q_ref, k_ref, v_ref,
    keep_ref, send_ref, branch_ref, joined_ref, bias_ref,
    *, heads, head_size,
):
    cols = heads * head_size
    scale = head_size ** (-0.5)
    branch = join_rows(own_ref, pair_ref)
    branch_ref[...] = branch
    grad_mixed = dot_t(branch, out_w_ref[...]).astype(bf16)
    cosine, low, high = cos_ref[...], low_ref[...], high_ref[...]

    def turn_back(v):
        return v * cosine - pltpu.roll(v, cols - HALF, 1) * low - pltpu.roll(v, HALF, 1) * high

    q, k, v = q_ref[...], k_ref[...], v_ref[...]
    tokens = mask_ref.shape[1]
    grad_q, grad_k, grad_v = [], [], []
    for s in range(mask_ref.shape[0]):
        at = slice(s * tokens, (s + 1) * tokens)
        allowed = mask_ref[s] > 0.5
        sums = [None, None, None]
        for h in range(heads):
            q_h = head_lanes(q[at], h, head_size)
            g_h = head_lanes(grad_mixed[at], h, head_size)
            scores = dot_t(q_h, k[at]) * scale
            masked = jnp.where(allowed, scores, -1000000000.0)
            raised = jnp.exp(masked - jnp.max(masked, axis=-1, keepdims=True))
            probs = raised / jnp.sum(raised, axis=-1, keepdims=True)
            grad_probs = dot_t(g_h, v[at])
            inner = jnp.sum(probs * grad_probs, axis=-1, keepdims=True)
            grad_scores = (probs * (grad_probs - inner)).astype(bf16)
            terms = (
                dot(grad_scores, head_lanes(k[at], h, head_size)),
                t_dot(grad_scores, q_h),
                t_dot(probs.astype(bf16), g_h),
            )
            sums = [t if a is None else a + t for a, t in zip(sums, terms)]
        grad_q.append(sums[0] * scale)
        grad_k.append(sums[1] * scale)
        grad_v.append(sums[2])
    joined = jnp.concatenate(
        [
            turn_back(jnp.concatenate(grad_q, axis=0)),
            turn_back(jnp.concatenate(grad_k, axis=0)),
            jnp.concatenate(grad_v, axis=0),
        ],
        axis=1,
    ).astype(bf16)
    joined_ref[...] = joined

    @pl.when(pl.program_id(0) == 0)
    def _():
        bias_ref[...] = jnp.zeros_like(bias_ref)

    bias_ref[...] += jnp.sum(joined.astype(f32), axis=0, keepdims=True)
    part_rows(dot_t(joined, w_ref[...]), keep_ref, send_ref)


def feed_kernel(
    own_ref, pair_ref, w_ref, down_ref, keep_ref, send_ref, normed_ref, gate_ref, upper_ref, inner_ref
):
    normed = join_rows(own_ref, pair_ref)
    normed_ref[...] = normed
    flat = (normed.shape[1], w_ref.shape[3])
    gate = dot(normed, w_ref[:, 0].reshape(flat))
    upper = dot(normed, w_ref[:, 1].reshape(flat))
    gate_ref[...] = gate
    upper_ref[...] = upper
    inner = (gate / (1.0 + jnp.exp(-gate)) * upper).astype(bf16)
    inner_ref[...] = inner
    part_rows(dot(inner, down_ref[...]), keep_ref, send_ref)


def feed_back_kernel(
    own_ref, pair_ref, w_ref, down_ref, gate_ref, upper_ref,
    keep_ref, send_ref, down_in_ref, grad_gate_ref, grad_upper_ref,
):
    down_in = join_rows(own_ref, pair_ref)
    down_in_ref[...] = down_in
    flat = (down_in.shape[1], w_ref.shape[3])
    grad_inner = dot_t(down_in, down_ref[...])
    gate, upper = gate_ref[...], upper_ref[...]
    sigmoid = 1.0 / (1.0 + jnp.exp(-gate))
    slope = sigmoid * (1.0 + gate * (1.0 - sigmoid))
    grad_gate = (grad_inner * upper * slope).astype(bf16)
    grad_upper = (grad_inner * (gate * sigmoid)).astype(bf16)
    grad_gate_ref[...] = grad_gate
    grad_upper_ref[...] = grad_upper
    partial = dot_t(grad_gate, w_ref[:, 0].reshape(flat)) + dot_t(grad_upper, w_ref[:, 1].reshape(flat))
    part_rows(partial, keep_ref, send_ref)


def combine_kernel(keep_ref, arrived_ref, own_ref, x_ref, y_ref, d_ref):
    own_ref[...] = keep_ref[0] + arrived_ref[0].astype(f32)
    for k, ref in ((1, x_ref), (2, y_ref), (3, d_ref)):
        ref[...] = (keep_ref[k] + arrived_ref[k].astype(f32)).astype(bf16)


def received(own_ref, x_ref, y_ref, d_ref):
    return own_ref[...] + x_ref[...].astype(f32) + (y_ref[...].astype(f32) + d_ref[...].astype(f32))


def norm_first_kernel(state_ref, gain_ref, shift_ref, normed_ref):
    xhat, _ = normalize(state_ref[...])
    normed_ref[...] = (xhat * gain_ref[...] + shift_ref[...]).astype(bf16)


def norm_kernel(state_ref, own_ref, x_ref, y_ref, d_ref, gain_ref, shift_ref, new_ref, normed_ref):
    state = state_ref[...] + received(own_ref, x_ref, y_ref, d_ref)
    new_ref[...] = state
    xhat, _ = normalize(state)
    normed_ref[...] = (xhat * gain_ref[...] + shift_ref[...]).astype(bf16)


def last_kernel(state_ref, own_ref, x_ref, y_ref, d_ref, out_ref):
    out_ref[...] = (state_ref[...] + received(own_ref, x_ref, y_ref, d_ref)).astype(bf16)


def norm_back_kernel(
    grad_ref, own_ref, x_ref, y_ref, d_ref, state_ref, gain_ref, new_ref, low_ref, sums_ref
):
    grad_normed = received(own_ref, x_ref, y_ref, d_ref)
    xhat, inverse = normalize(state_ref[...])
    scaled = grad_normed * gain_ref[...]
    inner = jnp.mean(scaled * xhat, axis=-1, keepdims=True)
    back = inverse * (scaled - jnp.mean(scaled, axis=-1, keepdims=True) - xhat * inner)
    grad = grad_ref[...] + back
    new_ref[...] = grad
    low_ref[...] = grad.astype(bf16)
    sums_ref[0:1] = jnp.sum(grad_normed * xhat, axis=0, keepdims=True)
    sums_ref[1:2] = jnp.sum(grad_normed, axis=0, keepdims=True)


def weight_rows_kernel(first_ref, second_ref, first_grad_ref, second_grad_ref, out_ref):
    product = t_dot(first_ref[...], first_grad_ref[...]) + t_dot(second_ref[...], second_grad_ref[...])
    product = product.astype(bf16)
    half = product.shape[0] // 2
    out_ref[0] = product[:half].reshape(out_ref.shape[1:])
    out_ref[1] = product[half:].reshape(out_ref.shape[1:])


def make_cube(mesh):
    shards, reps = 8, 4

    def swap(values, bit):
        return lax.ppermute(values, "shard", [(i, i ^ bit) for i in range(shards)])

    def local(
        hidden_in,
        segments,
        ln1_gain,
        ln1_bias,
        qkv_weight,
        qkv_bias,
        out_weight,
        ln2_gain,
        ln2_bias,
        gate_weight,
        up_weight,
        down_weight,
        cotangent,
    ):
        layers, rows = qkv_weight.shape[:2]
        width = hidden_in.shape[2]
        tokens = hidden_in.shape[1]
        part = tokens // 2
        head_size = width // HEADS
        heads = HEADS // shards
        cols = heads * head_size
        hidden = down_weight.shape[1]
        chips = shards // 2
        many = chips * tokens
        step = 2 * tokens
        me = lax.axis_index("shard")
        core = me % 2
        rep = lax.axis_index("rep")
        lower = rep < 2
        within = (rep == 1) | (rep == 2)

        smalls = (ln1_gain, ln1_bias, ln2_gain, ln2_bias, qkv_bias, segments.astype(bf16))
        small = lax.all_gather(
            jnp.concatenate([v.reshape(-1) for v in smalls]), "shard", axis=0, tiled=False
        )
        cuts = [0]
        for v in smalls:
            cuts.append(cuts[-1] + v.size)

        def whole_of(index):
            like = smalls[index]
            cut = small[:, cuts[index] : cuts[index + 1]].reshape(shards, layers, like.shape[1])
            return cut.transpose(1, 0, 2).reshape(layers, -1).astype(f32)

        gain1, shift1, gain2, shift2 = (whole_of(i) for i in range(4))
        bias_all = whole_of(4).reshape(layers, 3, shards, cols)
        bias_own = lax.dynamic_index_in_dim(bias_all, me, axis=2, keepdims=False)
        bias_own = bias_own.reshape(layers, 1, 3 * cols)
        all_segments = small[:, cuts[5] : cuts[6]]

        places = jnp.arange(tokens, dtype=jnp.int32)
        places = jnp.where(core == 0, places, (places + part) % tokens)
        exponents = jnp.arange(HALF, dtype=f32) * (2.0 / ROTARY)
        inverse = 10000.0 ** (-exponents)
        masks, tables = [], []
        for h in range(2):
            wanted = (me // 2 ^ jnp.arange(chips)) * 2 + h
            picked = (wanted[:, None] == jnp.arange(shards)[None]).astype(bf16)
            numbers = dot(picked, all_segments)
            numbers = jnp.where(core == 0, numbers, jnp.roll(numbers, part, axis=1))
            earlier = numbers[:, None, :] < numbers[:, :, None]
            positions = places - jnp.sum(earlier.astype(jnp.int32), axis=-1)
            allowed = (numbers[:, None, :] == numbers[:, :, None]) & (
                places[None, :] <= places[:, None]
            )
            masks.append(allowed.astype(f32))
            angles = positions.astype(f32).reshape(many, 1) * inverse
            cosine, sine = jnp.cos(angles), jnp.sin(angles)
            zero8 = jnp.zeros_like(sine)
            rest = jnp.zeros((many, head_size - ROTARY), f32)
            tables.append(
                [
                    jnp.tile(jnp.concatenate(pieces, axis=1), (1, heads))
                    for pieces in (
                        (cosine, cosine, rest + 1.0),
                        (-sine, zero8, rest),
                        (zero8, sine, rest),
                    )
                ]
            )

        def spread(blocks):
            return lax.all_to_all(blocks, "shard", split_axis=0, concat_axis=0, tiled=False)

        def qkv_columns(weight):
            cut = weight.reshape(rows, 3, shards, cols).transpose(2, 0, 1, 3)
            return spread(cut.reshape(shards, rows, 3 * cols)).reshape(width, 3 * cols)

        def feed_columns(gate, up):
            both = jnp.stack([v.reshape(rows, shards, hidden).transpose(1, 0, 2) for v in (gate, up)], axis=1)
            return spread(both)

        proj_in, feed_in = [], []
        for layer in range(layers):
            proj_in.append(qkv_columns(qkv_weight[layer]))
            feed_in.append(feed_columns(gate_weight[layer], up_weight[layer]))

        def gather(own):
            x, y, d = swap(own, 2), swap(own, 4), swap(own, 6)
            mine = jnp.stack([own, x, y, d])
            return mine, swap(mine, 1)

        combine = call(
            combine_kernel,
            None,
            [pl.BlockSpec(memory_space=pltpu.VMEM)] * 2,
            [pl.BlockSpec(memory_space=pltpu.VMEM)] * 4,
            [shape_of((part, width), f32)] + [shape_of((part, width), bf16)] * 3,
            1 << 20,
            5 << 20,
            16,
        )

        def scatter_sum(keep, send):
            own, x, y, d = combine(keep, swap(send, 1))
            return own, swap(x, 2), swap(y, 4), swap(d, 6)

        steps = chips // 2
        piece = pl.BlockSpec((2, part, width), lambda i: (i, 0, 0))

        def row_block(n):
            return pl.BlockSpec((step, n), lambda i: (i, 0))

        mask_block = pl.BlockSpec((2, tokens, tokens), lambda i: (i, 0, 0))
        table_blocks = [row_block(cols)] * 3
        part_shapes = [
            shape_of((chips, part, width), f32),
            shape_of((chips, part, width), bf16),
        ]
        options = dict(heads=heads, head_size=head_size)
        attend_flops = 2 * many * width * 4 * cols
        feed_flops = 2 * many * width * 3 * hidden
        attend = call(
            functools.partial(attend_kernel, **options),
            (steps,),
            [piece, piece, whole((width, 3 * cols)), whole((1, 3 * cols))]
            + table_blocks
            + [mask_block, whole((cols, width))],
            [piece, piece, row_block(width)] + [row_block(cols)] * 4,
            part_shapes + [shape_of((many, width), bf16)] + [shape_of((many, cols), bf16)] * 4,
            attend_flops,
            16 << 20,
        )
        attend_back = call(
            functools.partial(attend_back_kernel, **options),
            (steps,),
            [piece, piece, whole((width, 3 * cols))]
            + table_blocks
            + [mask_block, whole((cols, width))]
            + [row_block(cols)] * 3,
            [piece, piece, row_block(width), row_block(3 * cols), pl.BlockSpec((1, 3 * cols), lambda i: (0, 0))],
            part_shapes
            + [shape_of((many, width), bf16), shape_of((many, 3 * cols), bf16), shape_of((1, 3 * cols), f32)],
            attend_flops,
            16 << 20,
        )
        feed_weights = [whole((shards, 2, rows, hidden)), whole((hidden, width))]
        feed = call(
            feed_kernel,
            (steps,),
            [piece, piece] + feed_weights,
            [piece, piece, row_block(width)] + [row_block(hidden)] * 3,
            part_shapes
            + [shape_of((many, width), bf16)]
            + [shape_of((many, hidden), f32)] * 2
            + [shape_of((many, hidden), bf16)],
            feed_flops,
            24 << 20,
        )
        feed_back = call(
            feed_back_kernel,
            (steps,),
            [piece, piece] + feed_weights + [row_block(hidden)] * 2,
            [piece, piece, row_block(width)] + [row_block(hidden)] * 2,
            part_shapes + [shape_of((many, width), bf16)] + [shape_of((many, hidden), bf16)] * 2,
            feed_flops,
            24 << 20,
        )

        def small_call(kernel, n_in, out_shape):
            vmem = pl.BlockSpec(memory_space=pltpu.VMEM)
            return call(kernel, None, [vmem] * n_in, [vmem] * len(out_shape), out_shape, 1 << 20, 3 << 20, 16)

        low_shape, state_shape = shape_of((part, width), bf16), shape_of((part, width), f32)
        norm_first = small_call(norm_first_kernel, 3, [low_shape])
        norm = small_call(norm_kernel, 7, [state_shape, low_shape])
        last = small_call(last_kernel, 5, [low_shape])
        norm_back = small_call(norm_back_kernel, 7, [state_shape, low_shape, shape_of((2, width), f32)])

        def weight_columns(lefts, rights):
            n = rights[0].shape[1]
            left = pl.BlockSpec((many, rows), lambda s: (0, s))
            return call(
                weight_rows_kernel,
                (shards,),
                [left, left, whole((many, n)), whole((many, n))],
                pl.BlockSpec((2, 1, rows // 2, n), lambda s: (0, s, 0, 0)),
                shape_of((2, shards, rows // 2, n), bf16),
                4 * many * width * n,
                8 << 20,
                32,
            )(*lefts, *rights)

        def weight_rows(lefts, rights):
            m = lefts[0].shape[1]
            right = pl.BlockSpec((many, 512), lambda s: (0, s))
            return call(
                weight_rows_kernel,
                (width // 512,),
                [whole((many, m)), whole((many, m)), right, right],
                pl.BlockSpec((2, m // 2, 512), lambda s: (0, 0, s)),
                shape_of((2, m // 2, width), bf16),
                4 * many * width * m,
                8 << 20,
                32,
            )(*lefts, *rights)

        def total(grad, turn=lambda v: v):
            inward = lax.ppermute(grad, "rep", [(0, 1), (3, 2)])
            gone = jnp.where(lower, 0, 1)

            def add(index):
                picked = [lax.dynamic_index_in_dim(v, index, 0, keepdims=False) for v in (grad, inward)]
                return picked[0].astype(f32) + picked[1].astype(f32)

            middle = lax.ppermute(add(gone).astype(bf16), "rep", [(1, 2), (2, 1)])
            final = turn((add(1 - gone) + middle.astype(f32)).astype(bf16))
            other = lax.ppermute(final, "rep", [(1, 2), (2, 1)])
            final_out = lax.ppermute(final, "rep", [(1, 0), (2, 3)])
            other_out = lax.ppermute(other, "rep", [(1, 0), (2, 3)])
            mine = jnp.where(within, final, final_out)
            theirs = jnp.where(within, other, other_out)
            return jnp.where(lower, theirs, mine), jnp.where(lower, mine, theirs)

        def from_rows(grad):
            return jnp.concatenate(total(grad), axis=0).astype(f32)

        def from_columns(grad):
            halves = [v.transpose(1, 0, 2).reshape(rows // 2, -1) for v in total(grad, spread)]
            return jnp.concatenate(halves, axis=0).astype(f32)

        def from_qkv(grad):
            halves = [
                v.reshape(shards, rows // 2, 3, cols).transpose(1, 2, 0, 3).reshape(rows // 2, -1)
                for v in total(grad, spread)
            ]
            return jnp.concatenate(halves, axis=0).astype(f32)

        def share(values):
            first, second = values[:part], values[part:]
            kept = jnp.where(core == 0, first, second)
            arrived = swap(jnp.where(core == 0, second, first), 1)
            return [jnp.where(core == 0, kept, arrived), jnp.where(core == 0, arrived, kept)]

        def unshare(halves):
            kept = jnp.where(core == 0, halves[0], halves[1])
            arrived = swap(jnp.where(core == 0, halves[1], halves[0]), 1)
            both = [jnp.where(core == 0, kept, arrived), jnp.where(core == 0, arrived, kept)]
            return jnp.concatenate(both, axis=0)[None]

        states = [v.astype(f32) for v in share(hidden_in[0])]
        lows = [norm_first(states[h], gain1[:1], shift1[:1])[0] for h in range(2)]
        cotangents = share(cotangent[0])
        outs = [None, None]
        saved = [[None, None] for _ in range(layers)]
        for layer in range(layers):
            for h in range(2):
                gathered = gather(lows[h])
                keep, send, normed1, q, k, v, mixed = attend(
                    *gathered, proj_in[layer], bias_own[layer], *tables[h], masks[h], out_weight[layer]
                )
                state_mid, low = norm(
                    states[h], *scatter_sum(keep, send), gain2[layer : layer + 1], shift2[layer : layer + 1]
                )
                gathered = gather(low)
                keep, send, normed2, gate, upper, inner = feed(
                    *gathered, feed_in[layer], down_weight[layer]
                )
                saved[layer][h] = (
                    (states[h], normed1, q, k, v, mixed, state_mid, normed2, gate, upper, inner)
                )
                arrived = scatter_sum(keep, send)
                if layer + 1 < layers:
                    states[h], lows[h] = norm(
                        state_mid, *arrived, gain1[layer + 1 : layer + 2], shift1[layer + 1 : layer + 2]
                    )
                else:
                    outs[h] = last(state_mid, *arrived)[0]
        block_out = unshare(outs)

        lows = cotangents
        grads = [v.astype(f32) for v in cotangents]
        weight_grads = [None] * layers
        small_grads = [None] * layers
        for layer in reversed(range(layers)):
            down_ins, gate_grads, up_grads, branches, joineds = [], [], [], [], []
            sums2, sums1, bias_sums = [], [], []
            for h in range(2):
                states1, normed1, q, k, v, mixed, state_mid, normed2, gate, upper, inner = saved[layer][h]
                keep, send, down_in, grad_gate, grad_up = feed_back(
                    *gather(lows[h]), feed_in[layer], down_weight[layer], gate, upper
                )
                grad_mid, low, sums = norm_back(
                    grads[h], *scatter_sum(keep, send), state_mid, gain2[layer : layer + 1]
                )
                sums2.append(sums)
                keep, send, branch, joined, bias_sum = attend_back(
                    *gather(low), proj_in[layer], *tables[h], masks[h], out_weight[layer], q, k, v
                )
                grads[h], lows[h], sums = norm_back(
                    grad_mid, *scatter_sum(keep, send), states1, gain1[layer : layer + 1]
                )
                sums1.append(sums)
                bias_sums.append(bias_sum)
                for kept, value in zip(
                    (down_ins, gate_grads, up_grads, branches, joineds),
                    (down_in, grad_gate, grad_up, branch, joined),
                ):
                    kept.append(value)

            def both(index):
                return [saved[layer][h][index] for h in range(2)]

            weight_grads[layer] = (
                from_qkv(weight_columns(both(1), joineds)),
                from_rows(weight_rows(both(5), branches)),
                from_columns(weight_columns(both(7), gate_grads)),
                from_columns(weight_columns(both(7), up_grads)),
                from_rows(weight_rows(both(10), down_ins)),
            )
            placed = jnp.where(
                (jnp.arange(shards) == me)[None, :, None],
                (bias_sums[0] + bias_sums[1]).reshape(3, 1, cols),
                0.0,
            )
            small_grads[layer] = jnp.concatenate(
                [(sums1[0] + sums1[1]).reshape(-1), (sums2[0] + sums2[1]).reshape(-1), placed.reshape(-1)]
            )
        input_grad = unshare(lows)

        summed = jnp.stack(small_grads)
        for bit in (1, 2, 4):
            summed = summed + swap(summed, bit)
        for bit in (1, 2):
            summed = summed + lax.ppermute(summed, "rep", [(i, i ^ bit) for i in range(reps)])

        def owned(begin, count):
            cut = summed[:, begin : begin + count].reshape(layers, shards, count // shards)
            return lax.dynamic_index_in_dim(cut, me, axis=1, keepdims=False)

        stacked = [
            jnp.stack([weight_grads[layer][index] for layer in range(layers)]) for index in range(5)
        ]
        return (
            block_out,
            input_grad,
            owned(0, width),
            owned(width, width),
            stacked[0],
            owned(4 * width, 3 * width),
            stacked[1],
            owned(2 * width, width),
            owned(3 * width, width),
            stacked[2],
            stacked[3],
            stacked[4],
        )

    return local


class Exchange:
    def __init__(self, mesh):
        self.shards = mesh.shape["shard"]
        self.reps = mesh.shape["rep"]
        self.cube = self.shards == 8
        self.line = self.reps == 4

    def swap(self, values, bit):
        pairs = [(i, i ^ bit) for i in range(self.shards)]
        return lax.ppermute(values, "shard", pairs)

    def gather(self, own):
        if not self.cube:
            return lax.all_gather(own, "shard", axis=0, tiled=False)
        first = self.swap(own, 1)
        x, y, d = self.swap(own, 2), self.swap(own, 4), self.swap(own, 6)
        others = self.swap(jnp.stack([x, y, d]), 1)
        return jnp.stack([own, first, x, others[0], y, others[1], d, others[2]])

    def scatter_sum(self, blocks):
        if not self.cube:
            return lax.psum_scatter(blocks.astype(bf16), "shard", scatter_dimension=0, tiled=False).astype(f32)
        low = blocks.astype(bf16)
        arrived = self.swap(jnp.stack([low[1], low[3], low[5], low[7]]), 1).astype(f32)
        x = self.swap((blocks[2] + arrived[1]).astype(bf16), 2)
        y = self.swap((blocks[4] + arrived[2]).astype(bf16), 4)
        d = self.swap((blocks[6] + arrived[3]).astype(bf16), 6)
        own = blocks[0] + arrived[0]
        return own + x.astype(f32) + (y.astype(f32) + d.astype(f32))

    def spread(self, blocks):
        return lax.all_to_all(blocks, "shard", split_axis=0, concat_axis=0, tiled=False)

    def total(self, grad, turn=None):
        turn = turn or (lambda v: v)
        if not self.line:
            full = lax.psum(grad.astype(bf16), "rep")
            return jnp.stack([turn(full[0]), turn(full[1])]).astype(f32)
        rep = lax.axis_index("rep")
        low = grad.astype(bf16)
        inward = lax.ppermute(low, "rep", [(0, 1), (3, 2)])
        part = (grad + inward.astype(f32)).astype(bf16)
        lower = rep < 2
        sent = jnp.where(lower, part[0], part[1])
        kept = jnp.where(lower, part[1], part[0])
        middle = lax.ppermute(sent, "rep", [(1, 2), (2, 1)])
        final = turn((kept.astype(f32) + middle.astype(f32)).astype(bf16))
        other = lax.ppermute(final, "rep", [(1, 2), (2, 1)])
        whole = jnp.where(lower, jnp.stack([other, final]), jnp.stack([final, other]))
        outward = lax.ppermute(whole, "rep", [(1, 0), (2, 3)])
        return jnp.where((rep == 1) | (rep == 2), whole, outward).astype(f32)


def make_general(mesh):
    net = Exchange(mesh)
    shards = net.shards

    def local(
        hidden_in,
        segments,
        ln1_gain,
        ln1_bias,
        qkv_weight,
        qkv_bias,
        out_weight,
        ln2_gain,
        ln2_bias,
        gate_weight,
        up_weight,
        down_weight,
        cotangent,
    ):
        layers, rows = qkv_weight.shape[:2]
        width = hidden_in.shape[2]
        tokens = hidden_in.shape[1]
        head_size = width // HEADS
        scale = head_size ** (-0.5)
        own_heads = HEADS // shards
        cols = own_heads * head_size
        hidden_units = down_weight.shape[1]
        everyone = shards * tokens
        me = lax.axis_index("shard")

        small = jnp.concatenate(
            [v.reshape(-1) for v in (ln1_gain, ln1_bias, ln2_gain, ln2_bias, qkv_bias)]
        )
        small = lax.all_gather(small, "shard", axis=0, tiled=False)
        cuts = [0]
        for v in (ln1_gain, ln1_bias, ln2_gain, ln2_bias, qkv_bias):
            cuts.append(cuts[-1] + v.size)

        def whole_of(index, like):
            part = small[:, cuts[index] : cuts[index + 1]].reshape(shards, layers, like.shape[1])
            return part.transpose(1, 0, 2).reshape(layers, -1).astype(f32)

        gain1, shift1 = whole_of(0, ln1_gain), whole_of(1, ln1_bias)
        gain2, shift2 = whole_of(2, ln2_gain), whole_of(3, ln2_bias)
        bias_all = whole_of(4, qkv_bias).reshape(layers, 3, shards, cols)
        bias_own = lax.dynamic_index_in_dim(bias_all, me, axis=2, keepdims=False)
        bias_own = bias_own.reshape(layers, 3 * cols)

        group_segments = net.gather(segments[0].astype(bf16)).astype(jnp.int32)
        positions, allowed = positions_and_mask(group_segments)
        cosine, sine = rotary_tables(positions)
        allowed = allowed[:, None]

        def columns_of(weight):
            cut = weight.reshape(rows, shards, -1).transpose(1, 0, 2)
            return net.spread(cut).reshape(width, -1)

        def qkv_columns(weight):
            cut = weight.reshape(rows, 3, shards, cols).transpose(2, 0, 1, 3)
            return net.spread(cut).reshape(width, 3 * cols)

        proj_in = [qkv_columns(qkv_weight[layer]) for layer in range(layers)]
        weight_gate = [columns_of(gate_weight[layer]) for layer in range(layers)]
        weight_up = [columns_of(up_weight[layer]) for layer in range(layers)]

        def gather(values):
            return net.gather(values).reshape(everyone, -1)

        def scatter_sum(values):
            return net.scatter_sum(values.reshape(shards, tokens, -1))

        state = hidden_in[0].astype(f32)
        saved = []
        for layer in range(layers):
            xhat1, inverse1 = normalize(state)
            normed1 = gather((xhat1 * gain1[layer] + shift1[layer]).astype(bf16))
            joined = dot(normed1, proj_in[layer]) + bias_own[layer]
            split = joined.reshape(shards, tokens, 3, own_heads, head_size)
            query = rotate(split[:, :, 0], cosine, sine).astype(bf16)
            keys = rotate(split[:, :, 1], cosine, sine).astype(bf16)
            value = split[:, :, 2].astype(bf16)
            scores = (
                jnp.einsum("gqhd,gkhd->ghqk", query, keys, preferred_element_type=f32) * scale
            )
            masked = jnp.where(allowed, scores, -1000000000.0)
            peak = jnp.max(masked, axis=-1, keepdims=True)
            raised = jnp.exp(masked - peak)
            probs = raised / jnp.sum(raised, axis=-1, keepdims=True)
            probs_low = probs.astype(bf16)
            mixed = (
                jnp.einsum("ghqk,gkhd->gqhd", probs_low, value, preferred_element_type=f32)
                .astype(bf16)
                .reshape(everyone, cols)
            )
            state_mid = state + scatter_sum(dot(mixed, out_weight[layer]))
            xhat2, inverse2 = normalize(state_mid)
            normed2 = gather((xhat2 * gain2[layer] + shift2[layer]).astype(bf16))
            gate = dot(normed2, weight_gate[layer])
            upper = dot(normed2, weight_up[layer])
            inner = (jax.nn.silu(gate) * upper).astype(bf16)
            state = state_mid + scatter_sum(dot(inner, down_weight[layer]))
            saved.append(
                (xhat1, inverse1, normed1, query, keys, value, probs, mixed)
                + (xhat2, inverse2, normed2, gate, upper, inner)
            )
        block_out = state.astype(bf16)[None]

        def from_columns(grad):
            return grad.reshape(shards, 2, rows // 2, -1).transpose(1, 0, 2, 3)

        def turn_columns(half):
            return net.spread(half).transpose(1, 0, 2).reshape(rows // 2, -1)

        def turn_qkv(half):
            whole = net.spread(half).reshape(shards, rows // 2, 3, cols)
            return whole.transpose(1, 2, 0, 3).reshape(rows // 2, -1)

        def halves(grad):
            return grad.reshape(2, grad.shape[0] // 2, -1)

        grad_state = cotangent[0].astype(f32)
        weight_grads = [None] * layers
        small_grads = [None] * layers
        for layer in reversed(range(layers)):
            xhat1, inverse1, normed1, query, keys, value, probs, mixed = saved[layer][:8]
            xhat2, inverse2, normed2, gate, upper, inner = saved[layer][8:]
            down_in = gather(grad_state.astype(bf16))
            grad_inner = dot_t(down_in, down_weight[layer])
            sigmoid = jax.nn.sigmoid(gate)
            silu = gate * sigmoid
            grad_gate = (grad_inner * upper * (sigmoid * (1.0 + gate * (1.0 - sigmoid)))).astype(bf16)
            grad_up = (grad_inner * silu).astype(bf16)
            grad_normed2 = scatter_sum(
                dot_t(grad_gate, weight_gate[layer]) + dot_t(grad_up, weight_up[layer])
            )
            grad_down_weight = net.total(halves(t_dot(inner, down_in)))
            grad_gate_weight = net.total(from_columns(t_dot(normed2, grad_gate)), turn_columns)
            grad_up_weight = net.total(from_columns(t_dot(normed2, grad_up)), turn_columns)
            back2, gain2_grad, shift2_grad = normalize_back(
                grad_normed2, xhat2, inverse2, gain2[layer]
            )
            grad_state = grad_state + back2

            branch = gather(grad_state.astype(bf16))
            grad_mixed = dot_t(branch, out_weight[layer]).astype(bf16)
            grad_out_weight = net.total(halves(t_dot(mixed, branch)))
            grad_mixed = grad_mixed.reshape(shards, tokens, own_heads, head_size)
            grad_probs = jnp.einsum(
                "gqhd,gkhd->ghqk", grad_mixed, value, preferred_element_type=f32
            )
            grad_value = jnp.einsum(
                "ghqk,gqhd->gkhd", probs.astype(bf16), grad_mixed, preferred_element_type=f32
            )
            inner_sum = jnp.sum(probs * grad_probs, axis=-1, keepdims=True)
            grad_scores = (probs * (grad_probs - inner_sum)).astype(bf16)
            grad_query = (
                jnp.einsum("ghqk,gkhd->gqhd", grad_scores, keys, preferred_element_type=f32) * scale
            )
            grad_key = (
                jnp.einsum("ghqk,gqhd->gkhd", grad_scores, query, preferred_element_type=f32)
                * scale
            )
            grad_query = rotate(grad_query, cosine, -sine)
            grad_key = rotate(grad_key, cosine, -sine)
            grad_joined = jnp.stack([grad_query, grad_key, grad_value], axis=2)
            bias_grad = jnp.sum(grad_joined.astype(bf16).astype(f32), axis=(0, 1))
            grad_joined = grad_joined.reshape(everyone, 3 * cols).astype(bf16)
            grad_normed1 = scatter_sum(dot_t(grad_joined, proj_in[layer]))
            grad_qkv_weight = net.total(from_columns(t_dot(normed1, grad_joined)), turn_qkv)
            back1, gain1_grad, shift1_grad = normalize_back(
                grad_normed1, xhat1, inverse1, gain1[layer]
            )
            grad_state = grad_state + back1
            weight_grads[layer] = (
                grad_qkv_weight.reshape(rows, -1),
                grad_out_weight.reshape(rows, -1),
                grad_gate_weight.reshape(rows, -1),
                grad_up_weight.reshape(rows, -1),
                grad_down_weight.reshape(hidden_units, -1),
            )
            placed = jnp.where(
                (jnp.arange(shards) == me)[None, :, None], bias_grad.reshape(3, 1, cols), 0.0
            )
            small_grads[layer] = jnp.concatenate(
                [gain1_grad, shift1_grad, gain2_grad, shift2_grad, placed.reshape(-1)]
            )

        summed = lax.psum(jnp.stack(small_grads), ("shard", "rep"))

        def owned(begin, count):
            part = summed[:, begin : begin + count].reshape(layers, shards, count // shards)
            return lax.dynamic_index_in_dim(part, me, axis=1, keepdims=False)

        stacked = [
            jnp.stack([weight_grads[layer][index] for layer in range(layers)]) for index in range(5)
        ]
        return (
            block_out,
            grad_state.astype(bf16)[None],
            owned(0, width),
            owned(width, width),
            stacked[0],
            owned(4 * width, 3 * width),
            stacked[1],
            owned(2 * width, width),
            owned(3 * width, width),
            stacked[2],
            stacked[3],
            stacked[4],
        )

    return local


def solution(mesh):
    tokens3 = P(("shard", "rep"), None, None)
    vector = P(None, "shard")
    matrix = P(None, "shard", None)
    in_specs = (
        tokens3,
        P(("shard", "rep"), None),
        vector,
        vector,
        matrix,
        vector,
        matrix,
        vector,
        vector,
        matrix,
        matrix,
        matrix,
        tokens3,
    )
    out_specs = (
        tokens3,
        tokens3,
        vector,
        vector,
        matrix,
        vector,
        matrix,
        vector,
        vector,
        matrix,
        matrix,
        matrix,
    )
    cube = mesh.shape["shard"] == 8 and mesh.shape["rep"] == 4
    local = make_cube(mesh) if cube else make_general(mesh)
    return jax.shard_map(
        local, mesh=mesh, in_specs=in_specs, out_specs=out_specs, check_vma=False
    )
```

```python
import functools

import jax
import jax.numpy as jnp
from jax import lax
from jax.experimental import pallas as pl
from jax.experimental.pallas import tpu as pltpu
from jax.sharding import PartitionSpec as P

HEADS = 32
ROTARY = 16
HALF = ROTARY // 2

norm_eps = 1e-05
bf16 = jnp.bfloat16
f32 = jnp.float32


def dot(a, b):
    return jnp.dot(a, b, preferred_element_type=f32)


def dot_t(a, b):
    return lax.dot_general(a, b, (((1,), (1,)), ((), ())), preferred_element_type=f32)


def t_dot(a, b):
    return lax.dot_general(a, b, (((0,), (0,)), ((), ())), preferred_element_type=f32)


def normalize(values):
    centred = values - jnp.mean(values, axis=-1, keepdims=True)
    variance = jnp.mean(centred * centred, axis=-1, keepdims=True)
    inverse = lax.rsqrt(variance + norm_eps)
    return centred * inverse, inverse


def normalize_back(grad, xhat, inverse, gain):
    scaled = grad * gain
    inner = jnp.mean(scaled * xhat, axis=-1, keepdims=True)
    grad_in = inverse * (scaled - jnp.mean(scaled, axis=-1, keepdims=True) - xhat * inner)
    return grad_in, jnp.sum(grad * xhat, axis=0), jnp.sum(grad, axis=0)


def positions_and_mask(segments):
    length = segments.shape[-1]
    earlier = (segments[..., None, :] < segments[..., :, None]).astype(jnp.int32)
    starts = jnp.sum(earlier, axis=-1)
    places = jnp.arange(length, dtype=jnp.int32)
    positions = places - starts
    allowed = (segments[..., None, :] == segments[..., :, None]) & (
        places[None, :] <= places[:, None]
    )
    return positions, allowed


def rotary_tables(positions):
    exponents = jnp.arange(HALF, dtype=f32) * (2.0 / ROTARY)
    inverse = 10000.0 ** (-exponents)
    angles = positions.astype(f32)[..., None] * inverse
    return jnp.cos(angles)[..., None, :], jnp.sin(angles)[..., None, :]


def rotate(heads_in, cosine, sine):
    leading = heads_in[..., :HALF]
    trailing = heads_in[..., HALF:ROTARY]
    return jnp.concatenate(
        [
            leading * cosine - trailing * sine,
            trailing * cosine + leading * sine,
            heads_in[..., ROTARY:],
        ],
        axis=-1,
    )


def corner(values):
    if values.size < 1 << 20:
        return values
    short = values.reshape(-1, values.shape[-1])
    return lax.slice(short, (0, 0), (8, 128))


microsecond = 1_150_000_000


def call(kernel, grid, in_specs, out_specs, out_shape, vmem=48, aliases=None, weight=1000):
    reads = len(in_specs)

    def run(*operands, after=()):
        after = [corner(v) for v in after]

        def body(*refs):
            kernel(*refs[:reads], *refs[reads + len(after) :])

        specs = list(in_specs) + [pl.BlockSpec(memory_space=pl.ANY)] * len(after)
        return pl.pallas_call(
            body,
            grid=grid or (),
            in_specs=specs,
            out_specs=out_specs,
            out_shape=out_shape,
            input_output_aliases=aliases or {},
            compiler_params=pltpu.CompilerParams(vmem_limit_bytes=vmem << 20),
            cost_estimate=pl.CostEstimate(flops=weight, bytes_accessed=1000, transcendentals=0),
        )(*operands, *after)

    return run


def hold(values, after):
    anywhere = pl.BlockSpec(memory_space=pl.ANY)
    shape = jax.ShapeDtypeStruct(values.shape, values.dtype)
    return call(lambda *_: None, None, [anywhere], anywhere, shape, 48, aliases={0: 0})(values, after=after)


def whole(shape, layer=None):
    at = (layer or 0,) + (0,) * (len(shape) - 1)
    return pl.BlockSpec(shape, lambda *_: at, pipeline_mode=pl.Buffered(1))


def shape_of(shape, dtype):
    return jax.ShapeDtypeStruct(shape, dtype)


def head_lanes(values, head, head_size):
    lanes = lax.broadcasted_iota(jnp.int32, values.shape, 1)
    inside = (lanes >= head * head_size) & (lanes < (head + 1) * head_size)
    return jnp.where(inside, values, jnp.zeros_like(values))


def stack_heads(values, heads, head_size):
    return jnp.concatenate([head_lanes(values, h, head_size) for h in range(heads)], axis=0)


def own_lanes(blocks, heads, head_size):
    tokens = blocks.shape[0] // heads
    total = None
    for h in range(heads):
        term = head_lanes(blocks[h * tokens : (h + 1) * tokens], h, head_size)
        total = term if total is None else total + term
    return total


def attention(q_heads, keys, mask, heads, head_size):
    allowed = jnp.concatenate([mask] * heads, axis=0) > 0.5
    scores = dot_t(q_heads, keys) * head_size ** (-0.5)
    masked = jnp.where(allowed, scores, -1000000000.0)
    raised = jnp.exp(masked - jnp.max(masked, axis=-1, keepdims=True))
    return raised / jnp.sum(raised, axis=-1, keepdims=True)


def join_rows(own_ref, pair_ref):
    pieces = []
    for s in range(own_ref.shape[0]):
        pieces += [own_ref[s], pair_ref[s]]
    return jnp.concatenate(pieces, axis=0)


def part_rows(values, keep_ref, send_ref):
    count, half, _ = keep_ref.shape
    for s in range(count):
        first = 2 * s * half
        keep_ref[s] = values[first : first + half]
        send_ref[s] = values[first + half : first + 2 * half].astype(bf16)


def attend_kernel(
    own_ref, pair_ref, w_ref, bias_ref, cos_ref, low_ref, high_ref, mask_ref, out_w_ref,
    keep_ref, send_ref, normed_ref, q_ref, k_ref, v_ref, mixed_ref,
    *, heads, head_size,
):
    cols = heads * head_size
    normed = join_rows(own_ref, pair_ref)
    normed_ref[...] = normed
    joined = dot(normed, w_ref[...]) + bias_ref[...]
    cosine, low, high = cos_ref[...], low_ref[...], high_ref[...]

    def turn(v):
        return v * cosine + pltpu.roll(v, cols - HALF, 1) * low + pltpu.roll(v, HALF, 1) * high

    q = turn(joined[:, :cols]).astype(bf16)
    k = turn(joined[:, cols : 2 * cols]).astype(bf16)
    v = joined[:, 2 * cols :].astype(bf16)
    q_ref[...] = q
    k_ref[...] = k
    v_ref[...] = v
    tokens = mask_ref.shape[1]
    mixed = []
    for s in range(mask_ref.shape[0]):
        at = slice(s * tokens, (s + 1) * tokens)
        probs = attention(stack_heads(q[at], heads, head_size), k[at], mask_ref[s], heads, head_size)
        terms = dot(probs.astype(bf16), v[at])
        mixed.append(own_lanes(terms, heads, head_size).astype(bf16))
    mixed = jnp.concatenate(mixed, axis=0)
    mixed_ref[...] = mixed
    part_rows(dot(mixed, out_w_ref[0]), keep_ref, send_ref)


def attend_back_kernel(
    own_ref, pair_ref, w_ref, cos_ref, low_ref, high_ref, mask_ref, out_w_ref, q_ref, k_ref, v_ref,
    keep_ref, send_ref, branch_ref, joined_ref, bias_ref,
    *, heads, head_size,
):
    cols = heads * head_size
    scale = head_size ** (-0.5)
    branch = join_rows(own_ref, pair_ref)
    branch_ref[...] = branch
    grad_mixed = dot_t(branch, out_w_ref[0]).astype(bf16)
    cosine, low, high = cos_ref[...], low_ref[...], high_ref[...]

    def turn_back(v):
        return v * cosine - pltpu.roll(v, cols - HALF, 1) * low - pltpu.roll(v, HALF, 1) * high

    q, k, v = q_ref[...], k_ref[...], v_ref[...]
    tokens = mask_ref.shape[1]
    grad_q, grad_k, grad_v = [], [], []
    for s in range(mask_ref.shape[0]):
        at = slice(s * tokens, (s + 1) * tokens)
        q_heads = stack_heads(q[at], heads, head_size)
        g_heads = stack_heads(grad_mixed[at], heads, head_size)
        probs = attention(q_heads, k[at], mask_ref[s], heads, head_size)
        grad_probs = dot_t(g_heads, v[at])
        inner = jnp.sum(probs * grad_probs, axis=-1, keepdims=True)
        grad_scores = (probs * (grad_probs - inner)).astype(bf16)
        sums = (
            own_lanes(dot(grad_scores, k[at]), heads, head_size),
            t_dot(grad_scores, q_heads),
            t_dot(probs.astype(bf16), g_heads),
        )
        grad_q.append(sums[0] * scale)
        grad_k.append(sums[1] * scale)
        grad_v.append(sums[2])
    joined = jnp.concatenate(
        [
            turn_back(jnp.concatenate(grad_q, axis=0)),
            turn_back(jnp.concatenate(grad_k, axis=0)),
            jnp.concatenate(grad_v, axis=0),
        ],
        axis=1,
    ).astype(bf16)
    joined_ref[...] = joined

    @pl.when(pl.program_id(0) == 0)
    def _():
        bias_ref[...] = jnp.zeros_like(bias_ref)

    bias_ref[...] += jnp.sum(joined.astype(f32), axis=0, keepdims=True)
    part_rows(dot_t(joined, w_ref[...]), keep_ref, send_ref)


def feed_kernel(own_ref, pair_ref, w_ref, down_ref, keep_ref, send_ref, both_ref):
    both = dot(join_rows(own_ref, pair_ref), w_ref[...])
    both_ref[...] = both
    hidden = both.shape[1] // 2
    gate, upper = both[:, :hidden], both[:, hidden:]
    inner = (gate / (1.0 + jnp.exp(-gate)) * upper).astype(bf16)
    part_rows(dot(inner, down_ref[0]), keep_ref, send_ref)


def feed_back_kernel(own_ref, pair_ref, w_ref, down_ref, both_ref, keep_ref, send_ref):
    grad_inner = dot_t(join_rows(own_ref, pair_ref), down_ref[0])
    hidden = grad_inner.shape[1]
    gate, upper = both_ref[:, :hidden], both_ref[:, hidden:]
    sigmoid = 1.0 / (1.0 + jnp.exp(-gate))
    slope = sigmoid * (1.0 + gate * (1.0 - sigmoid))
    grad_gate = (grad_inner * upper * slope).astype(bf16)
    grad_upper = (grad_inner * (gate * sigmoid)).astype(bf16)
    grad_both = jnp.concatenate([grad_gate, grad_upper], axis=1)
    part_rows(dot_t(grad_both, w_ref[...]), keep_ref, send_ref)


def feed_again_kernel(normed_ref, down_in_ref, w_ref, down_ref, *refs):
    grad_both_ref, inner_ref, token_ref = refs[-3:]
    token_ref[...] = jnp.zeros_like(token_ref)
    both = dot(normed_ref[...], w_ref[...])
    grad_inner = dot_t(down_in_ref[...], down_ref[0])
    hidden = grad_inner.shape[1]
    gate, upper = both[:, :hidden], both[:, hidden:]
    sigmoid = 1.0 / (1.0 + jnp.exp(-gate))
    silu = gate * sigmoid
    inner_ref[...] = (silu * upper).astype(bf16)
    slope = sigmoid * (1.0 + gate * (1.0 - sigmoid))
    grad_both_ref[:, :hidden] = (grad_inner * upper * slope).astype(bf16)
    grad_both_ref[:, hidden:] = (grad_inner * silu).astype(bf16)


def all_rows_kernel(first_ref, second_ref, right_ref, out_ref):
    count = first_ref.shape[0]
    total = t_dot(first_ref[...], right_ref[:count]) + t_dot(second_ref[...], right_ref[count:])
    out_ref[0] = total.astype(bf16)


def all_down_kernel(left_ref, first_ref, second_ref, *refs):
    count = first_ref.shape[0]
    refs[-1][0] = t_dot(left_ref[:count], first_ref[...]) + t_dot(left_ref[count:], second_ref[...])


def weight_quarters_kernel(first_ref, second_ref, first_grad_ref, second_grad_ref, *refs):
    out_ref = refs[-1]
    product = t_dot(first_ref[...], first_grad_ref[...]) + t_dot(second_ref[...], second_grad_ref[...])
    product = product.astype(bf16)
    quarter = product.shape[0] // out_ref.shape[0]
    for k in range(out_ref.shape[0]):
        out_ref[k, 0] = product[k * quarter : (k + 1) * quarter]


def write_blocks_kernel(blocks_ref, *refs, place, outputs):
    place(blocks_ref, *refs[len(refs) - outputs :])


def combine_kernel(keep_ref, arrived_ref, own_ref, x_ref, y_ref, d_ref):
    own_ref[...] = keep_ref[0] + arrived_ref[0].astype(f32)
    for k, ref in ((1, x_ref), (2, y_ref), (3, d_ref)):
        ref[...] = (keep_ref[k] + arrived_ref[k].astype(f32)).astype(bf16)


def received(own_ref, x_ref, y_ref, d_ref):
    return own_ref[...] + x_ref[...].astype(f32) + (y_ref[...].astype(f32) + d_ref[...].astype(f32))


def norm_first_kernel(state_ref, gain_ref, shift_ref, normed_ref):
    xhat, _ = normalize(state_ref[...])
    normed_ref[...] = (xhat * gain_ref[...] + shift_ref[...]).astype(bf16)


def norm_kernel(state_ref, own_ref, x_ref, y_ref, d_ref, gain_ref, shift_ref, new_ref, normed_ref):
    state = state_ref[...] + received(own_ref, x_ref, y_ref, d_ref)
    new_ref[...] = state
    xhat, _ = normalize(state)
    normed_ref[...] = (xhat * gain_ref[...] + shift_ref[...]).astype(bf16)


def last_kernel(state_ref, own_ref, x_ref, y_ref, d_ref, out_ref):
    out_ref[...] = (state_ref[...] + received(own_ref, x_ref, y_ref, d_ref)).astype(bf16)


def norm_back_kernel(
    grad_ref, own_ref, x_ref, y_ref, d_ref, state_ref, gain_ref, new_ref, low_ref, sums_ref
):
    grad_normed = received(own_ref, x_ref, y_ref, d_ref)
    xhat, inverse = normalize(state_ref[...])
    scaled = grad_normed * gain_ref[...]
    inner = jnp.mean(scaled * xhat, axis=-1, keepdims=True)
    back = inverse * (scaled - jnp.mean(scaled, axis=-1, keepdims=True) - xhat * inner)
    grad = grad_ref[...] + back
    new_ref[...] = grad
    low_ref[...] = grad.astype(bf16)
    sums_ref[0:1] = jnp.sum(grad_normed * xhat, axis=0, keepdims=True)
    sums_ref[1:2] = jnp.sum(grad_normed, axis=0, keepdims=True)


def cut_qkv_kernel(weight_ref, out_ref):
    shards, _, n = out_ref.shape
    cols = n // 3
    for s in range(shards):
        for t in range(3):
            first = (t * shards + s) * cols
            out_ref[s, :, t * cols : (t + 1) * cols] = weight_ref[0, :, first : first + cols]


def cut_feed_kernel(gate_ref, up_ref, out_ref):
    shards, _, n = out_ref.shape
    n = n // 2
    for s in range(shards):
        out_ref[s, :, :n] = gate_ref[0, :, s * n : (s + 1) * n]
        out_ref[s, :, n:] = up_ref[0, :, s * n : (s + 1) * n]


def stack_kernel(a_ref, b_ref, c_ref, d_ref, out_ref):
    for k, ref in enumerate((a_ref, b_ref, c_ref, d_ref)):
        out_ref[k] = ref[...]


def join_kernel(first_ref, second_ref, out_ref):
    out_ref[0] = first_ref[...]
    out_ref[1] = second_ref[...]


def unpack_kernel(packed_ref, out_ref):
    out_ref[...] = packed_ref[:, :, : out_ref.shape[2]]


def pack_kernel(first_ref, packed_ref, out_ref):
    n = first_ref.shape[2]
    out_ref[:, :, :n] = first_ref[...]
    out_ref[:, :, n:] = packed_ref[:, :, n:]


def place_blocks(ref, out_ref):
    n = ref.shape[2]
    for s in range(ref.shape[0]):
        out_ref[0, :, s * n : (s + 1) * n] = ref[s].astype(f32)


def place_feed(ref, gate_ref, up_ref):
    shards, _, n = ref.shape
    n = n // 2
    for s in range(shards):
        gate_ref[0, :, s * n : (s + 1) * n] = ref[s, :, :n].astype(f32)
        up_ref[0, :, s * n : (s + 1) * n] = ref[s, :, n:].astype(f32)


def place_qkv(ref, out_ref):
    shards, _, n = ref.shape
    cols = n // 3
    for s in range(shards):
        for t in range(3):
            first = (t * shards + s) * cols
            out_ref[0, :, first : first + cols] = ref[s, :, t * cols : (t + 1) * cols].astype(f32)


def make_cube(mesh):
    shards, reps = 8, 4

    def swap(values, bit):
        return lax.ppermute(values, "shard", [(i, i ^ bit) for i in range(shards)])

    def local(
        hidden_in,
        segments,
        ln1_gain,
        ln1_bias,
        qkv_weight,
        qkv_bias,
        out_weight,
        ln2_gain,
        ln2_bias,
        gate_weight,
        up_weight,
        down_weight,
        cotangent,
    ):
        layers, rows = qkv_weight.shape[:2]
        width = hidden_in.shape[2]
        tokens = hidden_in.shape[1]
        part = tokens // 2
        head_size = width // HEADS
        heads = HEADS // shards
        cols = heads * head_size
        hidden = down_weight.shape[1]
        chips = shards // 2
        many = chips * tokens
        step = 2 * tokens
        me = lax.axis_index("shard")
        core = me % 2

        smalls = (ln1_gain, ln1_bias, ln2_gain, ln2_bias, qkv_bias, segments.astype(bf16))
        small = lax.all_gather(
            jnp.concatenate([v.reshape(-1) for v in smalls]), "shard", axis=0, tiled=False
        )
        cuts = [0]
        for v in smalls:
            cuts.append(cuts[-1] + v.size)

        def whole_of(index):
            like = smalls[index]
            cut = small[:, cuts[index] : cuts[index + 1]].reshape(shards, layers, like.shape[1])
            return cut.transpose(1, 0, 2).reshape(layers, -1).astype(f32)

        gain1, shift1, gain2, shift2 = (whole_of(i) for i in range(4))
        bias_all = whole_of(4).reshape(layers, 3, shards, cols)
        bias_own = lax.dynamic_index_in_dim(bias_all, me, axis=2, keepdims=False)
        bias_own = bias_own.reshape(layers, 1, 3 * cols)
        all_segments = small[:, cuts[5] : cuts[6]]

        places = jnp.arange(tokens, dtype=jnp.int32)
        places = jnp.where(core == 0, places, (places + part) % tokens)
        exponents = jnp.arange(HALF, dtype=f32) * (2.0 / ROTARY)
        inverse = 10000.0 ** (-exponents)
        masks, tables = [], []
        for h in range(2):
            wanted = (me // 2 ^ jnp.arange(chips)) * 2 + h
            picked = (wanted[:, None] == jnp.arange(shards)[None]).astype(bf16)
            numbers = dot(picked, all_segments)
            numbers = jnp.where(core == 0, numbers, jnp.roll(numbers, part, axis=1))
            earlier = numbers[:, None, :] < numbers[:, :, None]
            positions = places - jnp.sum(earlier.astype(jnp.int32), axis=-1)
            allowed = (numbers[:, None, :] == numbers[:, :, None]) & (
                places[None, :] <= places[:, None]
            )
            masks.append(allowed.astype(f32))
            angles = positions.astype(f32).reshape(many, 1) * inverse
            cosine, sine = jnp.cos(angles), jnp.sin(angles)
            zero8 = jnp.zeros_like(sine)
            rest = jnp.zeros((many, head_size - ROTARY), f32)
            tables.append(
                [
                    jnp.tile(jnp.concatenate(pieces, axis=1), (1, heads))
                    for pieces in (
                        (cosine, cosine, rest + 1.0),
                        (-sine, zero8, rest),
                        (zero8, sine, rest),
                    )
                ]
            )

        def spread(blocks):
            return lax.all_to_all(blocks, "shard", split_axis=0, concat_axis=0, tiled=False)

        def cut_columns(kernel, arrays, layer, n, after):
            cut_rows = rows // 4
            block = pl.BlockSpec((1, cut_rows, arrays[0].shape[2]), lambda i: (layer, i, 0))
            return call(
                kernel,
                (4,),
                [block] * len(arrays),
                pl.BlockSpec((shards, cut_rows, n), lambda i: (0, i, 0)),
                shape_of((shards, rows, n), bf16),
                24,
            )(*arrays, after=after)

        def cut_qkv(layer, after):
            return cut_columns(cut_qkv_kernel, [qkv_weight], layer, 3 * cols, after)

        def cut_feed(layer, after):
            return cut_columns(cut_feed_kernel, [gate_weight, up_weight], layer, 2 * hidden, after)

        def turned(blocks):
            return spread(blocks).reshape(width, blocks.shape[2])

        stack = call(
            stack_kernel,
            None,
            [pl.BlockSpec(memory_space=pltpu.VMEM)] * 4,
            pl.BlockSpec(memory_space=pltpu.VMEM),
            shape_of((chips, part, width), bf16),
            16,
        )
        combine = call(
            combine_kernel,
            None,
            [pl.BlockSpec(memory_space=pltpu.VMEM)] * 2,
            [pl.BlockSpec(memory_space=pltpu.VMEM)] * 4,
            [shape_of((part, width), f32)] + [shape_of((part, width), bf16)] * 3,
            16,
        )

        steps = chips // 2
        piece = pl.BlockSpec((2, part, width), lambda i: (i, 0, 0))

        def row_block(n):
            return pl.BlockSpec((step, n), lambda i: (i, 0))

        mask_block = pl.BlockSpec((2, tokens, tokens), lambda i: (i, 0, 0))
        table_blocks = [row_block(cols)] * 3
        part_shapes = [
            shape_of((chips, part, width), f32),
            shape_of((chips, part, width), bf16),
        ]
        options = dict(heads=heads, head_size=head_size)
        def attend(layer, *operands, after=()):
            return call(
                functools.partial(attend_kernel, **options),
                (steps,),
                [piece, piece, whole((width, 3 * cols)), whole((1, 3 * cols))]
                + table_blocks
                + [mask_block, whole((1, cols, width), layer)],
                [piece, piece, row_block(width)] + [row_block(cols)] * 4,
                part_shapes + [shape_of((many, width), bf16)] + [shape_of((many, cols), bf16)] * 4,
                weight=12 * microsecond,
            )(*operands, after=after)

        def attend_back(layer, *operands, after=()):
            bias_block = pl.BlockSpec((1, 3 * cols), lambda i: (0, 0))
            bias_shape = shape_of((1, 3 * cols), f32)
            return call(
                functools.partial(attend_back_kernel, **options),
                (steps,),
                [piece, piece, whole((width, 3 * cols))]
                + table_blocks
                + [mask_block, whole((1, cols, width), layer)]
                + [row_block(cols)] * 3,
                [piece, piece, row_block(width), row_block(3 * cols), bias_block],
                part_shapes
                + [shape_of((many, width), bf16), shape_of((many, 3 * cols), bf16), bias_shape],
                weight=12 * microsecond,
            )(*operands, after=after)

        def feed_weights(layer):
            return [whole((width, 2 * hidden)), whole((1, hidden, width), layer)]

        def feed(layer, *operands, after=()):
            return call(
                feed_kernel,
                (steps,),
                [piece, piece] + feed_weights(layer),
                [piece, piece, row_block(2 * hidden)],
                part_shapes + [shape_of((many, 2 * hidden), f32)],
                weight=12 * microsecond,
            )(*operands, after=after)

        def feed_back(layer, *operands, after=()):
            return call(
                feed_back_kernel,
                (steps,),
                [piece, piece] + feed_weights(layer) + [row_block(2 * hidden)],
                [piece, piece],
                part_shapes,
                weight=12 * microsecond,
            )(*operands, after=after)

        def small_call(kernel, n_in, out_shape):
            vmem = pl.BlockSpec(memory_space=pltpu.VMEM)
            return call(kernel, None, [vmem] * n_in, [vmem] * len(out_shape), out_shape, 16)

        low_shape, state_shape = shape_of((part, width), bf16), shape_of((part, width), f32)
        norm_first = small_call(norm_first_kernel, 3, [low_shape])
        norm = small_call(norm_kernel, 7, [state_shape, low_shape])
        last = small_call(last_kernel, 5, [low_shape])
        norm_back = small_call(norm_back_kernel, 7, [state_shape, low_shape, shape_of((2, width), f32)])

        written = {}
        shapes_of = dict(
            qkv=[qkv_weight.shape],
            feed=[gate_weight.shape, up_weight.shape],
            out=[out_weight.shape],
            down=[down_weight.shape],
        )
        places_of = dict(qkv=place_qkv, feed=place_feed, out=place_blocks)

        def write_blocks(layer, name, blocks, n, cut, first, at=0):
            parts, a, r, _ = blocks.shape
            shapes = shapes_of[name]
            earlier = written.get(name, [])
            each = r // cut
            begin = first // cut
            written[name] = call(
                functools.partial(write_blocks_kernel, place=places_of[name], outputs=len(shapes)),
                (parts, each),
                [pl.BlockSpec((None, a, cut, n), lambda i, j: (i, 0, j, at))]
                + [pl.BlockSpec(memory_space=pl.ANY)] * len(earlier),
                [pl.BlockSpec((1, cut, v[2]), lambda i, j: (layer, begin + i * each + j, 0)) for v in shapes],
                [shape_of(v, f32) for v in shapes],
                32,
                aliases={1 + k: k for k in range(len(earlier))},
            )(blocks, *earlier)

        quarter = rows // reps
        packed_shape = shape_of((reps, shards, quarter, 4 * cols), bf16)

        def weight_quarters(normed, joined, mixed, branch, after=()):
            left = pl.BlockSpec((many, rows), lambda s: (0, s))
            packed = call(
                weight_quarters_kernel,
                (shards,),
                [left, left, whole((many, 3 * cols)), whole((many, 3 * cols))],
                pl.BlockSpec((reps, 1, quarter, 3 * cols), lambda s: (0, s, 0, 0)),
                packed_shape,
                32,
            )(*normed, *joined, after=after)
            right = pl.BlockSpec((many, cols), lambda s: (0, s))
            return call(
                weight_quarters_kernel,
                (shards,),
                [whole((many, cols)), whole((many, cols)), right, right, pl.BlockSpec(memory_space=pl.ANY)],
                pl.BlockSpec((reps, 1, quarter, cols), lambda s: (0, s, 0, 3)),
                packed_shape,
                32,
                aliases={4: 0},
            )(*mixed, *branch, packed)

        def scatter_quarters(packed):
            return lax.psum_scatter(packed, "rep", scatter_dimension=0, tiled=False)

        def turn_quarters(own, after):
            vmem = pl.BlockSpec(memory_space=pltpu.VMEM)
            shape = shape_of((shards, quarter, 3 * cols), bf16)
            return spread(call(unpack_kernel, None, [vmem], vmem, shape, 16)(own, after=after))

        def gather_quarters(columns, own, after):
            vmem = pl.BlockSpec(memory_space=pltpu.VMEM)
            full = shape_of((shards, quarter, 4 * cols), bf16)
            own = call(pack_kernel, None, [vmem] * 2, vmem, full, 16)(columns, own, after=after)
            return lax.all_gather(own, "rep", axis=0, tiled=False)

        all_tokens = shards * reps * tokens
        half_tokens = all_tokens // 2

        def gather_all(halves, after=()):
            joined = call(
                join_kernel,
                None,
                [pl.BlockSpec(memory_space=pltpu.VMEM)] * 2,
                pl.BlockSpec(memory_space=pltpu.VMEM),
                shape_of((2, chips, part, width), bf16),
                24,
            )(*halves, after=after)
            return lax.all_gather(joined, "rep", axis=0, tiled=False).reshape(half_tokens, width)

        def with_pair(own, after):
            own = hold(own, after)
            return own, swap(own, 1)

        def feed_again(layer, normed, down_in, piece_at, count, earlier, after=()):
            block_rows = 2 * tokens
            side, piece = divmod(piece_at, count // 2)
            steps_in = all_tokens // count // block_rows
            source = pl.BlockSpec((block_rows, width), lambda i: (piece * steps_in + i, 0))

            def rows_of(n):
                return pl.BlockSpec((block_rows, n), lambda i: (piece_at * steps_in + i, 0))

            return call(
                feed_again_kernel,
                (steps_in,),
                [source, source]
                + feed_weights(layer)
                + [pl.BlockSpec(memory_space=pl.ANY)] * len(earlier),
                [rows_of(2 * hidden), rows_of(hidden), pl.BlockSpec((8, 128), lambda i: (0, 0))],
                [
                    shape_of((all_tokens, 2 * hidden), bf16),
                    shape_of((all_tokens, hidden), bf16),
                    shape_of((8, 128), f32),
                ],
                aliases={4 + k: k for k in range(len(earlier))},
                weight=20 * microsecond,
            )(normed[side], down_in[side], feed_in[layer], down_weight, *earlier, after=after)

        def all_columns(normed, grad_both, piece_at, count, after=()):
            n = grad_both.shape[1]
            r = rows // count
            left = pl.BlockSpec((half_tokens, r), lambda s: (0, s * count + piece_at))
            return call(
                all_rows_kernel,
                (shards,),
                [left, left, whole((all_tokens, n))],
                pl.BlockSpec((1, r, n), lambda s: (s, 0, 0)),
                shape_of((shards, r, n), bf16),
                weight=30 * microsecond,
            )(*normed, grad_both, after=after)

        def all_down(layer, inner, down_in, after=()):
            earlier = written.get("down", [])
            right = pl.BlockSpec((half_tokens, 256), lambda s: (0, s))
            written["down"] = call(
                all_down_kernel,
                (width // 256,),
                [whole((all_tokens, hidden)), right, right]
                + [pl.BlockSpec(memory_space=pl.ANY)] * len(earlier),
                [pl.BlockSpec((1, hidden, 256), lambda s: (layer, 0, s))],
                [shape_of(down_weight.shape, f32)],
                aliases={3 + k: k for k in range(len(earlier))},
                weight=20 * microsecond,
            )(inner, *down_in, *earlier, after=after)

        class Feed:
            def __init__(self, layer, normed, down_in, pieces, cuts):
                self.layer, self.normed, self.down_in = layer, normed, down_in
                self.pieces, self.cuts, self.done = pieces, cuts, 0
                self.carried, self.blocks = [], []

            def again(self, after):
                *self.carried, token = feed_again(
                    self.layer, self.normed, self.down_in, self.done, self.pieces, self.carried, after=after
                )
                self.done += 1
                return [token]

            def columns(self, after, before=()):
                got = all_columns(self.normed, self.carried[0], len(self.blocks), self.cuts, after=after)
                got = hold(got, self.blocks[-1:] + list(before))
                self.blocks.append(spread(got))
                return [got]

            def down(self, after):
                all_down(self.layer, self.carried[1], self.down_in, after=after)
                return after

            def write(self):
                r = rows // self.cuts
                for k, blocks in enumerate(self.blocks):
                    write_blocks(self.layer, "feed", blocks[None], blocks.shape[2], 32, k * r)

        def share(values):
            first, second = values[:part], values[part:]
            kept = jnp.where(core == 0, first, second)
            arrived = swap(jnp.where(core == 0, second, first), 1)
            return [jnp.where(core == 0, kept, arrived), jnp.where(core == 0, arrived, kept)]

        def unshare(halves):
            kept = jnp.where(core == 0, halves[0], halves[1])
            arrived = swap(jnp.where(core == 0, halves[1], halves[0]), 1)
            both = [jnp.where(core == 0, kept, arrived), jnp.where(core == 0, arrived, kept)]
            return jnp.concatenate(both, axis=0)[None]

        def row(values, layer):
            return values[layer : layer + 1]

        def send_low(low):
            return low, [swap(low, 2), swap(low, 4), swap(low, 6)]

        def collect(sent, after):
            mine = stack(sent[0], *sent[1], after=after)
            return mine, swap(mine, 1)

        def send_sums(outputs, after):
            own, x, y, d = combine(outputs[0], swap(outputs[1], 1), after=after)
            return own, swap(x, 2), swap(y, 4), swap(d, 6)

        def block(run, finish, ready, after=(), due=None, filler=None):
            (gathered, other), sent = ready[:2], ready[2]
            first = run(0, gathered, list(after))
            if other is None:
                other = collect(sent, [first[0]])
            if due is None:
                sums = send_sums(first, [other[0]])
                second = run(1, other, [sums[0]])
            else:
                second = run(1, other, [first[0]])
                sums = send_sums(first, [second[0]] + list(due))
            later = send_sums(second, [sums[0]])
            done = finish(0, sums, [later[0]])
            wait = [done[0]]
            sent = send_low(done[1]) if len(done) > 1 else None
            if filler:
                wait += filler(wait)
            end = finish(1, later, wait)
            if sent is None:
                return (first, second), (done, end), None, (gathered, other)
            inputs = (gathered, other)
            gathered, sent = collect(sent, [end[0]]), send_low(end[1])
            other = None if due is None else collect(sent, [gathered[0]])
            return (first, second), (done, end), (gathered, other, sent), inputs

        states = [v.astype(f32) for v in share(hidden_in[0])]
        cotangents = share(cotangent[0])
        lows = [norm_first(states[h], row(gain1, 0), row(shift1, 0))[0] for h in range(2)]
        proj_in, feed_in = [None] * layers, [None] * layers
        proj_in[0] = turned(cut_qkv(0, lows))
        sent = [send_low(low) for low in lows]
        gathered = collect(sent[0], [lows[1]] + masks + tables[0] + tables[1])
        ready = (gathered, collect(sent[1], [gathered[0]]), None)
        all_normed2, all_down_in = [None] * layers, [None] * layers
        saved = []
        for layer in range(layers):
            blocks = hold(cut_feed(layer, []), [proj_in[layer], ready[1][0]])
            feed_in[layer] = turned(blocks)
            first, done, ready, _ = block(
                lambda h, gathered, after: attend(
                    layer,
                    *gathered,
                    proj_in[layer],
                    bias_own[layer],
                    *tables[h],
                    masks[h],
                    out_weight,
                    after=after,
                ),
                lambda h, sums, after: norm(
                    states[h], *sums, row(gain2, layer), row(shift2, layer), after=after
                ),
                ready,
                [blocks],
                [feed_in[layer]],
            )
            mids = [v[0] for v in done]
            if layer == 0:
                sent = [send_low(hold(v, [mids[1]])) for v in cotangents]
                one = collect(sent[0], [ready[1][0]])
                back_ready = (one, collect(sent[1], [one[0]]), None)
                gathering = [gather_all([v[0] for v in back_ready[:2]])]
            if layer + 1 < layers:
                blocks = hold(cut_qkv(layer + 1, []), [feed_in[layer], ready[1][0]])
                proj_in[layer + 1] = turned(blocks)
                due = [proj_in[layer + 1]]
            else:
                blocks = ready[1][0]
                due = None
            second, done, ready, inputs = block(
                lambda h, gathered, after: feed(layer, *gathered, feed_in[layer], down_weight, after=after),
                lambda h, sums, after: (
                    norm(mids[h], *sums, row(gain1, layer + 1), row(shift1, layer + 1), after=after)
                    if layer + 1 < layers
                    else last(mids[h], *sums, after=after)
                ),
                ready,
                [blocks] + (gathering[:1] if layer + 1 == layers else []),
                due,
            )
            if layer + 1 == layers:
                all_down_in[-1] = with_pair(gathering[0], [second[0][0]])
                all_normed2[0] = with_pair(gathering[1], [second[1][0]])
            gathering.append(gather_all([v[0] for v in inputs]))
            saved.append(
                [(states[h],) + tuple(first[h][2:]) + (mids[h], second[h][2]) for h in range(2)]
            )
            if layer + 1 < layers:
                states = [v[0] for v in done]
        block_out = unshare([v[0] for v in done])

        grads = [v.astype(f32) for v in cotangents]
        small_grads, quarters, own = [None] * layers, [None] * layers, []
        fed = [None] * layers
        ready = back_ready
        starts = [second[0][2], second[1][2]]
        for layer in reversed(range(layers)):

            def both(index):
                return [saved[layer][h][index] for h in range(2)]

            filler = None
            if layer + 1 < layers:
                all_normed2[layer + 1] = with_pair(gathering[2], [ends[1][0]])
                fed[layer + 1] = Feed(layer + 1, all_normed2[layer + 1], all_down_in[layer + 1], 4, 1)

                def filler(wait):
                    return fed[layer + 1].again(wait)

                starts = starts + [all_normed2[layer + 1][0]]
            first, back, ready, inputs = block(
                lambda h, gathered, after: feed_back(
                    layer, *gathered, feed_in[layer], down_weight, saved[layer][h][7], after=after
                ),
                lambda h, sums, after: norm_back(
                    grads[h], *sums, saved[layer][h][6], row(gain2, layer), after=after
                ),
                ready,
                starts,
                filler=filler,
            )
            if layer + 1 < layers:
                gathering.append(gather_all([v[0] for v in inputs], [quarters[layer + 1]]))
            sums2 = back[0][2] + back[1][2]
            ahead = gathering[1:2] + [block_out] if layer > 0 else []
            if layer + 1 < layers:

                def filler(wait):
                    return fed[layer + 1].again(wait + own)

            second, ends, ready, _ = block(
                lambda h, gathered, after: attend_back(
                    layer,
                    *gathered,
                    proj_in[layer],
                    *tables[h],
                    masks[h],
                    out_weight,
                    *saved[layer][h][2:5],
                    after=after,
                ),
                lambda h, sums, after: norm_back(
                    back[h][0], *sums, saved[layer][h][0], row(gain1, layer), after=after
                ),
                ready,
                ahead,
                filler=filler,
            )
            branches, joineds = [v[2] for v in second], [v[3] for v in second]
            ended = [ends[0][0]] if layer > 0 else [ends[1][0]]
            quarters[layer] = weight_quarters(both(1), joineds, both(5), branches, after=ended)
            starts = [quarters[layer]]
            own.insert(0, scatter_quarters(quarters[layer]))
            grads, lows = [v[0] for v in ends], [v[1] for v in ends]
            sums1 = ends[0][2] + ends[1][2]
            placed = jnp.where(
                (jnp.arange(shards) == me)[None, :, None],
                (second[0][4] + second[1][4]).reshape(3, 1, cols),
                0.0,
            )
            small_grads[layer] = jnp.concatenate([sums1.reshape(-1), sums2.reshape(-1), placed.reshape(-1)])
        input_grad = unshare(lows)

        summed = [jnp.stack(small_grads)]

        def small_step():
            k, last_sum = len(summed) - 1, summed[-1]
            if k < 3:
                arrived = swap(last_sum, 1 << k)
            else:
                arrived = lax.ppermute(last_sum, "rep", [(i, i ^ (1 << (k - 3))) for i in range(reps)])
            summed.append(last_sum + arrived)
            return [summed[-1]]

        turned1 = turn_quarters(own[1], [second[1][2]])
        wait = fed[1].again([quarters[0], input_grad] + small_step())
        wait = fed[1].again(wait + small_step())
        wait = fed[1].columns(wait + small_step(), [turned1])
        all_down_in[0] = with_pair(gathering[3], wait)
        fed[0] = Feed(0, all_normed2[0], all_down_in[0], 2, 2)
        wait = fed[0].again(wait + small_step())
        packed1 = gather_quarters(turned1, own[1], wait + own[:1])
        wait = fed[0].again(wait + small_step())
        turned0 = turn_quarters(own[0], wait + [fed[1].blocks[0]])
        wait = fed[0].columns(wait, [turned0])
        packed0 = gather_quarters(turned0, own[0], wait)
        wait = fed[0].columns(wait)
        fed[1].down(wait)
        fed[0].down(wait)
        summed = summed[-1]
        for layer, packed in ((1, packed1), (0, packed0)):
            fed[layer].write()
            write_blocks(layer, "qkv", packed, 3 * cols, 32, 0)
            write_blocks(layer, "out", packed, cols, quarter, 0, 3)

        def owned(begin, count):
            cut = summed[:, begin : begin + count].reshape(layers, shards, count // shards)
            return lax.dynamic_index_in_dim(cut, me, axis=1, keepdims=False)

        return (
            block_out,
            input_grad,
            owned(0, width),
            owned(width, width),
            written["qkv"][0],
            owned(4 * width, 3 * width),
            written["out"][0],
            owned(2 * width, width),
            owned(3 * width, width),
            *written["feed"],
            written["down"][0],
        )

    return local


class Exchange:
    def __init__(self, mesh):
        self.shards = mesh.shape["shard"]
        self.reps = mesh.shape["rep"]
        self.cube = self.shards == 8
        self.line = self.reps == 4

    def swap(self, values, bit):
        pairs = [(i, i ^ bit) for i in range(self.shards)]
        return lax.ppermute(values, "shard", pairs)

    def gather(self, own):
        if not self.cube:
            return lax.all_gather(own, "shard", axis=0, tiled=False)
        first = self.swap(own, 1)
        x, y, d = self.swap(own, 2), self.swap(own, 4), self.swap(own, 6)
        others = self.swap(jnp.stack([x, y, d]), 1)
        return jnp.stack([own, first, x, others[0], y, others[1], d, others[2]])

    def scatter_sum(self, blocks):
        if not self.cube:
            return lax.psum_scatter(blocks.astype(bf16), "shard", scatter_dimension=0, tiled=False).astype(f32)
        low = blocks.astype(bf16)
        arrived = self.swap(jnp.stack([low[1], low[3], low[5], low[7]]), 1).astype(f32)
        x = self.swap((blocks[2] + arrived[1]).astype(bf16), 2)
        y = self.swap((blocks[4] + arrived[2]).astype(bf16), 4)
        d = self.swap((blocks[6] + arrived[3]).astype(bf16), 6)
        own = blocks[0] + arrived[0]
        return own + x.astype(f32) + (y.astype(f32) + d.astype(f32))

    def spread(self, blocks):
        return lax.all_to_all(blocks, "shard", split_axis=0, concat_axis=0, tiled=False)

    def total(self, grad, turn=None):
        turn = turn or (lambda v: v)
        if not self.line:
            full = lax.psum(grad.astype(bf16), "rep")
            return jnp.stack([turn(full[0]), turn(full[1])]).astype(f32)
        rep = lax.axis_index("rep")
        low = grad.astype(bf16)
        inward = lax.ppermute(low, "rep", [(0, 1), (3, 2)])
        part = (grad + inward.astype(f32)).astype(bf16)
        lower = rep < 2
        sent = jnp.where(lower, part[0], part[1])
        kept = jnp.where(lower, part[1], part[0])
        middle = lax.ppermute(sent, "rep", [(1, 2), (2, 1)])
        final = turn((kept.astype(f32) + middle.astype(f32)).astype(bf16))
        other = lax.ppermute(final, "rep", [(1, 2), (2, 1)])
        whole = jnp.where(lower, jnp.stack([other, final]), jnp.stack([final, other]))
        outward = lax.ppermute(whole, "rep", [(1, 0), (2, 3)])
        return jnp.where((rep == 1) | (rep == 2), whole, outward).astype(f32)


def make_general(mesh):
    net = Exchange(mesh)
    shards = net.shards

    def local(
        hidden_in,
        segments,
        ln1_gain,
        ln1_bias,
        qkv_weight,
        qkv_bias,
        out_weight,
        ln2_gain,
        ln2_bias,
        gate_weight,
        up_weight,
        down_weight,
        cotangent,
    ):
        layers, rows = qkv_weight.shape[:2]
        width = hidden_in.shape[2]
        tokens = hidden_in.shape[1]
        head_size = width // HEADS
        scale = head_size ** (-0.5)
        own_heads = HEADS // shards
        cols = own_heads * head_size
        hidden_units = down_weight.shape[1]
        everyone = shards * tokens
        me = lax.axis_index("shard")

        small = jnp.concatenate(
            [v.reshape(-1) for v in (ln1_gain, ln1_bias, ln2_gain, ln2_bias, qkv_bias)]
        )
        small = lax.all_gather(small, "shard", axis=0, tiled=False)
        cuts = [0]
        for v in (ln1_gain, ln1_bias, ln2_gain, ln2_bias, qkv_bias):
            cuts.append(cuts[-1] + v.size)

        def whole_of(index, like):
            part = small[:, cuts[index] : cuts[index + 1]].reshape(shards, layers, like.shape[1])
            return part.transpose(1, 0, 2).reshape(layers, -1).astype(f32)

        gain1, shift1 = whole_of(0, ln1_gain), whole_of(1, ln1_bias)
        gain2, shift2 = whole_of(2, ln2_gain), whole_of(3, ln2_bias)
        bias_all = whole_of(4, qkv_bias).reshape(layers, 3, shards, cols)
        bias_own = lax.dynamic_index_in_dim(bias_all, me, axis=2, keepdims=False)
        bias_own = bias_own.reshape(layers, 3 * cols)

        group_segments = net.gather(segments[0].astype(bf16)).astype(jnp.int32)
        positions, allowed = positions_and_mask(group_segments)
        cosine, sine = rotary_tables(positions)
        allowed = allowed[:, None]

        def columns_of(weight):
            cut = weight.reshape(rows, shards, -1).transpose(1, 0, 2)
            return net.spread(cut).reshape(width, -1)

        def qkv_columns(weight):
            cut = weight.reshape(rows, 3, shards, cols).transpose(2, 0, 1, 3)
            return net.spread(cut).reshape(width, 3 * cols)

        proj_in = [qkv_columns(qkv_weight[layer]) for layer in range(layers)]
        weight_gate = [columns_of(gate_weight[layer]) for layer in range(layers)]
        weight_up = [columns_of(up_weight[layer]) for layer in range(layers)]

        def gather(values):
            return net.gather(values).reshape(everyone, -1)

        def scatter_sum(values):
            return net.scatter_sum(values.reshape(shards, tokens, -1))

        state = hidden_in[0].astype(f32)
        saved = []
        for layer in range(layers):
            xhat1, inverse1 = normalize(state)
            normed1 = gather((xhat1 * gain1[layer] + shift1[layer]).astype(bf16))
            joined = dot(normed1, proj_in[layer]) + bias_own[layer]
            split = joined.reshape(shards, tokens, 3, own_heads, head_size)
            query = rotate(split[:, :, 0], cosine, sine).astype(bf16)
            keys = rotate(split[:, :, 1], cosine, sine).astype(bf16)
            value = split[:, :, 2].astype(bf16)
            scores = (
                jnp.einsum("gqhd,gkhd->ghqk", query, keys, preferred_element_type=f32) * scale
            )
            masked = jnp.where(allowed, scores, -1000000000.0)
            peak = jnp.max(masked, axis=-1, keepdims=True)
            raised = jnp.exp(masked - peak)
            probs = raised / jnp.sum(raised, axis=-1, keepdims=True)
            probs_low = probs.astype(bf16)
            mixed = (
                jnp.einsum("ghqk,gkhd->gqhd", probs_low, value, preferred_element_type=f32)
                .astype(bf16)
                .reshape(everyone, cols)
            )
            state_mid = state + scatter_sum(dot(mixed, out_weight[layer]))
            xhat2, inverse2 = normalize(state_mid)
            normed2 = gather((xhat2 * gain2[layer] + shift2[layer]).astype(bf16))
            gate = dot(normed2, weight_gate[layer])
            upper = dot(normed2, weight_up[layer])
            inner = (jax.nn.silu(gate) * upper).astype(bf16)
            state = state_mid + scatter_sum(dot(inner, down_weight[layer]))
            saved.append(
                (xhat1, inverse1, normed1, query, keys, value, probs, mixed)
                + (xhat2, inverse2, normed2, gate, upper, inner)
            )
        block_out = state.astype(bf16)[None]

        def from_columns(grad):
            return grad.reshape(shards, 2, rows // 2, -1).transpose(1, 0, 2, 3)

        def turn_columns(half):
            return net.spread(half).transpose(1, 0, 2).reshape(rows // 2, -1)

        def turn_qkv(half):
            whole = net.spread(half).reshape(shards, rows // 2, 3, cols)
            return whole.transpose(1, 2, 0, 3).reshape(rows // 2, -1)

        def halves(grad):
            return grad.reshape(2, grad.shape[0] // 2, -1)

        grad_state = cotangent[0].astype(f32)
        weight_grads = [None] * layers
        small_grads = [None] * layers
        for layer in reversed(range(layers)):
            xhat1, inverse1, normed1, query, keys, value, probs, mixed = saved[layer][:8]
            xhat2, inverse2, normed2, gate, upper, inner = saved[layer][8:]
            down_in = gather(grad_state.astype(bf16))
            grad_inner = dot_t(down_in, down_weight[layer])
            sigmoid = jax.nn.sigmoid(gate)
            silu = gate * sigmoid
            grad_gate = (grad_inner * upper * (sigmoid * (1.0 + gate * (1.0 - sigmoid)))).astype(bf16)
            grad_up = (grad_inner * silu).astype(bf16)
            grad_normed2 = scatter_sum(
                dot_t(grad_gate, weight_gate[layer]) + dot_t(grad_up, weight_up[layer])
            )
            grad_down_weight = net.total(halves(t_dot(inner, down_in)))
            grad_gate_weight = net.total(from_columns(t_dot(normed2, grad_gate)), turn_columns)
            grad_up_weight = net.total(from_columns(t_dot(normed2, grad_up)), turn_columns)
            back2, gain2_grad, shift2_grad = normalize_back(
                grad_normed2, xhat2, inverse2, gain2[layer]
            )
            grad_state = grad_state + back2

            branch = gather(grad_state.astype(bf16))
            grad_mixed = dot_t(branch, out_weight[layer]).astype(bf16)
            grad_out_weight = net.total(halves(t_dot(mixed, branch)))
            grad_mixed = grad_mixed.reshape(shards, tokens, own_heads, head_size)
            grad_probs = jnp.einsum(
                "gqhd,gkhd->ghqk", grad_mixed, value, preferred_element_type=f32
            )
            grad_value = jnp.einsum(
                "ghqk,gqhd->gkhd", probs.astype(bf16), grad_mixed, preferred_element_type=f32
            )
            inner_sum = jnp.sum(probs * grad_probs, axis=-1, keepdims=True)
            grad_scores = (probs * (grad_probs - inner_sum)).astype(bf16)
            grad_query = (
                jnp.einsum("ghqk,gkhd->gqhd", grad_scores, keys, preferred_element_type=f32) * scale
            )
            grad_key = (
                jnp.einsum("ghqk,gqhd->gkhd", grad_scores, query, preferred_element_type=f32)
                * scale
            )
            grad_query = rotate(grad_query, cosine, -sine)
            grad_key = rotate(grad_key, cosine, -sine)
            grad_joined = jnp.stack([grad_query, grad_key, grad_value], axis=2)
            bias_grad = jnp.sum(grad_joined.astype(bf16).astype(f32), axis=(0, 1))
            grad_joined = grad_joined.reshape(everyone, 3 * cols).astype(bf16)
            grad_normed1 = scatter_sum(dot_t(grad_joined, proj_in[layer]))
            grad_qkv_weight = net.total(from_columns(t_dot(normed1, grad_joined)), turn_qkv)
            back1, gain1_grad, shift1_grad = normalize_back(
                grad_normed1, xhat1, inverse1, gain1[layer]
            )
            grad_state = grad_state + back1
            weight_grads[layer] = (
                grad_qkv_weight.reshape(rows, -1),
                grad_out_weight.reshape(rows, -1),
                grad_gate_weight.reshape(rows, -1),
                grad_up_weight.reshape(rows, -1),
                grad_down_weight.reshape(hidden_units, -1),
            )
            placed = jnp.where(
                (jnp.arange(shards) == me)[None, :, None], bias_grad.reshape(3, 1, cols), 0.0
            )
            small_grads[layer] = jnp.concatenate(
                [gain1_grad, shift1_grad, gain2_grad, shift2_grad, placed.reshape(-1)]
            )

        summed = lax.psum(jnp.stack(small_grads), ("shard", "rep"))

        def owned(begin, count):
            part = summed[:, begin : begin + count].reshape(layers, shards, count // shards)
            return lax.dynamic_index_in_dim(part, me, axis=1, keepdims=False)

        stacked = [
            jnp.stack([weight_grads[layer][index] for layer in range(layers)]) for index in range(5)
        ]
        return (
            block_out,
            grad_state.astype(bf16)[None],
            owned(0, width),
            owned(width, width),
            stacked[0],
            owned(4 * width, 3 * width),
            stacked[1],
            owned(2 * width, width),
            owned(3 * width, width),
            stacked[2],
            stacked[3],
            stacked[4],
        )

    return local


def solution(mesh):
    tokens3 = P(("shard", "rep"), None, None)
    vector = P(None, "shard")
    matrix = P(None, "shard", None)
    in_specs = (
        tokens3,
        P(("shard", "rep"), None),
        vector,
        vector,
        matrix,
        vector,
        matrix,
        vector,
        vector,
        matrix,
        matrix,
        matrix,
        tokens3,
    )
    out_specs = (
        tokens3,
        tokens3,
        vector,
        vector,
        matrix,
        vector,
        matrix,
        vector,
        vector,
        matrix,
        matrix,
        matrix,
    )
    cube = mesh.shape["shard"] == 8 and mesh.shape["rep"] == 4
    local = make_cube(mesh) if cube else make_general(mesh)
    return jax.shard_map(
        local, mesh=mesh, in_specs=in_specs, out_specs=out_specs, check_vma=False
    )
```

```python
import functools

import jax
import jax.numpy as jnp
from jax import lax
from jax.experimental import pallas as pl
from jax.experimental.pallas import tpu as pltpu
from jax.sharding import PartitionSpec as P

HEADS = 32
ROTARY = 16
HALF = ROTARY // 2

norm_eps = 1e-05
bf16 = jnp.bfloat16
f32 = jnp.float32


def dot(a, b):
    return jnp.dot(a, b, preferred_element_type=f32)


def dot_t(a, b):
    return lax.dot_general(a, b, (((1,), (1,)), ((), ())), preferred_element_type=f32)


def t_dot(a, b):
    return lax.dot_general(a, b, (((0,), (0,)), ((), ())), preferred_element_type=f32)


def normalize(values):
    centred = values - jnp.mean(values, axis=-1, keepdims=True)
    variance = jnp.mean(centred * centred, axis=-1, keepdims=True)
    inverse = lax.rsqrt(variance + norm_eps)
    return centred * inverse, inverse


def normalize_back(grad, xhat, inverse, gain):
    scaled = grad * gain
    inner = jnp.mean(scaled * xhat, axis=-1, keepdims=True)
    grad_in = inverse * (scaled - jnp.mean(scaled, axis=-1, keepdims=True) - xhat * inner)
    return grad_in, jnp.sum(grad * xhat, axis=0), jnp.sum(grad, axis=0)


def positions_and_mask(segments):
    length = segments.shape[-1]
    earlier = (segments[..., None, :] < segments[..., :, None]).astype(jnp.int32)
    starts = jnp.sum(earlier, axis=-1)
    places = jnp.arange(length, dtype=jnp.int32)
    positions = places - starts
    allowed = (segments[..., None, :] == segments[..., :, None]) & (
        places[None, :] <= places[:, None]
    )
    return positions, allowed


def rotary_tables(positions):
    exponents = jnp.arange(HALF, dtype=f32) * (2.0 / ROTARY)
    inverse = 10000.0 ** (-exponents)
    angles = positions.astype(f32)[..., None] * inverse
    return jnp.cos(angles)[..., None, :], jnp.sin(angles)[..., None, :]


def rotate(heads_in, cosine, sine):
    leading = heads_in[..., :HALF]
    trailing = heads_in[..., HALF:ROTARY]
    return jnp.concatenate(
        [
            leading * cosine - trailing * sine,
            trailing * cosine + leading * sine,
            heads_in[..., ROTARY:],
        ],
        axis=-1,
    )


def corner(values):
    if values.size < 1 << 20:
        return values
    short = values.reshape(-1, values.shape[-1])
    return lax.slice(short, (0, 0), (8, 128))


microsecond = 1_150_000_000


def call(kernel, grid, in_specs, out_specs, out_shape, vmem=48, aliases=None, weight=1000):
    reads = len(in_specs)

    def run(*operands, after=(), pieces=True):
        after = [corner(v) for v in after] if pieces else list(after)

        def body(*refs):
            kernel(*refs[:reads], *refs[reads + len(after) :])

        specs = list(in_specs) + [pl.BlockSpec(memory_space=pl.ANY)] * len(after)
        return pl.pallas_call(
            body,
            grid=grid or (),
            in_specs=specs,
            out_specs=out_specs,
            out_shape=out_shape,
            input_output_aliases=aliases or {},
            compiler_params=pltpu.CompilerParams(vmem_limit_bytes=vmem << 20),
            cost_estimate=pl.CostEstimate(flops=weight, bytes_accessed=1000, transcendentals=0),
        )(*operands, *after)

    return run


def hold(values, after):
    anywhere = pl.BlockSpec(memory_space=pl.ANY)
    shape = jax.ShapeDtypeStruct(values.shape, values.dtype)
    run = call(lambda *_: None, None, [anywhere], anywhere, shape, 62, aliases={0: 0})
    return run(values, after=after, pieces=False)


def whole(shape, layer=None):
    at = (layer or 0,) + (0,) * (len(shape) - 1)
    return pl.BlockSpec(shape, lambda *_: at, pipeline_mode=pl.Buffered(1))


def shape_of(shape, dtype):
    return jax.ShapeDtypeStruct(shape, dtype)


def head_lanes(values, head, head_size):
    lanes = lax.broadcasted_iota(jnp.int32, values.shape, 1)
    inside = (lanes >= head * head_size) & (lanes < (head + 1) * head_size)
    return jnp.where(inside, values, jnp.zeros_like(values))


def stack_heads(values, heads, head_size):
    return jnp.concatenate([head_lanes(values, h, head_size) for h in range(heads)], axis=0)


def own_lanes(blocks, heads, head_size):
    tokens = blocks.shape[0] // heads
    total = None
    for h in range(heads):
        term = head_lanes(blocks[h * tokens : (h + 1) * tokens], h, head_size)
        total = term if total is None else total + term
    return total


def attention(q_heads, keys, mask, heads, head_size):
    allowed = jnp.concatenate([mask] * heads, axis=0) > 0.5
    scores = dot_t(q_heads, keys) * head_size ** (-0.5)
    masked = jnp.where(allowed, scores, -1000000000.0)
    raised = jnp.exp(masked - jnp.max(masked, axis=-1, keepdims=True))
    return raised / jnp.sum(raised, axis=-1, keepdims=True)


def join_rows(own_ref, pair_ref):
    pieces = []
    for s in range(own_ref.shape[0]):
        pieces += [own_ref[s], pair_ref[s]]
    return jnp.concatenate(pieces, axis=0)


def part_rows(values, keep_ref, send_ref):
    count, half, _ = keep_ref.shape
    for s in range(count):
        first = 2 * s * half
        keep_ref[s] = values[first : first + half]
        send_ref[s] = values[first + half : first + 2 * half].astype(bf16)


def attend_kernel(
    own_ref, pair_ref, w_ref, bias_ref, cos_ref, low_ref, high_ref, mask_ref, out_w_ref,
    keep_ref, send_ref, normed_ref, q_ref, k_ref, v_ref, mixed_ref,
    *, heads, head_size,
):
    cols = heads * head_size
    normed = join_rows(own_ref, pair_ref)
    normed_ref[...] = normed
    joined = dot(normed, w_ref[...]) + bias_ref[...]
    cosine, low, high = cos_ref[...], low_ref[...], high_ref[...]

    def turn(v):
        return v * cosine + pltpu.roll(v, cols - HALF, 1) * low + pltpu.roll(v, HALF, 1) * high

    q = turn(joined[:, :cols]).astype(bf16)
    k = turn(joined[:, cols : 2 * cols]).astype(bf16)
    v = joined[:, 2 * cols :].astype(bf16)
    q_ref[...] = q
    k_ref[...] = k
    v_ref[...] = v
    tokens = mask_ref.shape[1]
    mixed = []
    for s in range(mask_ref.shape[0]):
        at = slice(s * tokens, (s + 1) * tokens)
        probs = attention(stack_heads(q[at], heads, head_size), k[at], mask_ref[s], heads, head_size)
        terms = dot(probs.astype(bf16), v[at])
        mixed.append(own_lanes(terms, heads, head_size).astype(bf16))
    mixed = jnp.concatenate(mixed, axis=0)
    mixed_ref[...] = mixed
    part_rows(dot(mixed, out_w_ref[0]), keep_ref, send_ref)


def attend_back_kernel(
    own_ref, pair_ref, w_ref, cos_ref, low_ref, high_ref, mask_ref, out_w_ref, q_ref, k_ref, v_ref,
    keep_ref, send_ref, branch_ref, joined_ref, bias_ref,
    *, heads, head_size,
):
    cols = heads * head_size
    scale = head_size ** (-0.5)
    branch = join_rows(own_ref, pair_ref)
    branch_ref[...] = branch
    grad_mixed = dot_t(branch, out_w_ref[0]).astype(bf16)
    cosine, low, high = cos_ref[...], low_ref[...], high_ref[...]

    def turn_back(v):
        return v * cosine - pltpu.roll(v, cols - HALF, 1) * low - pltpu.roll(v, HALF, 1) * high

    q, k, v = q_ref[...], k_ref[...], v_ref[...]
    tokens = mask_ref.shape[1]
    grad_q, grad_k, grad_v = [], [], []
    for s in range(mask_ref.shape[0]):
        at = slice(s * tokens, (s + 1) * tokens)
        q_heads = stack_heads(q[at], heads, head_size)
        g_heads = stack_heads(grad_mixed[at], heads, head_size)
        probs = attention(q_heads, k[at], mask_ref[s], heads, head_size)
        grad_probs = dot_t(g_heads, v[at])
        inner = jnp.sum(probs * grad_probs, axis=-1, keepdims=True)
        grad_scores = (probs * (grad_probs - inner)).astype(bf16)
        sums = (
            own_lanes(dot(grad_scores, k[at]), heads, head_size),
            t_dot(grad_scores, q_heads),
            t_dot(probs.astype(bf16), g_heads),
        )
        grad_q.append(sums[0] * scale)
        grad_k.append(sums[1] * scale)
        grad_v.append(sums[2])
    joined = jnp.concatenate(
        [
            turn_back(jnp.concatenate(grad_q, axis=0)),
            turn_back(jnp.concatenate(grad_k, axis=0)),
            jnp.concatenate(grad_v, axis=0),
        ],
        axis=1,
    ).astype(bf16)
    joined_ref[...] = joined

    @pl.when(pl.program_id(0) == 0)
    def _():
        bias_ref[...] = jnp.zeros_like(bias_ref)

    bias_ref[...] += jnp.sum(joined.astype(f32), axis=0, keepdims=True)
    part_rows(dot_t(joined, w_ref[...]), keep_ref, send_ref)


def feed_kernel(own_ref, pair_ref, w_ref, down_ref, keep_ref, send_ref, both_ref):
    both = dot(join_rows(own_ref, pair_ref), w_ref[...])
    both_ref[...] = both
    hidden = both.shape[1] // 2
    gate, upper = both[:, :hidden], both[:, hidden:]
    inner = (gate / (1.0 + jnp.exp(-gate)) * upper).astype(bf16)
    part_rows(dot(inner, down_ref[0]), keep_ref, send_ref)


def feed_back_kernel(own_ref, pair_ref, w_ref, down_ref, both_ref, keep_ref, send_ref):
    grad_inner = dot_t(join_rows(own_ref, pair_ref), down_ref[0])
    hidden = grad_inner.shape[1]
    gate, upper = both_ref[:, :hidden], both_ref[:, hidden:]
    sigmoid = 1.0 / (1.0 + jnp.exp(-gate))
    slope = sigmoid * (1.0 + gate * (1.0 - sigmoid))
    grad_gate = (grad_inner * upper * slope).astype(bf16)
    grad_upper = (grad_inner * (gate * sigmoid)).astype(bf16)
    grad_both = jnp.concatenate([grad_gate, grad_upper], axis=1)
    part_rows(dot_t(grad_both, w_ref[...]), keep_ref, send_ref)


def feed_again_kernel(normed_ref, down_in_ref, w_ref, down_ref, *refs):
    grad_both_ref, inner_ref, token_ref = refs[-3:]
    token_ref[...] = jnp.zeros_like(token_ref)
    both = dot(normed_ref[...], w_ref[...])
    grad_inner = dot_t(down_in_ref[...], down_ref[0])
    hidden = grad_inner.shape[1]
    gate, upper = both[:, :hidden], both[:, hidden:]
    sigmoid = 1.0 / (1.0 + jnp.exp(-gate))
    silu = gate * sigmoid
    inner_ref[...] = (silu * upper).astype(bf16)
    slope = sigmoid * (1.0 + gate * (1.0 - sigmoid))
    grad_both_ref[:, :hidden] = (grad_inner * upper * slope).astype(bf16)
    grad_both_ref[:, hidden:] = (grad_inner * silu).astype(bf16)


def all_rows_kernel(first_ref, second_ref, right_ref, out_ref):
    count = first_ref.shape[0]
    total = t_dot(first_ref[...], right_ref[:count]) + t_dot(second_ref[...], right_ref[count:])
    out_ref[0] = total.astype(bf16)


def all_down_kernel(left_ref, first_ref, second_ref, *refs):
    count = first_ref.shape[0]
    refs[-1][0] = t_dot(left_ref[:count], first_ref[...]) + t_dot(left_ref[count:], second_ref[...])


def weight_quarters_kernel(first_ref, second_ref, first_grad_ref, second_grad_ref, *refs):
    out_ref = refs[-1]
    product = t_dot(first_ref[...], first_grad_ref[...]) + t_dot(second_ref[...], second_grad_ref[...])
    product = product.astype(bf16)
    quarter = product.shape[0] // out_ref.shape[0]
    for k in range(out_ref.shape[0]):
        out_ref[k, 0] = product[k * quarter : (k + 1) * quarter]


def write_blocks_kernel(blocks_ref, *refs, place, outputs):
    place(blocks_ref, *refs[len(refs) - outputs :])


def combine_kernel(keep_ref, arrived_ref, own_ref, x_ref, y_ref, d_ref):
    own_ref[...] = keep_ref[0] + arrived_ref[0].astype(f32)
    for k, ref in ((1, x_ref), (2, y_ref), (3, d_ref)):
        ref[...] = (keep_ref[k] + arrived_ref[k].astype(f32)).astype(bf16)


def received(own_ref, x_ref, y_ref, d_ref):
    return own_ref[...] + x_ref[...].astype(f32) + (y_ref[...].astype(f32) + d_ref[...].astype(f32))


def norm_first_kernel(state_ref, gain_ref, shift_ref, normed_ref):
    xhat, _ = normalize(state_ref[...])
    normed_ref[...] = (xhat * gain_ref[...] + shift_ref[...]).astype(bf16)


def norm_kernel(state_ref, own_ref, x_ref, y_ref, d_ref, gain_ref, shift_ref, new_ref, normed_ref):
    state = state_ref[...] + received(own_ref, x_ref, y_ref, d_ref)
    new_ref[...] = state
    xhat, _ = normalize(state)
    normed_ref[...] = (xhat * gain_ref[...] + shift_ref[...]).astype(bf16)


def last_kernel(state_ref, own_ref, x_ref, y_ref, d_ref, out_ref):
    out_ref[...] = (state_ref[...] + received(own_ref, x_ref, y_ref, d_ref)).astype(bf16)


def norm_back_kernel(
    grad_ref, own_ref, x_ref, y_ref, d_ref, state_ref, gain_ref, new_ref, low_ref, sums_ref
):
    grad_normed = received(own_ref, x_ref, y_ref, d_ref)
    xhat, inverse = normalize(state_ref[...])
    scaled = grad_normed * gain_ref[...]
    inner = jnp.mean(scaled * xhat, axis=-1, keepdims=True)
    back = inverse * (scaled - jnp.mean(scaled, axis=-1, keepdims=True) - xhat * inner)
    grad = grad_ref[...] + back
    new_ref[...] = grad
    low_ref[...] = grad.astype(bf16)
    sums_ref[0:1] = jnp.sum(grad_normed * xhat, axis=0, keepdims=True)
    sums_ref[1:2] = jnp.sum(grad_normed, axis=0, keepdims=True)


def cut_qkv_kernel(weight_ref, out_ref):
    shards, _, n = out_ref.shape
    cols = n // 3
    for s in range(shards):
        for t in range(3):
            first = (t * shards + s) * cols
            out_ref[s, :, t * cols : (t + 1) * cols] = weight_ref[0, :, first : first + cols]


def cut_feed_kernel(gate_ref, up_ref, out_ref):
    shards, _, n = out_ref.shape
    n = n // 2
    for s in range(shards):
        out_ref[s, :, :n] = gate_ref[0, :, s * n : (s + 1) * n]
        out_ref[s, :, n:] = up_ref[0, :, s * n : (s + 1) * n]


def stack_kernel(a_ref, b_ref, c_ref, d_ref, out_ref):
    for k, ref in enumerate((a_ref, b_ref, c_ref, d_ref)):
        out_ref[k] = ref[...]


def join_kernel(first_ref, second_ref, out_ref):
    out_ref[0] = first_ref[...]
    out_ref[1] = second_ref[...]


def unpack_kernel(packed_ref, out_ref):
    out_ref[...] = packed_ref[:, :, : out_ref.shape[2]]


def pack_kernel(first_ref, packed_ref, out_ref):
    n = first_ref.shape[2]
    out_ref[:, :, :n] = first_ref[...]
    out_ref[:, :, n:] = packed_ref[:, :, n:]


def place_blocks(ref, out_ref):
    n = ref.shape[2]
    for s in range(ref.shape[0]):
        out_ref[0, :, s * n : (s + 1) * n] = ref[s].astype(f32)


def place_feed(ref, gate_ref, up_ref):
    shards, _, n = ref.shape
    n = n // 2
    for s in range(shards):
        gate_ref[0, :, s * n : (s + 1) * n] = ref[s, :, :n].astype(f32)
        up_ref[0, :, s * n : (s + 1) * n] = ref[s, :, n:].astype(f32)


def place_qkv(ref, out_ref):
    shards, _, n = ref.shape
    cols = n // 3
    for s in range(shards):
        for t in range(3):
            first = (t * shards + s) * cols
            out_ref[0, :, first : first + cols] = ref[s, :, t * cols : (t + 1) * cols].astype(f32)


def make_cube(mesh):
    shards, reps = 8, 4

    def swap(values, bit):
        return lax.ppermute(values, "shard", [(i, i ^ bit) for i in range(shards)])

    def local(
        hidden_in,
        segments,
        ln1_gain,
        ln1_bias,
        qkv_weight,
        qkv_bias,
        out_weight,
        ln2_gain,
        ln2_bias,
        gate_weight,
        up_weight,
        down_weight,
        cotangent,
    ):
        layers, rows = qkv_weight.shape[:2]
        width = hidden_in.shape[2]
        tokens = hidden_in.shape[1]
        part = tokens // 2
        head_size = width // HEADS
        heads = HEADS // shards
        cols = heads * head_size
        hidden = down_weight.shape[1]
        chips = shards // 2
        many = chips * tokens
        step = 2 * tokens
        me = lax.axis_index("shard")
        core = me % 2

        smalls = (ln1_gain, ln1_bias, ln2_gain, ln2_bias, qkv_bias, segments.astype(bf16))
        small = lax.all_gather(
            jnp.concatenate([v.reshape(-1) for v in smalls]), "shard", axis=0, tiled=False
        )
        cuts = [0]
        for v in smalls:
            cuts.append(cuts[-1] + v.size)

        def whole_of(index):
            like = smalls[index]
            cut = small[:, cuts[index] : cuts[index + 1]].reshape(shards, layers, like.shape[1])
            return cut.transpose(1, 0, 2).reshape(layers, -1).astype(f32)

        gain1, shift1, gain2, shift2 = (whole_of(i) for i in range(4))
        bias_all = whole_of(4).reshape(layers, 3, shards, cols)
        bias_own = lax.dynamic_index_in_dim(bias_all, me, axis=2, keepdims=False)
        bias_own = bias_own.reshape(layers, 1, 3 * cols)
        all_segments = small[:, cuts[5] : cuts[6]]

        places = jnp.arange(tokens, dtype=jnp.int32)
        places = jnp.where(core == 0, places, (places + part) % tokens)
        exponents = jnp.arange(HALF, dtype=f32) * (2.0 / ROTARY)
        inverse = 10000.0 ** (-exponents)
        masks, tables = [], []
        for h in range(2):
            wanted = (me // 2 ^ jnp.arange(chips)) * 2 + h
            picked = (wanted[:, None] == jnp.arange(shards)[None]).astype(bf16)
            numbers = dot(picked, all_segments)
            numbers = jnp.where(core == 0, numbers, jnp.roll(numbers, part, axis=1))
            earlier = numbers[:, None, :] < numbers[:, :, None]
            positions = places - jnp.sum(earlier.astype(jnp.int32), axis=-1)
            allowed = (numbers[:, None, :] == numbers[:, :, None]) & (
                places[None, :] <= places[:, None]
            )
            masks.append(allowed.astype(f32))
            angles = positions.astype(f32).reshape(many, 1) * inverse
            cosine, sine = jnp.cos(angles), jnp.sin(angles)
            zero8 = jnp.zeros_like(sine)
            rest = jnp.zeros((many, head_size - ROTARY), f32)
            tables.append(
                [
                    jnp.tile(jnp.concatenate(pieces, axis=1), (1, heads))
                    for pieces in (
                        (cosine, cosine, rest + 1.0),
                        (-sine, zero8, rest),
                        (zero8, sine, rest),
                    )
                ]
            )

        def spread(blocks):
            return lax.all_to_all(blocks, "shard", split_axis=0, concat_axis=0, tiled=False)

        def cut_columns(kernel, arrays, layer, n, after):
            cut_rows = rows // 4
            block = pl.BlockSpec((1, cut_rows, arrays[0].shape[2]), lambda i: (layer, i, 0))
            return call(
                kernel,
                (4,),
                [block] * len(arrays),
                pl.BlockSpec((shards, cut_rows, n), lambda i: (0, i, 0)),
                shape_of((shards, rows, n), bf16),
                24,
            )(*arrays, after=after)

        def cut_qkv(layer, after):
            return cut_columns(cut_qkv_kernel, [qkv_weight], layer, 3 * cols, after)

        def cut_feed(layer, after):
            return cut_columns(cut_feed_kernel, [gate_weight, up_weight], layer, 2 * hidden, after)

        def turned(blocks):
            return spread(blocks).reshape(width, blocks.shape[2])

        stack = call(
            stack_kernel,
            None,
            [pl.BlockSpec(memory_space=pltpu.VMEM)] * 4,
            pl.BlockSpec(memory_space=pltpu.VMEM),
            shape_of((chips, part, width), bf16),
            16,
        )
        combine = call(
            combine_kernel,
            None,
            [pl.BlockSpec(memory_space=pltpu.VMEM)] * 2,
            [pl.BlockSpec(memory_space=pltpu.VMEM)] * 4,
            [shape_of((part, width), f32)] + [shape_of((part, width), bf16)] * 3,
            16,
        )

        steps = chips // 2
        piece = pl.BlockSpec((2, part, width), lambda i: (i, 0, 0))

        def row_block(n):
            return pl.BlockSpec((step, n), lambda i: (i, 0))

        mask_block = pl.BlockSpec((2, tokens, tokens), lambda i: (i, 0, 0))
        table_blocks = [row_block(cols)] * 3
        part_shapes = [
            shape_of((chips, part, width), f32),
            shape_of((chips, part, width), bf16),
        ]
        options = dict(heads=heads, head_size=head_size)
        def attend(layer, *operands, after=()):
            return call(
                functools.partial(attend_kernel, **options),
                (steps,),
                [piece, piece, whole((width, 3 * cols)), whole((1, 3 * cols))]
                + table_blocks
                + [mask_block, whole((1, cols, width), layer)],
                [piece, piece, row_block(width)] + [row_block(cols)] * 4,
                part_shapes + [shape_of((many, width), bf16)] + [shape_of((many, cols), bf16)] * 4,
                weight=12 * microsecond,
            )(*operands, after=after)

        def attend_back(layer, *operands, after=()):
            bias_block = pl.BlockSpec((1, 3 * cols), lambda i: (0, 0))
            bias_shape = shape_of((1, 3 * cols), f32)
            return call(
                functools.partial(attend_back_kernel, **options),
                (steps,),
                [piece, piece, whole((width, 3 * cols))]
                + table_blocks
                + [mask_block, whole((1, cols, width), layer)]
                + [row_block(cols)] * 3,
                [piece, piece, row_block(width), row_block(3 * cols), bias_block],
                part_shapes
                + [shape_of((many, width), bf16), shape_of((many, 3 * cols), bf16), bias_shape],
                weight=12 * microsecond,
            )(*operands, after=after)

        def feed_weights(layer):
            return [whole((width, 2 * hidden)), whole((1, hidden, width), layer)]

        def feed(layer, *operands, after=()):
            return call(
                feed_kernel,
                (steps,),
                [piece, piece] + feed_weights(layer),
                [piece, piece, row_block(2 * hidden)],
                part_shapes + [shape_of((many, 2 * hidden), f32)],
                weight=12 * microsecond,
            )(*operands, after=after)

        def feed_back(layer, *operands, after=()):
            return call(
                feed_back_kernel,
                (steps,),
                [piece, piece] + feed_weights(layer) + [row_block(2 * hidden)],
                [piece, piece],
                part_shapes,
                weight=12 * microsecond,
            )(*operands, after=after)

        def small_call(kernel, n_in, out_shape):
            vmem = pl.BlockSpec(memory_space=pltpu.VMEM)
            return call(kernel, None, [vmem] * n_in, [vmem] * len(out_shape), out_shape, 16)

        low_shape, state_shape = shape_of((part, width), bf16), shape_of((part, width), f32)
        norm_first = small_call(norm_first_kernel, 3, [low_shape])
        norm = small_call(norm_kernel, 7, [state_shape, low_shape])
        last = small_call(last_kernel, 5, [low_shape])
        norm_back = small_call(norm_back_kernel, 7, [state_shape, low_shape, shape_of((2, width), f32)])

        written = {}
        shapes_of = dict(
            qkv=[qkv_weight.shape],
            feed=[gate_weight.shape, up_weight.shape],
            out=[out_weight.shape],
            down=[down_weight.shape],
        )
        places_of = dict(qkv=place_qkv, feed=place_feed, out=place_blocks)

        def write_blocks(layer, name, blocks, n, cut, first, at=0, after=()):
            parts, a, r, _ = blocks.shape
            shapes = shapes_of[name]
            earlier = written.get(name, [])
            each = r // cut
            begin = first // cut
            written[name] = call(
                functools.partial(write_blocks_kernel, place=places_of[name], outputs=len(shapes)),
                (parts, each),
                [pl.BlockSpec((None, a, cut, n), lambda i, j: (i, 0, j, at))]
                + [pl.BlockSpec(memory_space=pl.ANY)] * len(earlier),
                [pl.BlockSpec((1, cut, v[2]), lambda i, j: (layer, begin + i * each + j, 0)) for v in shapes],
                [shape_of(v, f32) for v in shapes],
                32,
                aliases={1 + k: k for k in range(len(earlier))},
            )(blocks, *earlier, after=after)

        quarter = rows // reps
        packed_shape = shape_of((reps, shards, quarter, 4 * cols), bf16)

        def weight_quarters(normed, joined, mixed, branch, after=()):
            left = pl.BlockSpec((many, rows), lambda s: (0, s))
            packed = call(
                weight_quarters_kernel,
                (shards,),
                [left, left, whole((many, 3 * cols)), whole((many, 3 * cols))],
                pl.BlockSpec((reps, 1, quarter, 3 * cols), lambda s: (0, s, 0, 0)),
                packed_shape,
                32,
            )(*normed, *joined, after=after)
            right = pl.BlockSpec((many, cols), lambda s: (0, s))
            return call(
                weight_quarters_kernel,
                (shards,),
                [whole((many, cols)), whole((many, cols)), right, right, pl.BlockSpec(memory_space=pl.ANY)],
                pl.BlockSpec((reps, 1, quarter, cols), lambda s: (0, s, 0, 3)),
                packed_shape,
                32,
                aliases={4: 0},
            )(*mixed, *branch, packed)

        def scatter_quarters(packed):
            return lax.psum_scatter(packed, "rep", scatter_dimension=0, tiled=False)

        def turn_quarters(own, after):
            vmem = pl.BlockSpec(memory_space=pltpu.VMEM)
            shape = shape_of((shards, quarter, 3 * cols), bf16)
            return spread(call(unpack_kernel, None, [vmem], vmem, shape, 16)(own, after=after))

        def gather_quarters(columns, own, after):
            vmem = pl.BlockSpec(memory_space=pltpu.VMEM)
            full = shape_of((shards, quarter, 4 * cols), bf16)
            own = call(pack_kernel, None, [vmem] * 2, vmem, full, 16)(columns, own, after=after)
            return lax.all_gather(own, "rep", axis=0, tiled=False)

        all_tokens = shards * reps * tokens
        half_tokens = all_tokens // 2

        def gather_all(halves, after=()):
            joined = call(
                join_kernel,
                None,
                [pl.BlockSpec(memory_space=pltpu.VMEM)] * 2,
                pl.BlockSpec(memory_space=pltpu.VMEM),
                shape_of((2, chips, part, width), bf16),
                24,
            )(*halves, after=after)
            return lax.all_gather(joined, "rep", axis=0, tiled=False).reshape(half_tokens, width)

        def with_pair(own, after):
            own = hold(own, after)
            return own, swap(own, 1)

        def feed_again(layer, normed, down_in, piece_at, count, earlier, after=()):
            block_rows = 2 * tokens
            side, piece = divmod(piece_at, count // 2)
            steps_in = all_tokens // count // block_rows
            source = pl.BlockSpec((block_rows, width), lambda i: (piece * steps_in + i, 0))

            def rows_of(n):
                return pl.BlockSpec((block_rows, n), lambda i: (piece_at * steps_in + i, 0))

            return call(
                feed_again_kernel,
                (steps_in,),
                [source, source]
                + feed_weights(layer)
                + [pl.BlockSpec(memory_space=pl.ANY)] * len(earlier),
                [rows_of(2 * hidden), rows_of(hidden), pl.BlockSpec((8, 128), lambda i: (0, 0))],
                [
                    shape_of((all_tokens, 2 * hidden), bf16),
                    shape_of((all_tokens, hidden), bf16),
                    shape_of((8, 128), f32),
                ],
                aliases={4 + k: k for k in range(len(earlier))},
                weight=20 * microsecond,
            )(normed[side], down_in[side], feed_in[layer], down_weight, *earlier, after=after)

        def all_columns(normed, grad_both, piece_at, count, after=()):
            n = grad_both.shape[1]
            r = rows // count
            left = pl.BlockSpec((half_tokens, r), lambda s: (0, s * count + piece_at))
            return call(
                all_rows_kernel,
                (shards,),
                [left, left, whole((all_tokens, n))],
                pl.BlockSpec((1, r, n), lambda s: (s, 0, 0)),
                shape_of((shards, r, n), bf16),
                weight=30 * microsecond,
            )(*normed, grad_both, after=after)

        def all_down(layer, inner, down_in, after=()):
            earlier = written.get("down", [])
            right = pl.BlockSpec((half_tokens, 256), lambda s: (0, s))
            written["down"] = call(
                all_down_kernel,
                (width // 256,),
                [whole((all_tokens, hidden)), right, right]
                + [pl.BlockSpec(memory_space=pl.ANY)] * len(earlier),
                [pl.BlockSpec((1, hidden, 256), lambda s: (layer, 0, s))],
                [shape_of(down_weight.shape, f32)],
                aliases={3 + k: k for k in range(len(earlier))},
                weight=20 * microsecond,
            )(inner, *down_in, *earlier, after=after)

        class Feed:
            def __init__(self, layer, normed, down_in, pieces, cuts):
                self.layer, self.normed, self.down_in = layer, normed, down_in
                self.pieces, self.cuts, self.done = pieces, cuts, 0
                self.carried, self.blocks = [], []

            def again(self, after):
                *self.carried, token = feed_again(
                    self.layer, self.normed, self.down_in, self.done, self.pieces, self.carried, after=after
                )
                self.done += 1
                return [token]

            def columns_now(self, after):
                self.got = all_columns(self.normed, self.carried[0], len(self.blocks), self.cuts, after=after)
                return [self.got]

            def columns_held(self, before=()):
                got = hold(self.got, self.blocks[-1:] + list(before))
                self.blocks.append(spread(got))
                return [got]

            def columns(self, after, before=()):
                self.columns_now(after)
                return self.columns_held(before)

            def down(self, after):
                all_down(self.layer, self.carried[1], self.down_in, after=after)
                return after

            def write(self, after=()):
                r = rows // self.cuts
                for k, blocks in enumerate(self.blocks):
                    write_blocks(self.layer, "feed", blocks[None], blocks.shape[2], 32, k * r, after=after)

        def share(values):
            first, second = values[:part], values[part:]
            kept = jnp.where(core == 0, first, second)
            arrived = swap(jnp.where(core == 0, second, first), 1)
            return [jnp.where(core == 0, kept, arrived), jnp.where(core == 0, arrived, kept)]

        def unshare(halves):
            kept = jnp.where(core == 0, halves[0], halves[1])
            arrived = swap(jnp.where(core == 0, halves[1], halves[0]), 1)
            both = [jnp.where(core == 0, kept, arrived), jnp.where(core == 0, arrived, kept)]
            return jnp.concatenate(both, axis=0)[None]

        def row(values, layer):
            return values[layer : layer + 1]

        def send_low(low):
            return low, [swap(low, 2), swap(low, 4), swap(low, 6)]

        def collect(sent, after):
            mine = stack(sent[0], *sent[1], after=after)
            return mine, swap(mine, 1)

        def send_sums(outputs, after):
            own, x, y, d = combine(outputs[0], swap(outputs[1], 1), after=after)
            return own, swap(x, 2), swap(y, 4), swap(d, 6)

        def block(run, finish, ready, after=(), due=None, filler=None):
            (gathered, other), sent = ready[:2], ready[2]
            first = run(0, gathered, list(after))
            if other is None:
                other = collect(sent, [first[0]])
            if finish is None:
                return (first, run(1, other, [first[0]])), None, None, None
            if due is None:
                sums = send_sums(first, [other[0]])
                second = run(1, other, [sums[0]])
            else:
                second = run(1, other, [first[0]])
                sums = send_sums(first, [second[0]] + list(due))
            later = send_sums(second, [sums[0]])
            done = finish(0, sums, [later[0]])
            wait = [done[0]]
            sent = send_low(done[1]) if len(done) > 1 else None
            if filler:
                wait += filler(wait)
            end = finish(1, later, wait)
            if sent is None:
                return (first, second), (done, end), None, (gathered, other)
            inputs = (gathered, other)
            other_sent = send_low(end[1])
            wait = [end[0]] + (filler([end[0]]) if filler else [])
            gathered, sent = collect(sent, wait), other_sent
            other = None if due is None else collect(sent, [gathered[0]])
            return (first, second), (done, end), (gathered, other, sent), inputs

        cotangents = share(cotangent[0])
        states = [v.astype(f32) for v in share(hidden_in[0])]
        lows = [norm_first(states[h], row(gain1, 0), row(shift1, 0))[0] for h in range(2)]
        proj_in, feed_in = [None] * layers, [None] * layers
        proj_in[0] = turned(cut_qkv(0, lows))
        sent = [send_low(low) for low in lows]
        gathered = collect(sent[0], [lows[1]] + masks + tables[0] + tables[1])
        ready = (gathered, collect(sent[1], [gathered[0]]), None)
        all_normed2, all_down_in = [None] * layers, [None] * layers
        saved = []
        for layer in range(layers):
            blocks = hold(cut_feed(layer, []), [proj_in[layer], ready[1][0]])
            feed_in[layer] = turned(blocks)
            first, done, ready, _ = block(
                lambda h, gathered, after: attend(
                    layer,
                    *gathered,
                    proj_in[layer],
                    bias_own[layer],
                    *tables[h],
                    masks[h],
                    out_weight,
                    after=after,
                ),
                lambda h, sums, after: norm(
                    states[h], *sums, row(gain2, layer), row(shift2, layer), after=after
                ),
                ready,
                [blocks],
                [feed_in[layer]],
            )
            mids = [v[0] for v in done]
            if layer == 0:
                sent = [send_low(hold(v, [mids[1]])) for v in cotangents]
                one = collect(sent[0], [ready[1][0]])
                back_ready = (one, collect(sent[1], [one[0]]), None)
                gathering = [gather_all([v[0] for v in back_ready[:2]])]
            if layer + 1 < layers:
                blocks = hold(cut_qkv(layer + 1, []), [feed_in[layer], ready[1][0]])
                proj_in[layer + 1] = turned(blocks)
                due = [proj_in[layer + 1]]
            else:
                blocks = ready[1][0]
                due = None
            inputs = ready[:2]
            second, done, ready, _ = block(
                lambda h, gathered, after: feed(layer, *gathered, feed_in[layer], down_weight, after=after),
                (
                    lambda h, sums, after: norm(
                        mids[h], *sums, row(gain1, layer + 1), row(shift1, layer + 1), after=after
                    )
                )
                if layer + 1 < layers
                else None,
                ready,
                [blocks] + (gathering[:1] if layer + 1 == layers else []),
                due,
            )
            if layer + 1 == layers:
                all_down_in[-1] = with_pair(gathering[0], [second[0][0]])
                all_normed2[0] = with_pair(gathering[1], [second[1][0]])
            gathering.append(gather_all([v[0] for v in inputs]))
            saved.append(
                [(states[h],) + tuple(first[h][2:]) + (mids[h], second[h][2]) for h in range(2)]
            )
            if layer + 1 < layers:
                states = [v[0] for v in done]
        out_sums, out_mids = second, mids

        grads = [v.astype(f32) for v in cotangents]
        small_grads, quarters, own = [None] * layers, [None] * layers, []
        fed = [None] * layers
        ready = back_ready
        starts = [second[0][2], second[1][2]]
        for layer in reversed(range(layers)):

            def both(index):
                return [saved[layer][h][index] for h in range(2)]

            filler = None
            if layer + 1 < layers:
                all_normed2[layer + 1] = with_pair(gathering[2], [ends[1][0]])
                fed[layer + 1] = Feed(layer + 1, all_normed2[layer + 1], all_down_in[layer + 1], 4, 1)

                def filler(wait):
                    return fed[layer + 1].again(wait)

            first, back, ready, inputs = block(
                lambda h, gathered, after: feed_back(
                    layer, *gathered, feed_in[layer], down_weight, saved[layer][h][7], after=after
                ),
                lambda h, sums, after: norm_back(
                    grads[h], *sums, saved[layer][h][6], row(gain2, layer), after=after
                ),
                ready,
                starts,
                filler=filler,
            )
            if layer + 1 < layers:
                gathering.append(gather_all([v[0] for v in inputs], [quarters[layer + 1]]))
            sums2 = back[0][2] + back[1][2]
            ahead = gathering[1:2] if layer > 0 else []
            if layer + 1 < layers:

                def filler(wait):
                    return fed[layer + 1].again(wait + own)

            second, ends, ready, _ = block(
                lambda h, gathered, after: attend_back(
                    layer,
                    *gathered,
                    proj_in[layer],
                    *tables[h],
                    masks[h],
                    out_weight,
                    *saved[layer][h][2:5],
                    after=after,
                ),
                lambda h, sums, after: norm_back(
                    back[h][0], *sums, saved[layer][h][0], row(gain1, layer), after=after
                ),
                ready,
                ahead,
                filler=filler,
            )
            branches, joineds = [v[2] for v in second], [v[3] for v in second]
            ended = [ends[0][0]] if layer > 0 else [ends[1][0]]
            quarters[layer] = weight_quarters(both(1), joineds, both(5), branches, after=ended)
            starts = [quarters[layer]]
            own.insert(0, scatter_quarters(quarters[layer]))
            grads, lows = [v[0] for v in ends], [v[1] for v in ends]
            sums1 = ends[0][2] + ends[1][2]
            placed = jnp.where(
                (jnp.arange(shards) == me)[None, :, None],
                (second[0][4] + second[1][4]).reshape(3, 1, cols),
                0.0,
            )
            small_grads[layer] = jnp.concatenate([sums1.reshape(-1), sums2.reshape(-1), placed.reshape(-1)])
        input_grad = unshare(lows)

        summed = [jnp.stack(small_grads)]

        def small_step():
            summed.append(summed[-1] + swap(summed[-1], 1 << (len(summed) - 1)))
            return [summed[-1]]

        turned1 = turn_quarters(own[1], [second[1][2]])
        steps3 = small_step() + small_step() + small_step()
        wait = fed[1].columns([quarters[0], input_grad] + steps3, [turned1])
        packed1 = gather_quarters(turned1, own[1], wait)
        fed[1].down(wait)
        wait = [written["down"][0][1, :8, :128]]
        all_down_in[0] = with_pair(gathering[3], wait)
        fed[0] = Feed(0, all_normed2[0], all_down_in[0], 2, 2)
        wait = fed[0].again(wait)
        wait = fed[0].again(wait)
        out_moving = [send_sums(out_sums[h], wait) for h in range(2)]
        wait = fed[0].columns(wait, fed[1].blocks)
        wait = fed[0].columns_now(wait)
        outs = [last(out_mids[h], *out_moving[h], after=wait)[0] for h in range(2)]
        block_out = unshare(outs)
        turned0 = turn_quarters(own[0], wait + fed[0].blocks)
        fed[1].write(wait)
        packed0 = gather_quarters(turned0, own[0], wait)
        wait = fed[0].columns_held([turned0])
        fed[0].down(wait)

        norms = summed[-1][:, : 4 * width].reshape(layers, 4, shards, rows)
        biases = summed[-1][:, 4 * width :].reshape(layers, shards, 3 * rows)
        mine = jnp.concatenate(
            [
                lax.dynamic_index_in_dim(norms, me, axis=2, keepdims=False).reshape(layers, 4 * rows),
                lax.dynamic_index_in_dim(biases, me, axis=1, keepdims=False),
            ],
            axis=1,
        )
        mine = lax.all_gather(mine, "rep", axis=0, tiled=False)
        mine = (mine[0] + mine[1]) + (mine[2] + mine[3])
        fed[0].write()
        for layer, packed in ((1, packed1), (0, packed0)):
            write_blocks(layer, "qkv", packed, 3 * cols, 32, 0)
            write_blocks(layer, "out", packed, cols, quarter, 0, 3)

        def owned(k):
            return mine[:, k * rows : (k + 1) * rows]

        return (
            block_out,
            input_grad,
            owned(0),
            owned(1),
            written["qkv"][0],
            mine[:, 4 * rows :],
            written["out"][0],
            owned(2),
            owned(3),
            *written["feed"],
            written["down"][0],
        )

    return local


class Exchange:
    def __init__(self, mesh):
        self.shards = mesh.shape["shard"]
        self.reps = mesh.shape["rep"]
        self.cube = self.shards == 8
        self.line = self.reps == 4

    def swap(self, values, bit):
        pairs = [(i, i ^ bit) for i in range(self.shards)]
        return lax.ppermute(values, "shard", pairs)

    def gather(self, own):
        if not self.cube:
            return lax.all_gather(own, "shard", axis=0, tiled=False)
        first = self.swap(own, 1)
        x, y, d = self.swap(own, 2), self.swap(own, 4), self.swap(own, 6)
        others = self.swap(jnp.stack([x, y, d]), 1)
        return jnp.stack([own, first, x, others[0], y, others[1], d, others[2]])

    def scatter_sum(self, blocks):
        if not self.cube:
            return lax.psum_scatter(blocks.astype(bf16), "shard", scatter_dimension=0, tiled=False).astype(f32)
        low = blocks.astype(bf16)
        arrived = self.swap(jnp.stack([low[1], low[3], low[5], low[7]]), 1).astype(f32)
        x = self.swap((blocks[2] + arrived[1]).astype(bf16), 2)
        y = self.swap((blocks[4] + arrived[2]).astype(bf16), 4)
        d = self.swap((blocks[6] + arrived[3]).astype(bf16), 6)
        own = blocks[0] + arrived[0]
        return own + x.astype(f32) + (y.astype(f32) + d.astype(f32))

    def spread(self, blocks):
        return lax.all_to_all(blocks, "shard", split_axis=0, concat_axis=0, tiled=False)

    def total(self, grad, turn=None):
        turn = turn or (lambda v: v)
        if not self.line:
            full = lax.psum(grad.astype(bf16), "rep")
            return jnp.stack([turn(full[0]), turn(full[1])]).astype(f32)
        rep = lax.axis_index("rep")
        low = grad.astype(bf16)
        inward = lax.ppermute(low, "rep", [(0, 1), (3, 2)])
        part = (grad + inward.astype(f32)).astype(bf16)
        lower = rep < 2
        sent = jnp.where(lower, part[0], part[1])
        kept = jnp.where(lower, part[1], part[0])
        middle = lax.ppermute(sent, "rep", [(1, 2), (2, 1)])
        final = turn((kept.astype(f32) + middle.astype(f32)).astype(bf16))
        other = lax.ppermute(final, "rep", [(1, 2), (2, 1)])
        whole = jnp.where(lower, jnp.stack([other, final]), jnp.stack([final, other]))
        outward = lax.ppermute(whole, "rep", [(1, 0), (2, 3)])
        return jnp.where((rep == 1) | (rep == 2), whole, outward).astype(f32)


def make_general(mesh):
    net = Exchange(mesh)
    shards = net.shards

    def local(
        hidden_in,
        segments,
        ln1_gain,
        ln1_bias,
        qkv_weight,
        qkv_bias,
        out_weight,
        ln2_gain,
        ln2_bias,
        gate_weight,
        up_weight,
        down_weight,
        cotangent,
    ):
        layers, rows = qkv_weight.shape[:2]
        width = hidden_in.shape[2]
        tokens = hidden_in.shape[1]
        head_size = width // HEADS
        scale = head_size ** (-0.5)
        own_heads = HEADS // shards
        cols = own_heads * head_size
        hidden_units = down_weight.shape[1]
        everyone = shards * tokens
        me = lax.axis_index("shard")

        small = jnp.concatenate(
            [v.reshape(-1) for v in (ln1_gain, ln1_bias, ln2_gain, ln2_bias, qkv_bias)]
        )
        small = lax.all_gather(small, "shard", axis=0, tiled=False)
        cuts = [0]
        for v in (ln1_gain, ln1_bias, ln2_gain, ln2_bias, qkv_bias):
            cuts.append(cuts[-1] + v.size)

        def whole_of(index, like):
            part = small[:, cuts[index] : cuts[index + 1]].reshape(shards, layers, like.shape[1])
            return part.transpose(1, 0, 2).reshape(layers, -1).astype(f32)

        gain1, shift1 = whole_of(0, ln1_gain), whole_of(1, ln1_bias)
        gain2, shift2 = whole_of(2, ln2_gain), whole_of(3, ln2_bias)
        bias_all = whole_of(4, qkv_bias).reshape(layers, 3, shards, cols)
        bias_own = lax.dynamic_index_in_dim(bias_all, me, axis=2, keepdims=False)
        bias_own = bias_own.reshape(layers, 3 * cols)

        group_segments = net.gather(segments[0].astype(bf16)).astype(jnp.int32)
        positions, allowed = positions_and_mask(group_segments)
        cosine, sine = rotary_tables(positions)
        allowed = allowed[:, None]

        def columns_of(weight):
            cut = weight.reshape(rows, shards, -1).transpose(1, 0, 2)
            return net.spread(cut).reshape(width, -1)

        def qkv_columns(weight):
            cut = weight.reshape(rows, 3, shards, cols).transpose(2, 0, 1, 3)
            return net.spread(cut).reshape(width, 3 * cols)

        proj_in = [qkv_columns(qkv_weight[layer]) for layer in range(layers)]
        weight_gate = [columns_of(gate_weight[layer]) for layer in range(layers)]
        weight_up = [columns_of(up_weight[layer]) for layer in range(layers)]

        def gather(values):
            return net.gather(values).reshape(everyone, -1)

        def scatter_sum(values):
            return net.scatter_sum(values.reshape(shards, tokens, -1))

        state = hidden_in[0].astype(f32)
        saved = []
        for layer in range(layers):
            xhat1, inverse1 = normalize(state)
            normed1 = gather((xhat1 * gain1[layer] + shift1[layer]).astype(bf16))
            joined = dot(normed1, proj_in[layer]) + bias_own[layer]
            split = joined.reshape(shards, tokens, 3, own_heads, head_size)
            query = rotate(split[:, :, 0], cosine, sine).astype(bf16)
            keys = rotate(split[:, :, 1], cosine, sine).astype(bf16)
            value = split[:, :, 2].astype(bf16)
            scores = (
                jnp.einsum("gqhd,gkhd->ghqk", query, keys, preferred_element_type=f32) * scale
            )
            masked = jnp.where(allowed, scores, -1000000000.0)
            peak = jnp.max(masked, axis=-1, keepdims=True)
            raised = jnp.exp(masked - peak)
            probs = raised / jnp.sum(raised, axis=-1, keepdims=True)
            probs_low = probs.astype(bf16)
            mixed = (
                jnp.einsum("ghqk,gkhd->gqhd", probs_low, value, preferred_element_type=f32)
                .astype(bf16)
                .reshape(everyone, cols)
            )
            state_mid = state + scatter_sum(dot(mixed, out_weight[layer]))
            xhat2, inverse2 = normalize(state_mid)
            normed2 = gather((xhat2 * gain2[layer] + shift2[layer]).astype(bf16))
            gate = dot(normed2, weight_gate[layer])
            upper = dot(normed2, weight_up[layer])
            inner = (jax.nn.silu(gate) * upper).astype(bf16)
            state = state_mid + scatter_sum(dot(inner, down_weight[layer]))
            saved.append(
                (xhat1, inverse1, normed1, query, keys, value, probs, mixed)
                + (xhat2, inverse2, normed2, gate, upper, inner)
            )
        block_out = state.astype(bf16)[None]

        def from_columns(grad):
            return grad.reshape(shards, 2, rows // 2, -1).transpose(1, 0, 2, 3)

        def turn_columns(half):
            return net.spread(half).transpose(1, 0, 2).reshape(rows // 2, -1)

        def turn_qkv(half):
            whole = net.spread(half).reshape(shards, rows // 2, 3, cols)
            return whole.transpose(1, 2, 0, 3).reshape(rows // 2, -1)

        def halves(grad):
            return grad.reshape(2, grad.shape[0] // 2, -1)

        grad_state = cotangent[0].astype(f32)
        weight_grads = [None] * layers
        small_grads = [None] * layers
        for layer in reversed(range(layers)):
            xhat1, inverse1, normed1, query, keys, value, probs, mixed = saved[layer][:8]
            xhat2, inverse2, normed2, gate, upper, inner = saved[layer][8:]
            down_in = gather(grad_state.astype(bf16))
            grad_inner = dot_t(down_in, down_weight[layer])
            sigmoid = jax.nn.sigmoid(gate)
            silu = gate * sigmoid
            grad_gate = (grad_inner * upper * (sigmoid * (1.0 + gate * (1.0 - sigmoid)))).astype(bf16)
            grad_up = (grad_inner * silu).astype(bf16)
            grad_normed2 = scatter_sum(
                dot_t(grad_gate, weight_gate[layer]) + dot_t(grad_up, weight_up[layer])
            )
            grad_down_weight = net.total(halves(t_dot(inner, down_in)))
            grad_gate_weight = net.total(from_columns(t_dot(normed2, grad_gate)), turn_columns)
            grad_up_weight = net.total(from_columns(t_dot(normed2, grad_up)), turn_columns)
            back2, gain2_grad, shift2_grad = normalize_back(
                grad_normed2, xhat2, inverse2, gain2[layer]
            )
            grad_state = grad_state + back2

            branch = gather(grad_state.astype(bf16))
            grad_mixed = dot_t(branch, out_weight[layer]).astype(bf16)
            grad_out_weight = net.total(halves(t_dot(mixed, branch)))
            grad_mixed = grad_mixed.reshape(shards, tokens, own_heads, head_size)
            grad_probs = jnp.einsum(
                "gqhd,gkhd->ghqk", grad_mixed, value, preferred_element_type=f32
            )
            grad_value = jnp.einsum(
                "ghqk,gqhd->gkhd", probs.astype(bf16), grad_mixed, preferred_element_type=f32
            )
            inner_sum = jnp.sum(probs * grad_probs, axis=-1, keepdims=True)
            grad_scores = (probs * (grad_probs - inner_sum)).astype(bf16)
            grad_query = (
                jnp.einsum("ghqk,gkhd->gqhd", grad_scores, keys, preferred_element_type=f32) * scale
            )
            grad_key = (
                jnp.einsum("ghqk,gqhd->gkhd", grad_scores, query, preferred_element_type=f32)
                * scale
            )
            grad_query = rotate(grad_query, cosine, -sine)
            grad_key = rotate(grad_key, cosine, -sine)
            grad_joined = jnp.stack([grad_query, grad_key, grad_value], axis=2)
            bias_grad = jnp.sum(grad_joined.astype(bf16).astype(f32), axis=(0, 1))
            grad_joined = grad_joined.reshape(everyone, 3 * cols).astype(bf16)
            grad_normed1 = scatter_sum(dot_t(grad_joined, proj_in[layer]))
            grad_qkv_weight = net.total(from_columns(t_dot(normed1, grad_joined)), turn_qkv)
            back1, gain1_grad, shift1_grad = normalize_back(
                grad_normed1, xhat1, inverse1, gain1[layer]
            )
            grad_state = grad_state + back1
            weight_grads[layer] = (
                grad_qkv_weight.reshape(rows, -1),
                grad_out_weight.reshape(rows, -1),
                grad_gate_weight.reshape(rows, -1),
                grad_up_weight.reshape(rows, -1),
                grad_down_weight.reshape(hidden_units, -1),
            )
            placed = jnp.where(
                (jnp.arange(shards) == me)[None, :, None], bias_grad.reshape(3, 1, cols), 0.0
            )
            small_grads[layer] = jnp.concatenate(
                [gain1_grad, shift1_grad, gain2_grad, shift2_grad, placed.reshape(-1)]
            )

        summed = lax.psum(jnp.stack(small_grads), ("shard", "rep"))

        def owned(begin, count):
            part = summed[:, begin : begin + count].reshape(layers, shards, count // shards)
            return lax.dynamic_index_in_dim(part, me, axis=1, keepdims=False)

        stacked = [
            jnp.stack([weight_grads[layer][index] for layer in range(layers)]) for index in range(5)
        ]
        return (
            block_out,
            grad_state.astype(bf16)[None],
            owned(0, width),
            owned(width, width),
            stacked[0],
            owned(4 * width, 3 * width),
            stacked[1],
            owned(2 * width, width),
            owned(3 * width, width),
            stacked[2],
            stacked[3],
            stacked[4],
        )

    return local


def solution(mesh):
    tokens3 = P(("shard", "rep"), None, None)
    vector = P(None, "shard")
    matrix = P(None, "shard", None)
    in_specs = (
        tokens3,
        P(("shard", "rep"), None),
        vector,
        vector,
        matrix,
        vector,
        matrix,
        vector,
        vector,
        matrix,
        matrix,
        matrix,
        tokens3,
    )
    out_specs = (
        tokens3,
        tokens3,
        vector,
        vector,
        matrix,
        vector,
        matrix,
        vector,
        vector,
        matrix,
        matrix,
        matrix,
    )
    cube = mesh.shape["shard"] == 8 and mesh.shape["rep"] == 4
    local = make_cube(mesh) if cube else make_general(mesh)
    return jax.shard_map(
        local, mesh=mesh, in_specs=in_specs, out_specs=out_specs, check_vma=False
    )
```

```python
import functools

import jax
import jax.numpy as jnp
from jax import lax
from jax.experimental import pallas as pl
from jax.experimental.pallas import tpu as pltpu
from jax.sharding import PartitionSpec as P

HEADS = 32
ROTARY = 16
HALF = ROTARY // 2

norm_eps = 1e-05
bf16 = jnp.bfloat16
f32 = jnp.float32


def dot(a, b):
    return jnp.dot(a, b, preferred_element_type=f32)


def dot_t(a, b):
    return lax.dot_general(a, b, (((1,), (1,)), ((), ())), preferred_element_type=f32)


def t_dot(a, b):
    return lax.dot_general(a, b, (((0,), (0,)), ((), ())), preferred_element_type=f32)


def normalize(values):
    centred = values - jnp.mean(values, axis=-1, keepdims=True)
    variance = jnp.mean(centred * centred, axis=-1, keepdims=True)
    inverse = lax.rsqrt(variance + norm_eps)
    return centred * inverse, inverse


def normalize_back(grad, xhat, inverse, gain):
    scaled = grad * gain
    inner = jnp.mean(scaled * xhat, axis=-1, keepdims=True)
    grad_in = inverse * (scaled - jnp.mean(scaled, axis=-1, keepdims=True) - xhat * inner)
    return grad_in, jnp.sum(grad * xhat, axis=0), jnp.sum(grad, axis=0)


def positions_and_mask(segments):
    length = segments.shape[-1]
    earlier = (segments[..., None, :] < segments[..., :, None]).astype(jnp.int32)
    starts = jnp.sum(earlier, axis=-1)
    places = jnp.arange(length, dtype=jnp.int32)
    positions = places - starts
    allowed = (segments[..., None, :] == segments[..., :, None]) & (
        places[None, :] <= places[:, None]
    )
    return positions, allowed


def rotary_tables(positions):
    exponents = jnp.arange(HALF, dtype=f32) * (2.0 / ROTARY)
    inverse = 10000.0 ** (-exponents)
    angles = positions.astype(f32)[..., None] * inverse
    return jnp.cos(angles)[..., None, :], jnp.sin(angles)[..., None, :]


def rotate(heads_in, cosine, sine):
    leading = heads_in[..., :HALF]
    trailing = heads_in[..., HALF:ROTARY]
    return jnp.concatenate(
        [
            leading * cosine - trailing * sine,
            trailing * cosine + leading * sine,
            heads_in[..., ROTARY:],
        ],
        axis=-1,
    )


def corner(values):
    if values.size < 1 << 20:
        return values
    short = values.reshape(-1, values.shape[-1])
    return lax.slice(short, (0, 0), (8, 128))


microsecond = 1_150_000_000


def call(kernel, grid, in_specs, out_specs, out_shape, vmem=48, aliases=None, weight=1000):
    reads = len(in_specs)

    def run(*operands, after=(), pieces=True):
        after = [corner(v) for v in after] if pieces else list(after)

        def body(*refs):
            kernel(*refs[:reads], *refs[reads + len(after) :])

        specs = list(in_specs) + [pl.BlockSpec(memory_space=pl.ANY)] * len(after)
        return pl.pallas_call(
            body,
            grid=grid or (),
            in_specs=specs,
            out_specs=out_specs,
            out_shape=out_shape,
            input_output_aliases=aliases or {},
            compiler_params=pltpu.CompilerParams(vmem_limit_bytes=vmem << 20),
            cost_estimate=pl.CostEstimate(flops=weight, bytes_accessed=1000, transcendentals=0),
        )(*operands, *after)

    return run


def hold(values, after):
    anywhere = pl.BlockSpec(memory_space=pl.ANY)
    shape = jax.ShapeDtypeStruct(values.shape, values.dtype)
    run = call(lambda *_: None, None, [anywhere], anywhere, shape, 62, aliases={0: 0})
    return run(values, after=after, pieces=False)


def whole(shape, layer=None):
    at = (layer or 0,) + (0,) * (len(shape) - 1)
    return pl.BlockSpec(shape, lambda *_: at, pipeline_mode=pl.Buffered(1))


def shape_of(shape, dtype):
    return jax.ShapeDtypeStruct(shape, dtype)


def head_lanes(values, head, head_size):
    lanes = lax.broadcasted_iota(jnp.int32, values.shape, 1)
    inside = (lanes >= head * head_size) & (lanes < (head + 1) * head_size)
    return jnp.where(inside, values, jnp.zeros_like(values))


def widen(ref, cols):
    values = ref[...]
    return jnp.concatenate([values] * (cols // values.shape[1]), axis=1)


def stack_heads(values, heads, head_size):
    return jnp.concatenate([head_lanes(values, h, head_size) for h in range(heads)], axis=0)


def own_lanes(blocks, heads, head_size):
    tokens = blocks.shape[0] // heads
    total = None
    for h in range(heads):
        term = head_lanes(blocks[h * tokens : (h + 1) * tokens], h, head_size)
        total = term if total is None else total + term
    return total


def attention(q_heads, keys, mask, heads, head_size):
    allowed = jnp.concatenate([mask] * heads, axis=0) > 0.5
    scores = dot_t(q_heads, keys) * head_size ** (-0.5)
    masked = jnp.where(allowed, scores, -1000000000.0)
    raised = jnp.exp(masked - jnp.max(masked, axis=-1, keepdims=True))
    return raised / jnp.sum(raised, axis=-1, keepdims=True)


def join_rows(own_ref, pair_ref):
    pieces = []
    for s in range(own_ref.shape[0]):
        pieces += [own_ref[s], pair_ref[s]]
    return jnp.concatenate(pieces, axis=0)


def part_rows(values, keep_ref, send_ref):
    count, half, _ = keep_ref.shape
    for s in range(count):
        first = 2 * s * half
        keep_ref[s] = values[first : first + half]
        send_ref[s] = values[first + half : first + 2 * half].astype(bf16)


def attend_kernel(
    own_ref, pair_ref, w_ref, bias_ref, cos_ref, low_ref, high_ref, mask_ref, out_w_ref,
    keep_ref, send_ref, normed_ref, q_ref, k_ref, v_ref, mixed_ref,
    *, heads, head_size,
):
    cols = heads * head_size
    normed = join_rows(own_ref, pair_ref)
    normed_ref[...] = normed
    joined = dot(normed, w_ref[...]) + bias_ref[...]
    cosine, low, high = (widen(ref, cols) for ref in (cos_ref, low_ref, high_ref))

    def turn(v):
        return v * cosine + pltpu.roll(v, cols - HALF, 1) * low + pltpu.roll(v, HALF, 1) * high

    q = turn(joined[:, :cols]).astype(bf16)
    k = turn(joined[:, cols : 2 * cols]).astype(bf16)
    v = joined[:, 2 * cols :].astype(bf16)
    q_ref[...] = q
    k_ref[...] = k
    v_ref[...] = v
    tokens = mask_ref.shape[1]
    mixed = []
    for s in range(mask_ref.shape[0]):
        at = slice(s * tokens, (s + 1) * tokens)
        probs = attention(stack_heads(q[at], heads, head_size), k[at], mask_ref[s], heads, head_size)
        terms = dot(probs.astype(bf16), v[at])
        mixed.append(own_lanes(terms, heads, head_size).astype(bf16))
    mixed = jnp.concatenate(mixed, axis=0)
    mixed_ref[...] = mixed
    part_rows(dot(mixed, out_w_ref[0]), keep_ref, send_ref)


def attend_back_kernel(
    own_ref, pair_ref, w_ref, cos_ref, low_ref, high_ref, mask_ref, out_w_ref, q_ref, k_ref, v_ref,
    keep_ref, send_ref, branch_ref, joined_ref, bias_ref,
    *, heads, head_size,
):
    cols = heads * head_size
    scale = head_size ** (-0.5)
    branch = join_rows(own_ref, pair_ref)
    branch_ref[...] = branch
    grad_mixed = dot_t(branch, out_w_ref[0]).astype(bf16)
    cosine, low, high = (widen(ref, cols) for ref in (cos_ref, low_ref, high_ref))

    def turn_back(v):
        return v * cosine - pltpu.roll(v, cols - HALF, 1) * low - pltpu.roll(v, HALF, 1) * high

    q, k, v = q_ref[...], k_ref[...], v_ref[...]
    tokens = mask_ref.shape[1]
    grad_q, grad_k, grad_v = [], [], []
    for s in range(mask_ref.shape[0]):
        at = slice(s * tokens, (s + 1) * tokens)
        q_heads = stack_heads(q[at], heads, head_size)
        g_heads = stack_heads(grad_mixed[at], heads, head_size)
        probs = attention(q_heads, k[at], mask_ref[s], heads, head_size)
        grad_probs = dot_t(g_heads, v[at])
        inner = jnp.sum(probs * grad_probs, axis=-1, keepdims=True)
        grad_scores = (probs * (grad_probs - inner)).astype(bf16)
        sums = (
            own_lanes(dot(grad_scores, k[at]), heads, head_size),
            t_dot(grad_scores, q_heads),
            t_dot(probs.astype(bf16), g_heads),
        )
        grad_q.append(sums[0] * scale)
        grad_k.append(sums[1] * scale)
        grad_v.append(sums[2])
    joined = jnp.concatenate(
        [
            turn_back(jnp.concatenate(grad_q, axis=0)),
            turn_back(jnp.concatenate(grad_k, axis=0)),
            jnp.concatenate(grad_v, axis=0),
        ],
        axis=1,
    ).astype(bf16)
    joined_ref[...] = joined

    @pl.when(pl.program_id(0) == 0)
    def _():
        bias_ref[...] = jnp.zeros_like(bias_ref)

    bias_ref[...] += jnp.sum(joined.astype(f32), axis=0, keepdims=True)
    part_rows(dot_t(joined, w_ref[...]), keep_ref, send_ref)


def feed_kernel(own_ref, pair_ref, w_ref, down_ref, keep_ref, send_ref, both_ref):
    both = dot(join_rows(own_ref, pair_ref), w_ref[...])
    both_ref[...] = both
    hidden = both.shape[1] // 2
    gate, upper = both[:, :hidden], both[:, hidden:]
    inner = (gate / (1.0 + jnp.exp(-gate)) * upper).astype(bf16)
    part_rows(dot(inner, down_ref[0]), keep_ref, send_ref)


def feed_back_kernel(own_ref, pair_ref, w_ref, down_ref, both_ref, keep_ref, send_ref):
    grad_inner = dot_t(join_rows(own_ref, pair_ref), down_ref[0])
    hidden = grad_inner.shape[1]
    gate, upper = both_ref[:, :hidden], both_ref[:, hidden:]
    sigmoid = 1.0 / (1.0 + jnp.exp(-gate))
    slope = sigmoid * (1.0 + gate * (1.0 - sigmoid))
    grad_gate = (grad_inner * upper * slope).astype(bf16)
    grad_upper = (grad_inner * (gate * sigmoid)).astype(bf16)
    grad_both = jnp.concatenate([grad_gate, grad_upper], axis=1)
    part_rows(dot_t(grad_both, w_ref[...]), keep_ref, send_ref)


def feed_again_kernel(normed_ref, down_in_ref, w_ref, down_ref, *refs):
    grad_both_ref, inner_ref, token_ref = refs[-3:]
    token_ref[...] = jnp.zeros_like(token_ref)
    both = dot(normed_ref[...], w_ref[...])
    grad_inner = dot_t(down_in_ref[...], down_ref[0])
    hidden = grad_inner.shape[1]
    gate, upper = both[:, :hidden], both[:, hidden:]
    sigmoid = 1.0 / (1.0 + jnp.exp(-gate))
    silu = gate * sigmoid
    inner_ref[...] = (silu * upper).astype(bf16)
    slope = sigmoid * (1.0 + gate * (1.0 - sigmoid))
    grad_both_ref[:, :hidden] = (grad_inner * upper * slope).astype(bf16)
    grad_both_ref[:, hidden:] = (grad_inner * silu).astype(bf16)


def all_rows_kernel(first_ref, second_ref, right_ref, out_ref):
    count = first_ref.shape[0]
    total = t_dot(first_ref[...], right_ref[:count]) + t_dot(second_ref[...], right_ref[count:])
    out_ref[0] = total.astype(bf16)


def all_down_kernel(left_ref, first_ref, second_ref, *refs):
    count = first_ref.shape[0]
    refs[-1][0] = t_dot(left_ref[:count], first_ref[...]) + t_dot(left_ref[count:], second_ref[...])


def weight_quarters_kernel(first_ref, second_ref, first_grad_ref, second_grad_ref, *refs):
    out_ref = refs[-1]
    product = t_dot(first_ref[...], first_grad_ref[...]) + t_dot(second_ref[...], second_grad_ref[...])
    product = product.astype(bf16)
    quarter = product.shape[0] // out_ref.shape[0]
    for k in range(out_ref.shape[0]):
        out_ref[k, 0] = product[k * quarter : (k + 1) * quarter]


def write_blocks_kernel(blocks_ref, *refs, place, outputs):
    place(blocks_ref, *refs[len(refs) - outputs :])


def combine_kernel(keep_ref, arrived_ref, own_ref, x_ref, y_ref, d_ref):
    own_ref[...] = keep_ref[0] + arrived_ref[0].astype(f32)
    for k, ref in ((1, x_ref), (2, y_ref), (3, d_ref)):
        ref[...] = (keep_ref[k] + arrived_ref[k].astype(f32)).astype(bf16)


def received(own_ref, x_ref, y_ref, d_ref):
    return own_ref[...] + x_ref[...].astype(f32) + (y_ref[...].astype(f32) + d_ref[...].astype(f32))


def norm_first_kernel(state_ref, gain_ref, shift_ref, normed_ref):
    xhat, _ = normalize(state_ref[...])
    normed_ref[...] = (xhat * gain_ref[...] + shift_ref[...]).astype(bf16)


def norm_kernel(state_ref, own_ref, x_ref, y_ref, d_ref, gain_ref, shift_ref, new_ref, normed_ref):
    state = state_ref[...] + received(own_ref, x_ref, y_ref, d_ref)
    new_ref[...] = state
    xhat, _ = normalize(state)
    normed_ref[...] = (xhat * gain_ref[...] + shift_ref[...]).astype(bf16)


def last_kernel(state_ref, own_ref, x_ref, y_ref, d_ref, out_ref):
    out_ref[...] = (state_ref[...] + received(own_ref, x_ref, y_ref, d_ref)).astype(bf16)


def norm_back_kernel(
    grad_ref, own_ref, x_ref, y_ref, d_ref, state_ref, gain_ref, new_ref, low_ref, sums_ref
):
    grad_normed = received(own_ref, x_ref, y_ref, d_ref)
    xhat, inverse = normalize(state_ref[...])
    scaled = grad_normed * gain_ref[...]
    inner = jnp.mean(scaled * xhat, axis=-1, keepdims=True)
    back = inverse * (scaled - jnp.mean(scaled, axis=-1, keepdims=True) - xhat * inner)
    grad = grad_ref[...] + back
    new_ref[...] = grad
    low_ref[...] = grad.astype(bf16)
    sums_ref[0:1] = jnp.sum(grad_normed * xhat, axis=0, keepdims=True)
    sums_ref[1:2] = jnp.sum(grad_normed, axis=0, keepdims=True)


def cut_qkv_kernel(weight_ref, out_ref):
    shards, _, n = out_ref.shape
    cols = n // 3
    for s in range(shards):
        for t in range(3):
            first = (t * shards + s) * cols
            out_ref[s, :, t * cols : (t + 1) * cols] = weight_ref[0, :, first : first + cols]


def cut_feed_kernel(gate_ref, up_ref, out_ref):
    shards, _, n = out_ref.shape
    n = n // 2
    for s in range(shards):
        out_ref[s, :, :n] = gate_ref[0, :, s * n : (s + 1) * n]
        out_ref[s, :, n:] = up_ref[0, :, s * n : (s + 1) * n]


def stack_kernel(a_ref, b_ref, c_ref, d_ref, out_ref):
    for k, ref in enumerate((a_ref, b_ref, c_ref, d_ref)):
        out_ref[k] = ref[...]


def join_kernel(first_ref, second_ref, out_ref):
    out_ref[0] = first_ref[...]
    out_ref[1] = second_ref[...]


def unpack_kernel(packed_ref, out_ref):
    out_ref[...] = packed_ref[:, :, : out_ref.shape[2]]


def pack_kernel(first_ref, packed_ref, out_ref):
    n = first_ref.shape[2]
    out_ref[:, :, :n] = first_ref[...]
    out_ref[:, :, n:] = packed_ref[:, :, n:]


def place_blocks(ref, out_ref):
    n = ref.shape[2]
    for s in range(ref.shape[0]):
        out_ref[0, :, s * n : (s + 1) * n] = ref[s].astype(f32)


def place_feed(ref, gate_ref, up_ref):
    shards, _, n = ref.shape
    n = n // 2
    for s in range(shards):
        gate_ref[0, :, s * n : (s + 1) * n] = ref[s, :, :n].astype(f32)
        up_ref[0, :, s * n : (s + 1) * n] = ref[s, :, n:].astype(f32)


def place_qkv(ref, out_ref):
    shards, _, n = ref.shape
    cols = n // 3
    for s in range(shards):
        for t in range(3):
            first = (t * shards + s) * cols
            out_ref[0, :, first : first + cols] = ref[s, :, t * cols : (t + 1) * cols].astype(f32)


def make_cube(mesh):
    shards, reps = 8, 4

    def swap(values, bit):
        return lax.ppermute(values, "shard", [(i, i ^ bit) for i in range(shards)])

    def local(
        hidden_in,
        segments,
        ln1_gain,
        ln1_bias,
        qkv_weight,
        qkv_bias,
        out_weight,
        ln2_gain,
        ln2_bias,
        gate_weight,
        up_weight,
        down_weight,
        cotangent,
    ):
        layers, rows = qkv_weight.shape[:2]
        width = hidden_in.shape[2]
        tokens = hidden_in.shape[1]
        part = tokens // 2
        head_size = width // HEADS
        heads = HEADS // shards
        cols = heads * head_size
        hidden = down_weight.shape[1]
        chips = shards // 2
        many = chips * tokens
        step = 2 * tokens
        me = lax.axis_index("shard")
        core = me % 2

        smalls = (ln1_gain, ln1_bias, ln2_gain, ln2_bias, qkv_bias, segments.astype(bf16))
        small = lax.all_gather(
            jnp.concatenate([v.reshape(-1) for v in smalls]), "shard", axis=0, tiled=False
        )
        cuts = [0]
        for v in smalls:
            cuts.append(cuts[-1] + v.size)

        def whole_of(index):
            like = smalls[index]
            cut = small[:, cuts[index] : cuts[index + 1]].reshape(shards, layers, like.shape[1])
            return cut.transpose(1, 0, 2).reshape(layers, -1).astype(f32)

        gain1, shift1, gain2, shift2 = (whole_of(i) for i in range(4))
        bias_all = whole_of(4).reshape(layers, 3, shards, cols)
        bias_own = lax.dynamic_index_in_dim(bias_all, me, axis=2, keepdims=False)
        bias_own = bias_own.reshape(layers, 1, 3 * cols)
        all_segments = small[:, cuts[5] : cuts[6]]

        places = jnp.arange(tokens, dtype=jnp.int32)
        places = jnp.where(core == 0, places, (places + part) % tokens)
        exponents = jnp.arange(HALF, dtype=f32) * (2.0 / ROTARY)
        inverse = 10000.0 ** (-exponents)
        masks, tables = [], []
        for h in range(2):
            wanted = (me // 2 ^ jnp.arange(chips)) * 2 + h
            picked = (wanted[:, None] == jnp.arange(shards)[None]).astype(bf16)
            numbers = dot(picked, all_segments)
            numbers = jnp.where(core == 0, numbers, jnp.roll(numbers, part, axis=1))
            earlier = numbers[:, None, :] < numbers[:, :, None]
            positions = places - jnp.sum(earlier.astype(jnp.int32), axis=-1)
            allowed = (numbers[:, None, :] == numbers[:, :, None]) & (
                places[None, :] <= places[:, None]
            )
            masks.append(allowed.astype(f32))
            angles = positions.astype(f32).reshape(many, 1) * inverse
            cosine, sine = jnp.cos(angles), jnp.sin(angles)
            zero8 = jnp.zeros_like(sine)
            rest = jnp.zeros((many, head_size - ROTARY), f32)
            tables.append(
                [
                    jnp.tile(jnp.concatenate(pieces, axis=1), (1, heads // 2))
                    for pieces in (
                        (cosine, cosine, rest + 1.0),
                        (-sine, zero8, rest),
                        (zero8, sine, rest),
                    )
                ]
            )

        def spread(blocks):
            return lax.all_to_all(blocks, "shard", split_axis=0, concat_axis=0, tiled=False)

        def cut_columns(kernel, arrays, layer, n, after):
            cut_rows = rows // 4
            block = pl.BlockSpec((1, cut_rows, arrays[0].shape[2]), lambda i: (layer, i, 0))
            return call(
                kernel,
                (4,),
                [block] * len(arrays),
                pl.BlockSpec((shards, cut_rows, n), lambda i: (0, i, 0)),
                shape_of((shards, rows, n), bf16),
                24,
            )(*arrays, after=after)

        def cut_qkv(layer, after):
            return cut_columns(cut_qkv_kernel, [qkv_weight], layer, 3 * cols, after)

        def cut_feed(layer, after):
            return cut_columns(cut_feed_kernel, [gate_weight, up_weight], layer, 2 * hidden, after)

        def turned(blocks):
            return spread(blocks).reshape(width, blocks.shape[2])

        stack = call(
            stack_kernel,
            None,
            [pl.BlockSpec(memory_space=pltpu.VMEM)] * 4,
            pl.BlockSpec(memory_space=pltpu.VMEM),
            shape_of((chips, part, width), bf16),
            16,
        )
        combine = call(
            combine_kernel,
            None,
            [pl.BlockSpec(memory_space=pltpu.VMEM)] * 2,
            [pl.BlockSpec(memory_space=pltpu.VMEM)] * 4,
            [shape_of((part, width), f32)] + [shape_of((part, width), bf16)] * 3,
            16,
        )

        steps = chips // 2
        piece = pl.BlockSpec((2, part, width), lambda i: (i, 0, 0))

        def row_block(n):
            return pl.BlockSpec((step, n), lambda i: (i, 0))

        mask_block = pl.BlockSpec((2, tokens, tokens), lambda i: (i, 0, 0))
        table_blocks = [row_block(cols // 2)] * 3
        part_shapes = [
            shape_of((chips, part, width), f32),
            shape_of((chips, part, width), bf16),
        ]
        options = dict(heads=heads, head_size=head_size)
        def attend(layer, *operands, after=()):
            return call(
                functools.partial(attend_kernel, **options),
                (steps,),
                [piece, piece, whole((width, 3 * cols)), whole((1, 3 * cols))]
                + table_blocks
                + [mask_block, whole((1, cols, width), layer)],
                [piece, piece, row_block(width)] + [row_block(cols)] * 4,
                part_shapes + [shape_of((many, width), bf16)] + [shape_of((many, cols), bf16)] * 4,
                weight=12 * microsecond,
            )(*operands, after=after)

        def attend_back(layer, *operands, after=()):
            bias_block = pl.BlockSpec((1, 3 * cols), lambda i: (0, 0))
            bias_shape = shape_of((1, 3 * cols), f32)
            return call(
                functools.partial(attend_back_kernel, **options),
                (steps,),
                [piece, piece, whole((width, 3 * cols))]
                + table_blocks
                + [mask_block, whole((1, cols, width), layer)]
                + [row_block(cols)] * 3,
                [piece, piece, row_block(width), row_block(3 * cols), bias_block],
                part_shapes
                + [shape_of((many, width), bf16), shape_of((many, 3 * cols), bf16), bias_shape],
                weight=12 * microsecond,
            )(*operands, after=after)

        def feed_weights(layer):
            return [whole((width, 2 * hidden)), whole((1, hidden, width), layer)]

        def feed(layer, *operands, after=()):
            return call(
                feed_kernel,
                (steps,),
                [piece, piece] + feed_weights(layer),
                [piece, piece, row_block(2 * hidden)],
                part_shapes + [shape_of((many, 2 * hidden), f32)],
                weight=12 * microsecond,
            )(*operands, after=after)

        def feed_back(layer, *operands, after=()):
            return call(
                feed_back_kernel,
                (steps,),
                [piece, piece] + feed_weights(layer) + [row_block(2 * hidden)],
                [piece, piece],
                part_shapes,
                weight=12 * microsecond,
            )(*operands, after=after)

        def small_call(kernel, n_in, out_shape):
            vmem = pl.BlockSpec(memory_space=pltpu.VMEM)
            return call(kernel, None, [vmem] * n_in, [vmem] * len(out_shape), out_shape, 16)

        low_shape, state_shape = shape_of((part, width), bf16), shape_of((part, width), f32)
        norm_first = small_call(norm_first_kernel, 3, [low_shape])
        norm = small_call(norm_kernel, 7, [state_shape, low_shape])
        last = small_call(last_kernel, 5, [low_shape])
        norm_back = small_call(norm_back_kernel, 7, [state_shape, low_shape, shape_of((2, width), f32)])

        written = {}
        shapes_of = dict(
            qkv=[qkv_weight.shape],
            feed=[gate_weight.shape, up_weight.shape],
            out=[out_weight.shape],
            down=[down_weight.shape],
        )
        places_of = dict(qkv=place_qkv, feed=place_feed, out=place_blocks)

        def write_blocks(layer, name, blocks, n, cut, first, at=0, after=()):
            parts, a, r, _ = blocks.shape
            shapes = shapes_of[name]
            earlier = written.get(name, [])
            each = r // cut
            begin = first // cut
            written[name] = call(
                functools.partial(write_blocks_kernel, place=places_of[name], outputs=len(shapes)),
                (parts, each),
                [pl.BlockSpec((None, a, cut, n), lambda i, j: (i, 0, j, at))]
                + [pl.BlockSpec(memory_space=pl.ANY)] * len(earlier),
                [pl.BlockSpec((1, cut, v[2]), lambda i, j: (layer, begin + i * each + j, 0)) for v in shapes],
                [shape_of(v, f32) for v in shapes],
                32,
                aliases={1 + k: k for k in range(len(earlier))},
            )(blocks, *earlier, after=after)

        quarter = rows // reps
        packed_shape = shape_of((reps, shards, quarter, 4 * cols), bf16)

        def weight_quarters(normed, joined, mixed, branch, after=()):
            left = pl.BlockSpec((many, rows), lambda s: (0, s))
            packed = call(
                weight_quarters_kernel,
                (shards,),
                [left, left, whole((many, 3 * cols)), whole((many, 3 * cols))],
                pl.BlockSpec((reps, 1, quarter, 3 * cols), lambda s: (0, s, 0, 0)),
                packed_shape,
                32,
            )(*normed, *joined, after=after)
            right = pl.BlockSpec((many, cols), lambda s: (0, s))
            return call(
                weight_quarters_kernel,
                (shards,),
                [whole((many, cols)), whole((many, cols)), right, right, pl.BlockSpec(memory_space=pl.ANY)],
                pl.BlockSpec((reps, 1, quarter, cols), lambda s: (0, s, 0, 3)),
                packed_shape,
                32,
                aliases={4: 0},
            )(*mixed, *branch, packed)

        def scatter_quarters(packed):
            return lax.psum_scatter(packed, "rep", scatter_dimension=0, tiled=False)

        def turn_quarters(own, after):
            vmem = pl.BlockSpec(memory_space=pltpu.VMEM)
            shape = shape_of((shards, quarter, 3 * cols), bf16)
            return spread(call(unpack_kernel, None, [vmem], vmem, shape, 16)(own, after=after))

        def gather_quarters(columns, own, after):
            vmem = pl.BlockSpec(memory_space=pltpu.VMEM)
            full = shape_of((shards, quarter, 4 * cols), bf16)
            own = call(pack_kernel, None, [vmem] * 2, vmem, full, 16)(columns, own, after=after)
            return lax.all_gather(own, "rep", axis=0, tiled=False)

        all_tokens = shards * reps * tokens
        half_tokens = all_tokens // 2

        def gather_all(halves, after=()):
            joined = call(
                join_kernel,
                None,
                [pl.BlockSpec(memory_space=pltpu.VMEM)] * 2,
                pl.BlockSpec(memory_space=pltpu.VMEM),
                shape_of((2, chips, part, width), bf16),
                24,
            )(*halves, after=after)
            return lax.all_gather(joined, "rep", axis=0, tiled=False).reshape(half_tokens, width)

        def with_pair(own, after):
            own = hold(own, after)
            return own, swap(own, 1)

        def feed_again(layer, normed, down_in, piece_at, count, earlier, after=()):
            block_rows = 2 * tokens
            side, piece = divmod(piece_at, count // 2)
            steps_in = all_tokens // count // block_rows
            source = pl.BlockSpec((block_rows, width), lambda i: (piece * steps_in + i, 0))

            def rows_of(n):
                return pl.BlockSpec((block_rows, n), lambda i: (piece_at * steps_in + i, 0))

            return call(
                feed_again_kernel,
                (steps_in,),
                [source, source]
                + feed_weights(layer)
                + [pl.BlockSpec(memory_space=pl.ANY)] * len(earlier),
                [rows_of(2 * hidden), rows_of(hidden), pl.BlockSpec((8, 128), lambda i: (0, 0))],
                [
                    shape_of((all_tokens, 2 * hidden), bf16),
                    shape_of((all_tokens, hidden), bf16),
                    shape_of((8, 128), f32),
                ],
                aliases={4 + k: k for k in range(len(earlier))},
                weight=20 * microsecond,
            )(normed[side], down_in[side], feed_in[layer], down_weight, *earlier, after=after)

        def all_columns(normed, grad_both, piece_at, count, after=()):
            n = grad_both.shape[1]
            r = rows // count
            left = pl.BlockSpec((half_tokens, r), lambda s: (0, s * count + piece_at))
            return call(
                all_rows_kernel,
                (shards,),
                [left, left, whole((all_tokens, n))],
                pl.BlockSpec((1, r, n), lambda s: (s, 0, 0)),
                shape_of((shards, r, n), bf16),
                weight=30 * microsecond,
            )(*normed, grad_both, after=after)

        def all_down(layer, inner, down_in, after=()):
            earlier = written.get("down", [])
            right = pl.BlockSpec((half_tokens, 256), lambda s: (0, s))
            written["down"] = call(
                all_down_kernel,
                (width // 256,),
                [whole((all_tokens, hidden)), right, right]
                + [pl.BlockSpec(memory_space=pl.ANY)] * len(earlier),
                [pl.BlockSpec((1, hidden, 256), lambda s: (layer, 0, s))],
                [shape_of(down_weight.shape, f32)],
                aliases={3 + k: k for k in range(len(earlier))},
                weight=20 * microsecond,
            )(inner, *down_in, *earlier, after=after)

        class Feed:
            def __init__(self, layer, normed, down_in, pieces, cuts):
                self.layer, self.normed, self.down_in = layer, normed, down_in
                self.pieces, self.cuts, self.done = pieces, cuts, 0
                self.carried, self.blocks = [], []

            def again(self, after):
                *self.carried, token = feed_again(
                    self.layer, self.normed, self.down_in, self.done, self.pieces, self.carried, after=after
                )
                self.done += 1
                return [token]

            def columns_now(self, after):
                self.got = all_columns(self.normed, self.carried[0], len(self.blocks), self.cuts, after=after)
                return [self.got]

            def columns_held(self, before=()):
                got = hold(self.got, self.blocks[-1:] + list(before))
                self.blocks.append(spread(got))
                return [got]

            def columns(self, after, before=()):
                self.columns_now(after)
                return self.columns_held(before)

            def down(self, after):
                all_down(self.layer, self.carried[1], self.down_in, after=after)
                return after

            def write(self, after=()):
                r = rows // self.cuts
                for k, blocks in enumerate(self.blocks):
                    write_blocks(self.layer, "feed", blocks[None], blocks.shape[2], 32, k * r, after=after)

        def share(values):
            first, second = values[:part], values[part:]
            kept = jnp.where(core == 0, first, second)
            arrived = swap(jnp.where(core == 0, second, first), 1)
            return [jnp.where(core == 0, kept, arrived), jnp.where(core == 0, arrived, kept)]

        def unshare(halves):
            kept = jnp.where(core == 0, halves[0], halves[1])
            arrived = swap(jnp.where(core == 0, halves[1], halves[0]), 1)
            both = [jnp.where(core == 0, kept, arrived), jnp.where(core == 0, arrived, kept)]
            return jnp.concatenate(both, axis=0)[None]

        def row(values, layer):
            return values[layer : layer + 1]

        def send_low(low):
            return low, [swap(low, 2), swap(low, 4), swap(low, 6)]

        def collect(sent, after):
            mine = stack(sent[0], *sent[1], after=after)
            return mine, swap(mine, 1)

        def send_sums(outputs, after):
            own, x, y, d = combine(outputs[0], swap(outputs[1], 1), after=after)
            return own, swap(x, 2), swap(y, 4), swap(d, 6)

        def block(run, finish, ready, after=(), due=None, filler=None):
            (gathered, other), sent = ready[:2], ready[2]
            first = run(0, gathered, list(after))
            if other is None:
                other = collect(sent, [first[0]])
            if finish is None:
                return (first, run(1, other, [first[0]])), None, None, None
            if due is None:
                sums = send_sums(first, [other[0]])
                second = run(1, other, [sums[0]])
            else:
                second = run(1, other, [first[0]])
                sums = send_sums(first, [second[0]] + list(due))
            later = send_sums(second, [sums[0]])
            done = finish(0, sums, [later[0]])
            wait = [done[0]]
            sent = send_low(done[1]) if len(done) > 1 else None
            if filler:
                wait += filler(wait)
            end = finish(1, later, wait)
            if sent is None:
                return (first, second), (done, end), None, (gathered, other)
            inputs = (gathered, other)
            other_sent = send_low(end[1])
            wait = [end[0]] + (filler([end[0]]) if filler else [])
            gathered, sent = collect(sent, wait), other_sent
            other = None if due is None else collect(sent, [gathered[0]])
            return (first, second), (done, end), (gathered, other, sent), inputs

        cotangents = share(cotangent[0])
        states = [v.astype(f32) for v in share(hidden_in[0])]
        lows = [norm_first(states[h], row(gain1, 0), row(shift1, 0))[0] for h in range(2)]
        proj_in, feed_in = [None] * layers, [None] * layers
        proj_in[0] = turned(cut_qkv(0, lows))
        sent = [send_low(low) for low in lows]
        gathered = collect(sent[0], [lows[1]] + masks + tables[0] + tables[1])
        ready = (gathered, collect(sent[1], [gathered[0]]), None)
        all_normed2, all_down_in = [None] * layers, [None] * layers
        saved = []
        for layer in range(layers):
            blocks = hold(cut_feed(layer, []), [proj_in[layer], ready[1][0]])
            feed_in[layer] = turned(blocks)
            first, done, ready, _ = block(
                lambda h, gathered, after: attend(
                    layer,
                    *gathered,
                    proj_in[layer],
                    bias_own[layer],
                    *tables[h],
                    masks[h],
                    out_weight,
                    after=after,
                ),
                lambda h, sums, after: norm(
                    states[h], *sums, row(gain2, layer), row(shift2, layer), after=after
                ),
                ready,
                [blocks],
                [feed_in[layer]],
            )
            mids = [v[0] for v in done]
            if layer == 0:
                sent = [send_low(hold(v, [mids[1]])) for v in cotangents]
                one = collect(sent[0], [ready[1][0]])
                back_ready = (one, collect(sent[1], [one[0]]), None)
                gathering = [gather_all([v[0] for v in back_ready[:2]])]
            if layer + 1 < layers:
                blocks = hold(cut_qkv(layer + 1, []), [feed_in[layer], ready[1][0]])
                proj_in[layer + 1] = turned(blocks)
                due = [proj_in[layer + 1]]
            else:
                blocks = ready[1][0]
                due = None
            inputs = ready[:2]
            second, done, ready, _ = block(
                lambda h, gathered, after: feed(layer, *gathered, feed_in[layer], down_weight, after=after),
                (
                    lambda h, sums, after: norm(
                        mids[h], *sums, row(gain1, layer + 1), row(shift1, layer + 1), after=after
                    )
                )
                if layer + 1 < layers
                else None,
                ready,
                [blocks] + (gathering[:1] if layer + 1 == layers else []),
                due,
            )
            if layer + 1 == layers:
                all_down_in[-1] = with_pair(gathering[0], [second[0][0]])
                all_normed2[0] = with_pair(gathering[1], [second[1][0]])
            gathering.append(gather_all([v[0] for v in inputs]))
            saved.append(
                [(states[h],) + tuple(first[h][2:]) + (mids[h], second[h][2]) for h in range(2)]
            )
            if layer + 1 < layers:
                states = [v[0] for v in done]
        out_sums, out_mids = second, mids

        grads = [v.astype(f32) for v in cotangents]
        small_grads, quarters, own = [None] * layers, [None] * layers, []
        fed = [None] * layers
        ready = back_ready
        starts = [second[0][2], second[1][2]]
        for layer in reversed(range(layers)):

            def both(index):
                return [saved[layer][h][index] for h in range(2)]

            filler = None
            if layer + 1 < layers:
                all_normed2[layer + 1] = with_pair(gathering[2], [ends[1][0]])
                fed[layer + 1] = Feed(layer + 1, all_normed2[layer + 1], all_down_in[layer + 1], 4, 1)

                def filler(wait):
                    return fed[layer + 1].again(wait)

            first, back, ready, inputs = block(
                lambda h, gathered, after: feed_back(
                    layer, *gathered, feed_in[layer], down_weight, saved[layer][h][7], after=after
                ),
                lambda h, sums, after: norm_back(
                    grads[h], *sums, saved[layer][h][6], row(gain2, layer), after=after
                ),
                ready,
                starts,
                filler=filler,
            )
            if layer + 1 < layers:
                gathering.append(gather_all([v[0] for v in inputs], [quarters[layer + 1]]))
            sums2 = back[0][2] + back[1][2]
            ahead = gathering[1:2] if layer > 0 else []
            if layer + 1 < layers:

                def filler(wait):
                    return fed[layer + 1].again(wait + own)

            second, ends, ready, _ = block(
                lambda h, gathered, after: attend_back(
                    layer,
                    *gathered,
                    proj_in[layer],
                    *tables[h],
                    masks[h],
                    out_weight,
                    *saved[layer][h][2:5],
                    after=after,
                ),
                lambda h, sums, after: norm_back(
                    back[h][0], *sums, saved[layer][h][0], row(gain1, layer), after=after
                ),
                ready,
                ahead,
                filler=filler,
            )
            branches, joineds = [v[2] for v in second], [v[3] for v in second]
            ended = [ends[0][0]] if layer > 0 else [ends[1][0]]
            quarters[layer] = weight_quarters(both(1), joineds, both(5), branches, after=ended)
            starts = [quarters[layer]]
            own.insert(0, scatter_quarters(quarters[layer]))
            grads, lows = [v[0] for v in ends], [v[1] for v in ends]
            sums1 = ends[0][2] + ends[1][2]
            placed = jnp.where(
                (jnp.arange(shards) == me)[None, :, None],
                (second[0][4] + second[1][4]).reshape(3, 1, cols),
                0.0,
            )
            small_grads[layer] = jnp.concatenate([sums1.reshape(-1), sums2.reshape(-1), placed.reshape(-1)])
        input_grad = unshare(lows)

        summed = [jnp.stack(small_grads)]

        def small_step():
            summed.append(summed[-1] + swap(summed[-1], 1 << (len(summed) - 1)))
            return [summed[-1]]

        turned1 = turn_quarters(own[1], [second[1][2]])
        steps3 = small_step() + small_step() + small_step()
        wait = fed[1].columns([quarters[0], input_grad] + steps3, [turned1])
        packed1 = gather_quarters(turned1, own[1], wait)
        fed[1].down(wait)
        wait = [written["down"][0][1, :8, :128]]
        all_down_in[0] = with_pair(gathering[3], wait)
        fed[0] = Feed(0, all_normed2[0], all_down_in[0], 2, 2)
        wait = fed[0].again(wait)
        wait = fed[0].again(wait)
        out_moving = [send_sums(out_sums[h], wait) for h in range(2)]
        wait = fed[0].columns(wait, fed[1].blocks)
        wait = fed[0].columns_now(wait)
        outs = [last(out_mids[h], *out_moving[h], after=wait)[0] for h in range(2)]
        block_out = unshare(outs)
        turned0 = turn_quarters(own[0], wait + fed[0].blocks)
        fed[1].write(wait)
        packed0 = gather_quarters(turned0, own[0], wait)
        wait = fed[0].columns_held([turned0])
        fed[0].down(wait)

        norms = summed[-1][:, : 4 * width].reshape(layers, 4, shards, rows)
        biases = summed[-1][:, 4 * width :].reshape(layers, shards, 3 * rows)
        mine = jnp.concatenate(
            [
                lax.dynamic_index_in_dim(norms, me, axis=2, keepdims=False).reshape(layers, 4 * rows),
                lax.dynamic_index_in_dim(biases, me, axis=1, keepdims=False),
            ],
            axis=1,
        )
        mine = lax.all_gather(mine, "rep", axis=0, tiled=False)
        mine = (mine[0] + mine[1]) + (mine[2] + mine[3])
        fed[0].write()
        for layer, packed in ((1, packed1), (0, packed0)):
            write_blocks(layer, "qkv", packed, 3 * cols, 32, 0)
            write_blocks(layer, "out", packed, cols, quarter, 0, 3)

        def owned(k):
            return mine[:, k * rows : (k + 1) * rows]

        return (
            block_out,
            input_grad,
            owned(0),
            owned(1),
            written["qkv"][0],
            mine[:, 4 * rows :],
            written["out"][0],
            owned(2),
            owned(3),
            *written["feed"],
            written["down"][0],
        )

    return local


class Exchange:
    def __init__(self, mesh):
        self.shards = mesh.shape["shard"]
        self.reps = mesh.shape["rep"]
        self.cube = self.shards == 8
        self.line = self.reps == 4

    def swap(self, values, bit):
        pairs = [(i, i ^ bit) for i in range(self.shards)]
        return lax.ppermute(values, "shard", pairs)

    def gather(self, own):
        if not self.cube:
            return lax.all_gather(own, "shard", axis=0, tiled=False)
        first = self.swap(own, 1)
        x, y, d = self.swap(own, 2), self.swap(own, 4), self.swap(own, 6)
        others = self.swap(jnp.stack([x, y, d]), 1)
        return jnp.stack([own, first, x, others[0], y, others[1], d, others[2]])

    def scatter_sum(self, blocks):
        if not self.cube:
            return lax.psum_scatter(blocks.astype(bf16), "shard", scatter_dimension=0, tiled=False).astype(f32)
        low = blocks.astype(bf16)
        arrived = self.swap(jnp.stack([low[1], low[3], low[5], low[7]]), 1).astype(f32)
        x = self.swap((blocks[2] + arrived[1]).astype(bf16), 2)
        y = self.swap((blocks[4] + arrived[2]).astype(bf16), 4)
        d = self.swap((blocks[6] + arrived[3]).astype(bf16), 6)
        own = blocks[0] + arrived[0]
        return own + x.astype(f32) + (y.astype(f32) + d.astype(f32))

    def spread(self, blocks):
        return lax.all_to_all(blocks, "shard", split_axis=0, concat_axis=0, tiled=False)

    def total(self, grad, turn=None):
        turn = turn or (lambda v: v)
        if not self.line:
            full = lax.psum(grad.astype(bf16), "rep")
            return jnp.stack([turn(full[0]), turn(full[1])]).astype(f32)
        rep = lax.axis_index("rep")
        low = grad.astype(bf16)
        inward = lax.ppermute(low, "rep", [(0, 1), (3, 2)])
        part = (grad + inward.astype(f32)).astype(bf16)
        lower = rep < 2
        sent = jnp.where(lower, part[0], part[1])
        kept = jnp.where(lower, part[1], part[0])
        middle = lax.ppermute(sent, "rep", [(1, 2), (2, 1)])
        final = turn((kept.astype(f32) + middle.astype(f32)).astype(bf16))
        other = lax.ppermute(final, "rep", [(1, 2), (2, 1)])
        whole = jnp.where(lower, jnp.stack([other, final]), jnp.stack([final, other]))
        outward = lax.ppermute(whole, "rep", [(1, 0), (2, 3)])
        return jnp.where((rep == 1) | (rep == 2), whole, outward).astype(f32)


def make_general(mesh):
    net = Exchange(mesh)
    shards = net.shards

    def local(
        hidden_in,
        segments,
        ln1_gain,
        ln1_bias,
        qkv_weight,
        qkv_bias,
        out_weight,
        ln2_gain,
        ln2_bias,
        gate_weight,
        up_weight,
        down_weight,
        cotangent,
    ):
        layers, rows = qkv_weight.shape[:2]
        width = hidden_in.shape[2]
        tokens = hidden_in.shape[1]
        head_size = width // HEADS
        scale = head_size ** (-0.5)
        own_heads = HEADS // shards
        cols = own_heads * head_size
        hidden_units = down_weight.shape[1]
        everyone = shards * tokens
        me = lax.axis_index("shard")

        small = jnp.concatenate(
            [v.reshape(-1) for v in (ln1_gain, ln1_bias, ln2_gain, ln2_bias, qkv_bias)]
        )
        small = lax.all_gather(small, "shard", axis=0, tiled=False)
        cuts = [0]
        for v in (ln1_gain, ln1_bias, ln2_gain, ln2_bias, qkv_bias):
            cuts.append(cuts[-1] + v.size)

        def whole_of(index, like):
            part = small[:, cuts[index] : cuts[index + 1]].reshape(shards, layers, like.shape[1])
            return part.transpose(1, 0, 2).reshape(layers, -1).astype(f32)

        gain1, shift1 = whole_of(0, ln1_gain), whole_of(1, ln1_bias)
        gain2, shift2 = whole_of(2, ln2_gain), whole_of(3, ln2_bias)
        bias_all = whole_of(4, qkv_bias).reshape(layers, 3, shards, cols)
        bias_own = lax.dynamic_index_in_dim(bias_all, me, axis=2, keepdims=False)
        bias_own = bias_own.reshape(layers, 3 * cols)

        group_segments = net.gather(segments[0].astype(bf16)).astype(jnp.int32)
        positions, allowed = positions_and_mask(group_segments)
        cosine, sine = rotary_tables(positions)
        allowed = allowed[:, None]

        def columns_of(weight):
            cut = weight.reshape(rows, shards, -1).transpose(1, 0, 2)
            return net.spread(cut).reshape(width, -1)

        def qkv_columns(weight):
            cut = weight.reshape(rows, 3, shards, cols).transpose(2, 0, 1, 3)
            return net.spread(cut).reshape(width, 3 * cols)

        proj_in = [qkv_columns(qkv_weight[layer]) for layer in range(layers)]
        weight_gate = [columns_of(gate_weight[layer]) for layer in range(layers)]
        weight_up = [columns_of(up_weight[layer]) for layer in range(layers)]

        def gather(values):
            return net.gather(values).reshape(everyone, -1)

        def scatter_sum(values):
            return net.scatter_sum(values.reshape(shards, tokens, -1))

        state = hidden_in[0].astype(f32)
        saved = []
        for layer in range(layers):
            xhat1, inverse1 = normalize(state)
            normed1 = gather((xhat1 * gain1[layer] + shift1[layer]).astype(bf16))
            joined = dot(normed1, proj_in[layer]) + bias_own[layer]
            split = joined.reshape(shards, tokens, 3, own_heads, head_size)
            query = rotate(split[:, :, 0], cosine, sine).astype(bf16)
            keys = rotate(split[:, :, 1], cosine, sine).astype(bf16)
            value = split[:, :, 2].astype(bf16)
            scores = (
                jnp.einsum("gqhd,gkhd->ghqk", query, keys, preferred_element_type=f32) * scale
            )
            masked = jnp.where(allowed, scores, -1000000000.0)
            peak = jnp.max(masked, axis=-1, keepdims=True)
            raised = jnp.exp(masked - peak)
            probs = raised / jnp.sum(raised, axis=-1, keepdims=True)
            probs_low = probs.astype(bf16)
            mixed = (
                jnp.einsum("ghqk,gkhd->gqhd", probs_low, value, preferred_element_type=f32)
                .astype(bf16)
                .reshape(everyone, cols)
            )
            state_mid = state + scatter_sum(dot(mixed, out_weight[layer]))
            xhat2, inverse2 = normalize(state_mid)
            normed2 = gather((xhat2 * gain2[layer] + shift2[layer]).astype(bf16))
            gate = dot(normed2, weight_gate[layer])
            upper = dot(normed2, weight_up[layer])
            inner = (jax.nn.silu(gate) * upper).astype(bf16)
            state = state_mid + scatter_sum(dot(inner, down_weight[layer]))
            saved.append(
                (xhat1, inverse1, normed1, query, keys, value, probs, mixed)
                + (xhat2, inverse2, normed2, gate, upper, inner)
            )
        block_out = state.astype(bf16)[None]

        def from_columns(grad):
            return grad.reshape(shards, 2, rows // 2, -1).transpose(1, 0, 2, 3)

        def turn_columns(half):
            return net.spread(half).transpose(1, 0, 2).reshape(rows // 2, -1)

        def turn_qkv(half):
            whole = net.spread(half).reshape(shards, rows // 2, 3, cols)
            return whole.transpose(1, 2, 0, 3).reshape(rows // 2, -1)

        def halves(grad):
            return grad.reshape(2, grad.shape[0] // 2, -1)

        grad_state = cotangent[0].astype(f32)
        weight_grads = [None] * layers
        small_grads = [None] * layers
        for layer in reversed(range(layers)):
            xhat1, inverse1, normed1, query, keys, value, probs, mixed = saved[layer][:8]
            xhat2, inverse2, normed2, gate, upper, inner = saved[layer][8:]
            down_in = gather(grad_state.astype(bf16))
            grad_inner = dot_t(down_in, down_weight[layer])
            sigmoid = jax.nn.sigmoid(gate)
            silu = gate * sigmoid
            grad_gate = (grad_inner * upper * (sigmoid * (1.0 + gate * (1.0 - sigmoid)))).astype(bf16)
            grad_up = (grad_inner * silu).astype(bf16)
            grad_normed2 = scatter_sum(
                dot_t(grad_gate, weight_gate[layer]) + dot_t(grad_up, weight_up[layer])
            )
            grad_down_weight = net.total(halves(t_dot(inner, down_in)))
            grad_gate_weight = net.total(from_columns(t_dot(normed2, grad_gate)), turn_columns)
            grad_up_weight = net.total(from_columns(t_dot(normed2, grad_up)), turn_columns)
            back2, gain2_grad, shift2_grad = normalize_back(
                grad_normed2, xhat2, inverse2, gain2[layer]
            )
            grad_state = grad_state + back2

            branch = gather(grad_state.astype(bf16))
            grad_mixed = dot_t(branch, out_weight[layer]).astype(bf16)
            grad_out_weight = net.total(halves(t_dot(mixed, branch)))
            grad_mixed = grad_mixed.reshape(shards, tokens, own_heads, head_size)
            grad_probs = jnp.einsum(
                "gqhd,gkhd->ghqk", grad_mixed, value, preferred_element_type=f32
            )
            grad_value = jnp.einsum(
                "ghqk,gqhd->gkhd", probs.astype(bf16), grad_mixed, preferred_element_type=f32
            )
            inner_sum = jnp.sum(probs * grad_probs, axis=-1, keepdims=True)
            grad_scores = (probs * (grad_probs - inner_sum)).astype(bf16)
            grad_query = (
                jnp.einsum("ghqk,gkhd->gqhd", grad_scores, keys, preferred_element_type=f32) * scale
            )
            grad_key = (
                jnp.einsum("ghqk,gqhd->gkhd", grad_scores, query, preferred_element_type=f32)
                * scale
            )
            grad_query = rotate(grad_query, cosine, -sine)
            grad_key = rotate(grad_key, cosine, -sine)
            grad_joined = jnp.stack([grad_query, grad_key, grad_value], axis=2)
            bias_grad = jnp.sum(grad_joined.astype(bf16).astype(f32), axis=(0, 1))
            grad_joined = grad_joined.reshape(everyone, 3 * cols).astype(bf16)
            grad_normed1 = scatter_sum(dot_t(grad_joined, proj_in[layer]))
            grad_qkv_weight = net.total(from_columns(t_dot(normed1, grad_joined)), turn_qkv)
            back1, gain1_grad, shift1_grad = normalize_back(
                grad_normed1, xhat1, inverse1, gain1[layer]
            )
            grad_state = grad_state + back1
            weight_grads[layer] = (
                grad_qkv_weight.reshape(rows, -1),
                grad_out_weight.reshape(rows, -1),
                grad_gate_weight.reshape(rows, -1),
                grad_up_weight.reshape(rows, -1),
                grad_down_weight.reshape(hidden_units, -1),
            )
            placed = jnp.where(
                (jnp.arange(shards) == me)[None, :, None], bias_grad.reshape(3, 1, cols), 0.0
            )
            small_grads[layer] = jnp.concatenate(
                [gain1_grad, shift1_grad, gain2_grad, shift2_grad, placed.reshape(-1)]
            )

        summed = lax.psum(jnp.stack(small_grads), ("shard", "rep"))

        def owned(begin, count):
            part = summed[:, begin : begin + count].reshape(layers, shards, count // shards)
            return lax.dynamic_index_in_dim(part, me, axis=1, keepdims=False)

        stacked = [
            jnp.stack([weight_grads[layer][index] for layer in range(layers)]) for index in range(5)
        ]
        return (
            block_out,
            grad_state.astype(bf16)[None],
            owned(0, width),
            owned(width, width),
            stacked[0],
            owned(4 * width, 3 * width),
            stacked[1],
            owned(2 * width, width),
            owned(3 * width, width),
            stacked[2],
            stacked[3],
            stacked[4],
        )

    return local


def solution(mesh):
    tokens3 = P(("shard", "rep"), None, None)
    vector = P(None, "shard")
    matrix = P(None, "shard", None)
    in_specs = (
        tokens3,
        P(("shard", "rep"), None),
        vector,
        vector,
        matrix,
        vector,
        matrix,
        vector,
        vector,
        matrix,
        matrix,
        matrix,
        tokens3,
    )
    out_specs = (
        tokens3,
        tokens3,
        vector,
        vector,
        matrix,
        vector,
        matrix,
        vector,
        vector,
        matrix,
        matrix,
        matrix,
    )
    cube = mesh.shape["shard"] == 8 and mesh.shape["rep"] == 4
    local = make_cube(mesh) if cube else make_general(mesh)
    return jax.shard_map(
        local, mesh=mesh, in_specs=in_specs, out_specs=out_specs, check_vma=False
    )
```
